32 devices in a mesh: groups: 2 (over x), span: 16 (over z, y, core).
Axes of the slice: x: 2, y: 2, z: 4, core: 2. Of those that a mesh axis runs over, the one named last changes fastest.
Arguments:
- queries: bfloat16 [8192, 2560], P(('groups', 'span')), parts along dimension 0, may hold values from -100 to 100
- cross_queries: bfloat16 [8192, 2560], P(('groups', 'span')), parts along dimension 0, may hold values from -100 to 100
- frame_kv: bfloat16 [8192, 5120], P(('groups', 'span')), parts along dimension 0, may hold values from -7 to 7
- sink_kv: bfloat16 [32, 64, 5120], P(('groups', 'span')), parts along dimension 0, may hold values from -5 to 5
- prompt_kv: bfloat16 [4, 512, 5120], P('groups', 'span'), parts along dimension 0, may hold values from -7 to 7
- switch: int32 [8], P('groups'), parts along dimension 0, may hold values from 0 to 4
Outputs:
- self_out: bfloat16 [8192, 2560], P(('groups', 'span')), parts along dimension 0
- cross_out: bfloat16 [8192, 2560], P(('groups', 'span')), parts along dimension 0
The draws below stay inside these ranges and needn't reach their ends.
There are 2 independent parts, one for each index of `groups`. The reference program is written for one: setup_inputs(seed, part) draws one part's arguments, and reference() takes and returns one part's arrays. A program takes and returns all parts, laid end to end along the dimension named above; each array names one. Nothing has to cross between parts.
All inputs are finite; a program needn't handle non-finite values.
Results may differ from the reference program's by a relative error of at most 0.006.
Values may be sent and summed in bfloat16 or wider, within the bound.
No kernel may reach another device: no remote copies, remote signals or barrier semaphores. Data moves between devices by JAX's collectives and lax.ppermute only.
A program may use at most 128 MiB of HBM per device.

```python
import math
import jax
import jax.numpy as jnp
from jax import lax

HEADS = 20
HDIM = 128
FRAME = 256
WIN = 4
PTOK = 512
PROMPTS = 2
HD = 2560
STREAMS = 4
TOKENS = 4096
N_SPAN = 16


def clipped_normal(key, shape):
    return jnp.clip(jax.random.normal(key, shape, jnp.float32), -5.0, 5.0)


def frame_keys(key):
    key_rows = clipped_normal(jax.random.fold_in(key, 7), (TOKENS, HEADS * HDIM))
    return key_rows


def draw_frame_kv(key, part):
    values = clipped_normal(jax.random.fold_in(key, 8), (TOKENS, HEADS * HDIM))
    return jnp.concatenate([frame_keys(key), values], axis=1).astype(jnp.bfloat16)


def draw_queries(key, part):
    query_rows = clipped_normal(jax.random.fold_in(key, 9), (TOKENS, HEADS * HDIM))
    return query_rows.astype(jnp.bfloat16)


def draw_prompt_kv(key, part):
    stacked = []
    for prompt in range(PROMPTS):
        key_rows = clipped_normal(jax.random.fold_in(key, 20 + prompt), (PTOK, HEADS * HDIM))
        values = clipped_normal(jax.random.fold_in(key, 40 + prompt), (PTOK, HEADS * HDIM))
        stacked.append(jnp.concatenate([key_rows, values], axis=1))
    return jnp.stack(stacked, axis=0).astype(jnp.bfloat16)


def draw_cross_queries(key, part):
    query_rows = clipped_normal(jax.random.fold_in(key, 13), (TOKENS, HEADS * HDIM))
    return query_rows.astype(jnp.bfloat16)


def place_ends(entries, stream_key, smallest, largest):
    spot = [jax.random.randint(jax.random.fold_in(stream_key, axis), (), 0, length) for axis, length in enumerate(entries.shape)]
    longest = entries.shape.index(max(entries.shape))
    neighbour = spot[:longest] + [(spot[longest] + 1) % entries.shape[longest]] + spot[longest + 1:]
    return entries.at[tuple(spot)].set(smallest).at[tuple(neighbour)].set(largest)


def shard_levels(own_key, extent, cuts, smallest, high):
    loudness, own = 1.0, jax.random.fold_in(own_key, 6)
    for axis_at, shards_of in cuts:
        steps = jnp.exp(jax.random.uniform(jax.random.fold_in(own, axis_at), (shards_of,), jnp.float32, smallest / len(cuts), high / len(cuts)))
        loudness = loudness * jnp.repeat(steps, extent[axis_at] // shards_of).reshape([-1 if axis == axis_at else 1 for axis in range(len(extent))])
    return loudness


def scatter_about(rng, dims, spread, most, pieces=(), held_as=jnp.bfloat16):
    level = shard_levels(rng, dims, pieces, -0.22, 0.18) if pieces else 1.0
    result = jax.random.normal(rng, dims, jnp.float32) * spread * level
    return jnp.minimum(jnp.maximum(result, -most), most).astype(held_as)


def setup_inputs(seed: int = 0, part: int = 0) -> dict:
    keys = jax.random.split(jax.random.key(seed), 7)
    part_keys = jax.random.split(jax.random.fold_in(keys[6], part), 7)
    return {
        "queries": draw_queries(jax.random.fold_in(jax.random.fold_in(keys[6], part), 71), part),
        "cross_queries": draw_cross_queries(jax.random.fold_in(jax.random.fold_in(keys[6], part), 71), part),
        "frame_kv": draw_frame_kv(jax.random.fold_in(jax.random.fold_in(keys[6], part), 71), part),
        "sink_kv": scatter_about(part_keys[3], (N_SPAN, FRAME // WIN, 2 * HD), 1.0, 5.0, ((0, 16),)),
        "prompt_kv": draw_prompt_kv(jax.random.fold_in(jax.random.fold_in(keys[6], part), 71), part),
        "switch": place_ends(jax.random.randint(part_keys[5], (STREAMS,), 0, WIN + 1), jax.random.fold_in(part_keys[5], 1), 0, WIN).astype(jnp.int32),
    }


def softmax_blend(query_rows, key_rows, value_rows, visible):
    scores = jnp.einsum('qhd,khd->hqk', query_rows, key_rows) * (1.0 / math.sqrt(HDIM))
    if visible is not None:
        scores = jnp.where(visible[None], scores, -jnp.inf)
    row_max = lax.optimization_barrier(jnp.max(scores, axis=-1, keepdims=True))
    weights = jnp.exp(scores - row_max)
    totals = lax.optimization_barrier(jnp.sum(weights, axis=-1))
    rounded = lax.optimization_barrier(weights.astype(jnp.bfloat16)).astype(jnp.float32)
    blended = jnp.einsum('hqk,khd->qhd', rounded, value_rows)
    return (blended / jnp.transpose(totals)[:, :, None]).astype(jnp.bfloat16)

def reference(queries, cross_queries, frame_kv, sink_kv, prompt_kv, switch):
    streams = N_SPAN // WIN
    stream_queries = jnp.transpose(queries.astype(jnp.float32).reshape(WIN, streams, FRAME, HEADS, HDIM), (1, 0, 2, 3, 4)).reshape(streams, WIN * FRAME, HEADS, HDIM)
    stream_kv = jnp.transpose(frame_kv.astype(jnp.float32).reshape(WIN, streams, FRAME, 2, HEADS, HDIM), (1, 0, 2, 3, 4, 5)).reshape(streams, WIN * FRAME, 2, HEADS, HDIM)
    stream_sink = jnp.transpose(sink_kv.astype(jnp.float32).reshape(WIN, streams, FRAME // WIN, 2, HEADS, HDIM), (1, 0, 2, 3, 4, 5)).reshape(streams, FRAME, 2, HEADS, HDIM)
    key_block = jnp.concatenate([jnp.zeros((FRAME,), jnp.int32), jnp.repeat(jnp.arange(WIN, dtype=jnp.int32) + 1, FRAME)])
    query_frame = jnp.repeat(jnp.arange(WIN, dtype=jnp.int32), FRAME)
    visible = key_block[None, :] <= query_frame[:, None] + 1

    def one_stream(inputs_one):
        query_rows, kv_rows, sink_rows = inputs_one
        key_rows = jnp.concatenate([sink_rows[:, 0], kv_rows[:, 0]], axis=0)
        value_rows = jnp.concatenate([sink_rows[:, 1], kv_rows[:, 1]], axis=0)
        return softmax_blend(query_rows, key_rows, value_rows, visible).reshape(WIN * FRAME, HEADS * HDIM)
    per_stream = lax.map(one_stream, (stream_queries, stream_kv, stream_sink))
    self_out = jnp.transpose(per_stream.reshape(streams, WIN, FRAME, HEADS * HDIM), (1, 0, 2, 3)).reshape(N_SPAN * FRAME, HEADS * HDIM)
    devices = jnp.arange(N_SPAN, dtype=jnp.int32)
    window_place = devices // streams
    stream_index = devices % streams
    prompt_id = (window_place >= switch[stream_index]).astype(jnp.int32)
    frame_queries = cross_queries.astype(jnp.float32).reshape(N_SPAN, FRAME, HEADS, HDIM)
    bank = prompt_kv.astype(jnp.float32).reshape(PROMPTS, PTOK, 2, HEADS, HDIM)

    def one_frame(inputs_one):
        query_rows, chosen = inputs_one
        picked = lax.dynamic_index_in_dim(bank, chosen.astype(jnp.int32), 0, keepdims=False)
        return softmax_blend(query_rows, picked[:, 0], picked[:, 1], None).reshape(FRAME, HEADS * HDIM)
    cross_out = lax.map(one_frame, (frame_queries, prompt_id)).reshape(N_SPAN * FRAME, HEADS * HDIM)
    return (self_out, cross_out)
```

```python
import math

import jax
import jax.numpy as jnp
from jax import lax
from jax.experimental import pallas as pl
from jax.experimental.pallas import tpu as pltpu
from jax.sharding import PartitionSpec as P

HEADS = 20
HDIM = 128
WIN = 4
CHUNKS = 4
PER = HEADS // CHUNKS
CW = PER * HDIM
WIDTH = HEADS * HDIM
STAT = 16
LOG_SCALE = math.log2(math.e) / math.sqrt(HDIM)
VMEM = 48 * 1024 * 1024


def diagonal():
    rows = lax.broadcasted_iota(jnp.int32, (HDIM, HDIM), 0)
    cols = lax.broadcasted_iota(jnp.int32, (HDIM, HDIM), 1)
    return rows == cols


def stat_rows(column):
    eye = diagonal()
    groups = column.shape[0] // HDIM
    tops, mids, lows = [], [], []
    for group in range(groups):
        part = column[group * HDIM : (group + 1) * HDIM]
        row = jnp.sum(jnp.where(eye, part, 0.0), axis=0, keepdims=True)
        top = row.astype(jnp.bfloat16).astype(jnp.float32)
        mid = (row - top).astype(jnp.bfloat16).astype(jnp.float32)
        tops.append(top)
        mids.append(mid)
        lows.append(row - top - mid)
    used = tops + mids + lows
    used.append(jnp.zeros((STAT - len(used), HDIM), jnp.float32))
    return jnp.concatenate(used, axis=0).astype(jnp.bfloat16)


def stat_column(tile, groups):
    eye = diagonal()
    tile = tile.astype(jnp.float32)
    columns = []
    for group in range(groups):
        row = (
            tile[group : group + 1]
            + tile[groups + group : groups + group + 1]
            + tile[2 * groups + group : 2 * groups + group + 1]
        )
        columns.append(jnp.sum(jnp.where(eye, row, 0.0), axis=1, keepdims=True))
    return jnp.concatenate(columns, axis=0)


def fresh_state(query, keys, values):
    scores = lax.dot_general(
        query, keys, (((1,), (1,)), ((), ())), preferred_element_type=jnp.float32
    )
    top = jnp.max(scores, axis=1, keepdims=True)
    weights = jnp.exp2((scores - top) * LOG_SCALE)
    total = jnp.sum(weights, axis=1, keepdims=True)
    blended = jnp.dot(weights.astype(jnp.bfloat16), values, preferred_element_type=jnp.float32)
    return top * LOG_SCALE, total, blended


def merge_states(states):
    if len(states) == 1:
        return states[0]
    top = states[0][0]
    for state in states[1:]:
        top = jnp.maximum(top, state[0])
    total, blended = 0.0, 0.0
    for state in states:
        factor = jnp.exp2(state[0] - top)
        total = total + state[1] * factor
        blended = blended + state[2] * factor
    return top, total, blended


def stacked(refs):
    pieces = [ref[...] for ref in refs]
    return pieces[0] if len(pieces) == 1 else jnp.concatenate(pieces, axis=0)


class Block:
    def __init__(self, array, rows, index, base):
        self.array, self.rows, self.index, self.base = array, rows, index, base

    def spec(self):
        index, base = self.index, self.base
        return pl.BlockSpec((self.rows, HDIM), lambda head: (index, base + head))


def attend(queries, pairs, parts, heads, out_rows=None, final=None, name="attend"):
    count = len(queries)
    frame = queries[0].rows
    blocks = list(queries)
    for key, value in pairs:
        blocks += [key, value]
    blocks += parts
    operands = [block.array for block in blocks]
    in_specs = [block.spec() for block in blocks]
    aliases = {}
    if final is None:
        out_shape = jax.ShapeDtypeStruct((out_rows, heads * HDIM), jnp.bfloat16)
        out_specs = pl.BlockSpec((count * (frame + STAT), HDIM), lambda head: (0, head))
    else:
        onto, shape, base = final
        out_shape = jax.ShapeDtypeStruct(shape, jnp.bfloat16)
        out_specs = pl.BlockSpec((frame, HDIM), lambda head: (0, base + head))
        if onto is not None:
            aliases = {len(operands): 0}
            operands.append(onto)
            in_specs.append(pl.BlockSpec(memory_space=pl.ANY))

    def kernel(*refs):
        out = refs[-1]
        query_refs = refs[:count]
        key_refs = refs[count : count + 2 * len(pairs) : 2]
        value_refs = refs[count + 1 : count + 2 * len(pairs) : 2]
        part_refs = refs[count + 2 * len(pairs) : count + 2 * len(pairs) + len(parts)]
        if pairs:
            keys, values = stacked(key_refs), stacked(value_refs)
        for at in range(count):
            states = []
            if pairs:
                states.append(fresh_state(query_refs[at][...], keys, values))
            for part in part_refs:
                states.append(
                    (
                        stat_column(part[frame : frame + STAT], frame // HDIM),
                        1.0,
                        part[:frame].astype(jnp.float32),
                    )
                )
            top, total, blended = merge_states(states)
            rows = (blended / total).astype(jnp.bfloat16)
            if final is None:
                start = at * (frame + STAT)
                out[start : start + frame] = rows
                out[start + frame : start + frame + STAT] = stat_rows(top + jnp.log2(total))
            else:
                out[...] = rows

    key_rows = sum(key.rows for key, _ in pairs)
    return pl.pallas_call(
        kernel,
        out_shape=out_shape,
        grid=(heads,),
        in_specs=in_specs,
        out_specs=out_specs,
        input_output_aliases=aliases,
        compiler_params=pltpu.CompilerParams(vmem_limit_bytes=VMEM),
        cost_estimate=pl.CostEstimate(
            flops=4 * heads * count * frame * key_rows * HDIM,
            bytes_accessed=2 * heads * HDIM * (count * frame * 2 + 2 * key_rows),
            transcendentals=heads * count * frame * key_rows,
        ),
        name=name,
    )(*operands)


def chunk_rows(array):
    return jnp.concatenate(
        [array[:, at : at + CW] for at in range(0, array.shape[1], CW)], axis=0
    )


def fill(array, rows):
    if array.shape[0] == rows:
        return array
    return jnp.pad(array, ((0, rows - array.shape[0]), (0, 0)))


def shards(queries, cross_queries, frame_kv, sink_kv, prompt_kv, switch):
    streams = lax.axis_size("span") // WIN
    device = lax.axis_index("span")
    place = device // streams
    stream = device % streams
    frame = queries.shape[0]
    sink = sink_kv.reshape(sink_kv.shape[1], sink_kv.shape[2])
    sink_rows = sink.shape[0]
    prompt_rows = prompt_kv.shape[1]
    part_rows = frame + STAT
    kvs_rows = 2 * frame + 2 * sink_rows
    prompt = chunk_rows(prompt_kv.reshape(-1, prompt_kv.shape[2]))
    own_sink = chunk_rows(sink)

    def move(value, pairs):
        both = [(a * streams + s, b * streams + s) for a, b in pairs for s in range(streams)]
        return lax.ppermute(value, "span", both)

    def across(value, flip):
        pairs = [(at, (at // streams) * streams + ((at % streams) ^ flip)) for at in range(WIN * streams)]
        return lax.ppermute(value, "span", pairs)

    def choose(branches, *operands):
        return lax.switch(place, branches, *operands)

    def query_cols(array, *chunks):
        return jnp.concatenate([array[:, c * CW : (c + 1) * CW] for c in chunks], axis=0)

    def kvs(chunk):
        low = chunk * CW
        return jnp.concatenate(
            [
                frame_kv[:, low : low + CW],
                frame_kv[:, WIDTH + low : WIDTH + low + CW],
                sink[:, low : low + CW],
                sink[:, WIDTH + low : WIDTH + low + CW],
            ],
            axis=0,
        )

    def own_query(array, chunk):
        return Block(array, frame, 0, chunk * PER)

    def own_pairs(frame_array, sink_array, chunk):
        base = chunk * PER
        return [
            (Block(frame_array, frame, 0, base), Block(frame_array, frame, 0, HEADS + base)),
            (Block(sink_array, sink_rows, 0, base), Block(sink_array, sink_rows, 0, HEADS + base)),
        ]

    def kvs_pairs(array):
        first = 2 * frame // sink_rows
        return [
            (Block(array, frame, 0, 0), Block(array, frame, 1, 0)),
            (Block(array, sink_rows, first, 0), Block(array, sink_rows, first + 1, 0)),
        ]

    def sink_pair(array, chunk):
        return (
            Block(array, sink_rows, chunk, 0),
            Block(array, sink_rows, CHUNKS + chunk, 0),
        )

    def part(array, index):
        return Block(array, part_rows, index, 0)

    stream_ids = jnp.arange(switch.shape[0], dtype=jnp.int32)

    def picked_by(which):
        at = jnp.sum(jnp.where(stream_ids == which, switch, 0))
        return (place >= at).astype(jnp.int32)

    pick, other_pick = picked_by(stream), picked_by(stream ^ 1)

    def spread(shard):
        held = [shard]
        flip = streams // 2
        while flip > 1:
            held = held + [across(each, flip) for each in held]
            flip //= 2

        def chosen(which):
            parts = [
                lax.dynamic_index_in_dim(
                    each.reshape(2 * CHUNKS, 2, prompt_rows, CW), which, 1, keepdims=False
                )
                for each in held
            ]
            return jnp.concatenate(parts, axis=1).reshape(-1, CW)

        return chosen(pick), across(chosen(other_pick), 1)

    prompt_size = prompt.shape[0]
    same = max(prompt_size, 2 * frame, own_sink.shape[0])
    wide = max(kvs_rows, prompt_size, 2 * part_rows)

    up1 = move(prompt, [(0, 1), (1, 2), (2, 3)])
    down1 = move(
        choose(
            [
                lambda q, p: fill(p, same),
                lambda q, p: fill(p, same),
                lambda q, p: fill(query_cols(q, 0, 1), same),
                lambda q, p: fill(p, same),
            ],
            queries,
            prompt,
        ),
        [(3, 2), (2, 1), (1, 0)],
    )
    up2 = move(
        jnp.where(place == 0, kvs(0), kvs(3)),
        [(0, 1), (1, 2)],
    )
    down2 = move(
        choose(
            [
                lambda q, s: fill(s, same),
                lambda q, s: fill(s, same),
                lambda q, s: fill(s, same),
                lambda q, s: fill(query_cols(q, 0, 1), same),
            ],
            queries,
            own_sink,
        ),
        [(3, 1), (1, 0)],
    )
    stages = [spread(prompt)]
    home = attend(
        [own_query(queries, 0)],
        own_pairs(frame_kv, sink, 0),
        [],
        HEADS,
        out_rows=part_rows,
        name="home",
    )
    up3 = move(
        choose(
            [lambda k, r: fill(k, wide)] + [lambda k, r: fill(r, wide)] * 3,
            kvs(3),
            up1,
        ),
        [(0, 1), (1, 2), (2, 3)],
    )
    down3 = move(
        choose(
            [lambda q, p: fill(p, same)] * 3 + [lambda q, p: fill(query_cols(q, 2, 3), same)],
            queries,
            prompt,
        ),
        [(3, 2), (2, 1)],
    )
    stages.append(
        spread(jnp.where(place == 0, down1[:prompt_size], up1))
    )

    def visit(q2, q3, came, frame_array, sink_array, chunk):
        return attend(
            [q2, q3],
            own_pairs(frame_array, sink_array, chunk) + kvs_pairs(came),
            [],
            PER,
            out_rows=wide,
            name="visit",
        )

    up4 = move(
        choose(
            [lambda k, f, s, c, d1, d2: fill(k, wide)]
            + [
                lambda k, f, s, c, d1, d2: visit(
                    Block(d1, frame, 0, 0), Block(d2, frame, 0, 0), c, f, s, 0
                )
            ]
            + [lambda k, f, s, c, d1, d2: fill(k, wide)] * 2,
            kvs(1),
            frame_kv,
            sink,
            up2,
            down1,
            down2,
        ),
        [(0, 1), (1, 2)],
    )
    down4 = move(
        choose(
            [lambda q, r: r] * 3 + [lambda q, r: fill(query_cols(q, 0, 1), same)],
            queries,
            down1,
        ),
        [(3, 2), (2, 1)],
    )
    up5 = move(
        choose(
            [lambda k, r: fill(k, wide)] + [lambda k, r: r] * 3,
            kvs(2),
            up3,
        ),
        [(0, 1), (1, 2), (2, 3)],
    )
    down5 = move(
        choose(
            [
                lambda q, s, r: r,
                lambda q, s, r: r,
                lambda q, s, r: fill(
                    jnp.concatenate([q[:, 2 * CW : 3 * CW], r[:frame]], axis=0), same
                ),
                lambda q, s, r: fill(s, same),
            ],
            queries,
            own_sink,
            down3,
        ),
        [(3, 2), (2, 1), (1, 0)],
    )
    stages.append(
        spread(
            choose(
                [
                    lambda u3, d1, d3, d5: d5[:prompt_size],
                    lambda u3, d1, d3, d5: d3[:prompt_size],
                    lambda u3, d1, d3, d5: d1[:prompt_size],
                    lambda u3, d1, d3, d5: u3[:prompt_size],
                ],
                up3,
                down1,
                down3,
                down5,
            )
        )
    )

    def join(query, came, frame_array, sink_array, chunk, rows):
        return attend(
            [query],
            own_pairs(frame_array, sink_array, chunk),
            [part(came, 1)],
            PER,
            out_rows=rows,
            name="join",
        )

    two = 2 * part_rows
    up6 = move(
        choose(
            [lambda f, s, u4, d1, d2, d4: jnp.zeros((two, CW), jnp.bfloat16)]
            + [
                lambda f, s, u4, d1, d2, d4: attend(
                    [Block(d1, frame, 1, 0), Block(d2, frame, 1, 0)],
                    own_pairs(f, s, 1) + kvs_pairs(u4),
                    [],
                    PER,
                    out_rows=two,
                    name="visit",
                )
            ]
            + [lambda f, s, u4, d1, d2, d4: join(Block(d4, frame, 0, 0), u4, f, s, 0, two)]
            + [lambda f, s, u4, d1, d2, d4: jnp.zeros((two, CW), jnp.bfloat16)],
            frame_kv,
            sink,
            up4,
            down1,
            down2,
            down4,
        ),
        [(1, 2), (2, 3)],
    )
    down6 = move(
        choose(
            [lambda s, r: r] * 2 + [lambda s, r: fill(s, same)] * 2,
            own_sink,
            down4,
        ),
        [(2, 1), (1, 0)],
    )
    stages.append(
        spread(
            choose(
                [
                    lambda u3, u5, d4, d6: d6[:prompt_size],
                    lambda u3, u5, d4, d6: d4[:prompt_size],
                    lambda u3, u5, d4, d6: u3[:prompt_size],
                    lambda u3, u5, d4, d6: u5[:prompt_size],
                ],
                up3,
                up5,
                down4,
                down6,
            )
        )
    )
    up7 = move(
        choose(
            [lambda f, s, u2, u5, d3, d5: jnp.zeros((two, CW), jnp.bfloat16)]
            + [
                lambda f, s, u2, u5, d3, d5: attend(
                    [Block(d5, frame, 0, 0), Block(d5, frame, 1, 0)],
                    own_pairs(f, s, 2) + kvs_pairs(u5),
                    [],
                    PER,
                    out_rows=two,
                    name="visit",
                )
            ]
            + [
                lambda f, s, u2, u5, d3, d5: attend(
                    [Block(d3, frame, 1, 0)],
                    own_pairs(f, s, 3) + kvs_pairs(u2) + kvs_pairs(u5),
                    [],
                    PER,
                    out_rows=two,
                    name="all_d",
                )
            ]
            + [lambda f, s, u2, u5, d3, d5: jnp.zeros((two, CW), jnp.bfloat16)],
            frame_kv,
            sink,
            up2,
            up5,
            down3,
            down5,
        ),
        [(1, 2), (2, 3)],
    )
    down7 = move(down5, [(2, 1)])
    last8 = move(
        choose(
            [lambda f, s, u6, d4, d6: d6] * 2
            + [lambda f, s, u6, d4, d6: join(Block(d4, frame, 1, 0), u6, f, s, 1, same)]
            + [lambda f, s, u6, d4, d6: d6],
            frame_kv,
            sink,
            up6,
            down4,
            down6,
        ),
        [(2, 3), (1, 0)],
    )
    down9 = move(down7, [(1, 0)])
    up9 = move(
        choose(
            [lambda f, s, u7, d3: jnp.zeros((part_rows, CW), jnp.bfloat16)] * 2
            + [lambda f, s, u7, d3: join(Block(d3, frame, 0, 0), u7, f, s, 2, part_rows)]
            + [lambda f, s, u7, d3: jnp.zeros((part_rows, CW), jnp.bfloat16)],
            frame_kv,
            sink,
            up7,
            down3,
        ),
        [(2, 3)],
    )

    mine = [stage[0] for stage in stages]
    theirs = [stage[1] for stage in stages]
    cross_out = cross(cross_queries, mine + theirs)

    def finish(q, h, pairs_of, parts_of):
        out = None
        for chunk in range(CHUNKS):
            out = attend(
                [own_query(q, chunk)],
                pairs_of(chunk),
                [Block(h, part_rows, 0, chunk * PER)] + parts_of(chunk),
                PER,
                final=(out, q.shape, chunk * PER),
                name="finish",
            )
        return out

    def finish0(q, h, u, d, l8, d9, u9):
        late = [d[2], l8, d9]
        return finish(q, h, lambda c: [sink_pair(each, c) for each in late], lambda c: [])

    def finish1(q, h, u, d, l8, d9, u9):
        late = [d[6], d[7]]
        came = [u[2], u[4], u[5], u[3]]
        return finish(
            q,
            h,
            lambda c: kvs_pairs(came[c]) + [sink_pair(each, c) for each in late],
            lambda c: [],
        )

    def finish2(q, h, u, d, l8, d9, u9):
        came = [u[4], u[6], u[7]]
        return finish(
            q,
            h,
            lambda c: [sink_pair(d[5], c)] + ((kvs_pairs(u[2]) + kvs_pairs(u[5])) if c == 3 else []),
            lambda c: [part(came[c], 0)] if c < 3 else [],
        )

    def finish3(q, h, u, d, l8, d9, u9):
        came = [u[6], l8, u9, u[7]]
        return finish(q, h, lambda c: [], lambda c: [part(came[c], 0)])

    ups = {2: up2, 3: up3, 4: up4, 5: up5, 6: up6, 7: up7}
    downs = {2: down2, 5: down5, 6: down6, 7: down7}
    self_out = choose(
        [finish0, finish1, finish2, finish3], queries, home, ups, downs, last8, down9, up9
    )
    return (self_out, cross_out)


def cross(queries, arrays):
    frame = queries.shape[0]

    def kernel(*refs):
        query, out = refs[0], refs[-1]
        keys, values = stacked(refs[1:-1:2]), stacked(refs[2:-1:2])
        _, total, blended = fresh_state(query[...], keys, values)
        out[...] = (blended / total).astype(jnp.bfloat16)

    operands, in_specs = [queries], [pl.BlockSpec((frame, HDIM), lambda head: (0, head))]
    for array in arrays:
        rows = array.shape[0] // (2 * CHUNKS)
        operands += [array, array]
        in_specs += [
            pl.BlockSpec((rows, HDIM), lambda head: (head // PER, head % PER)),
            pl.BlockSpec((rows, HDIM), lambda head: (CHUNKS + head // PER, head % PER)),
        ]
    key_rows = sum(array.shape[0] for array in arrays) // (2 * CHUNKS)
    return pl.pallas_call(
        kernel,
        out_shape=jax.ShapeDtypeStruct(queries.shape, jnp.bfloat16),
        grid=(HEADS,),
        in_specs=in_specs,
        out_specs=pl.BlockSpec((frame, HDIM), lambda head: (0, head)),
        compiler_params=pltpu.CompilerParams(vmem_limit_bytes=VMEM),
        cost_estimate=pl.CostEstimate(
            flops=4 * HEADS * frame * key_rows * HDIM,
            bytes_accessed=2 * WIDTH * (2 * frame + 2 * key_rows),
            transcendentals=HEADS * frame * key_rows,
        ),
        name="cross",
    )(*operands)


def solution(mesh):
    in_specs = (
        P(("groups", "span"), None),
        P(("groups", "span"), None),
        P(("groups", "span"), None),
        P(("groups", "span"), None, None),
        P("groups", "span", None),
        P("groups"),
    )
    out_specs = (P(("groups", "span"), None), P(("groups", "span"), None))
    return jax.shard_map(shards, mesh=mesh, in_specs=in_specs, out_specs=out_specs, check_vma=False)
```

```python
import math

import jax
import jax.numpy as jnp
from jax import lax
from jax.experimental import pallas as pl
from jax.experimental.pallas import tpu as pltpu
from jax.sharding import PartitionSpec as P

HEADS = 20
HDIM = 128
WIN = 4
CHUNKS = 4
PER = HEADS // CHUNKS
CW = PER * HDIM
WIDTH = HEADS * HDIM
STAT = 16
LOG_SCALE = math.log2(math.e) / math.sqrt(HDIM)
VMEM = 48 * 1024 * 1024
ANYWHERE = pl.BlockSpec(memory_space=pl.ANY)
SCALAR = pl.BlockSpec(memory_space=pltpu.SMEM)
INSIDE = pl.BlockSpec(memory_space=pltpu.VMEM)


def diagonal():
    rows = lax.broadcasted_iota(jnp.int32, (HDIM, HDIM), 0)
    cols = lax.broadcasted_iota(jnp.int32, (HDIM, HDIM), 1)
    return rows == cols


def stat_rows(column):
    eye = diagonal()
    groups = column.shape[0] // HDIM
    tops, mids, lows = [], [], []
    for group in range(groups):
        part = column[group * HDIM : (group + 1) * HDIM]
        row = jnp.sum(jnp.where(eye, part, 0.0), axis=0, keepdims=True)
        top = row.astype(jnp.bfloat16).astype(jnp.float32)
        mid = (row - top).astype(jnp.bfloat16).astype(jnp.float32)
        tops.append(top)
        mids.append(mid)
        lows.append(row - top - mid)
    used = tops + mids + lows
    used.append(jnp.zeros((STAT - len(used), HDIM), jnp.float32))
    return jnp.concatenate(used, axis=0).astype(jnp.bfloat16)


def stat_column(tile, groups):
    eye = diagonal()
    tile = tile.astype(jnp.float32)
    columns = []
    for group in range(groups):
        row = (
            tile[group : group + 1]
            + tile[groups + group : groups + group + 1]
            + tile[2 * groups + group : 2 * groups + group + 1]
        )
        columns.append(jnp.sum(jnp.where(eye, row, 0.0), axis=1, keepdims=True))
    return jnp.concatenate(columns, axis=0)


def fresh_state(query, keys, values):
    scores = lax.dot_general(
        query, keys, (((1,), (1,)), ((), ())), preferred_element_type=jnp.float32
    )
    top = jnp.max(scores, axis=1, keepdims=True)
    weights = jnp.exp2((scores - top) * LOG_SCALE).astype(jnp.bfloat16)
    beside = jnp.concatenate([values, jnp.ones_like(values)], axis=1)
    both = jnp.dot(weights, beside, preferred_element_type=jnp.float32)
    return top * LOG_SCALE, both[:, HDIM:], both[:, :HDIM]


def merge_states(states):
    if len(states) == 1:
        return states[0]
    top = states[0][0]
    for state in states[1:]:
        top = jnp.maximum(top, state[0])
    total, blended = 0.0, 0.0
    for state in states:
        factor = jnp.exp2(state[0] - top)
        total = total + state[1] * factor
        blended = blended + state[2] * factor
    return top, total, blended


def stacked(pieces):
    return pieces[0] if len(pieces) == 1 else jnp.concatenate(pieces, axis=0)


class Block:
    def __init__(self, array, row, rows, col=0):
        self.array, self.row, self.rows, self.col = array, row, rows, col


class Operands:
    def __init__(self):
        self.arrays = []

    def index(self, array):
        for at, each in enumerate(self.arrays):
            if each is array:
                return at
        self.arrays.append(array)
        return len(self.arrays) - 1


def attend(jobs, out_shape, name, after=()):
    operands = Operands()

    def located(block):
        return (operands.index(block.array), block.row, block.rows, block.col)

    plan = [
        (
            [located(q) for q in queries],
            [(located(k), located(v)) for k, v in pairs],
            [located(p) for p in parts],
            out_col,
        )
        for queries, pairs, parts, out_col in jobs
    ]
    count = len(operands.arrays)

    def kernel(*refs):
        out = refs[-1]

        def read(where, head):
            at, row, rows, col = where
            return refs[at][row : row + rows, col + head * HDIM : col + (head + 1) * HDIM]

        for queries, pairs, parts, out_col in plan:
            for head in range(PER):
                if pairs:
                    keys = stacked([read(k, head) for k, _ in pairs])
                    values = stacked([read(v, head) for _, v in pairs])
                cols = slice(head * HDIM, (head + 1) * HDIM)
                for at, query in enumerate(queries):
                    frame = query[2]
                    states = []
                    if pairs:
                        states.append(fresh_state(read(query, head), keys, values))
                    for part in parts:
                        rows = read(part, head)
                        states.append(
                            (
                                stat_column(rows[frame : frame + STAT], frame // HDIM),
                                1.0,
                                rows[:frame].astype(jnp.float32),
                            )
                        )
                    top, total, blended = merge_states(states)
                    done = (blended / total).astype(jnp.bfloat16)
                    if out_col is None:
                        start = at * (frame + STAT)
                        out[start : start + frame, cols] = done
                        out[start + frame : start + frame + STAT, cols] = stat_rows(
                            top + jnp.log2(total)
                        )
                    else:
                        out[:, out_col + head * HDIM : out_col + (head + 1) * HDIM] = done

    work = sum(
        PER * len(queries) * queries[0].rows * sum(k.rows for k, _ in pairs)
        for queries, pairs, _, _ in jobs
    )
    return pl.pallas_call(
        kernel,
        out_shape=jax.ShapeDtypeStruct(out_shape, jnp.bfloat16),
        in_specs=[INSIDE] * count + [ANYWHERE] * len(after),
        out_specs=INSIDE,
        compiler_params=pltpu.CompilerParams(vmem_limit_bytes=VMEM),
        cost_estimate=pl.CostEstimate(
            flops=4 * work * HDIM, bytes_accessed=4_000_000, transcendentals=work
        ),
        name=name,
    )(*operands.arrays, *after)


def home(queries, frame_kv, sink):
    frame = queries.shape[0]

    def kernel(query, key, value, sink_key, sink_value, out):
        for head in range(PER):
            cols = slice(head * HDIM, (head + 1) * HDIM)
            keys = jnp.concatenate([key[:, cols], sink_key[:, cols]], axis=0)
            values = jnp.concatenate([value[:, cols], sink_value[:, cols]], axis=0)
            top, total, blended = fresh_state(query[:, cols], keys, values)
            out[:frame, cols] = (blended / total).astype(jnp.bfloat16)
            out[frame:, cols] = stat_rows(top + jnp.log2(total))

    def block(array, first):
        return pl.BlockSpec((array.shape[0], CW), lambda at: (0, first + at))

    return pl.pallas_call(
        kernel,
        out_shape=jax.ShapeDtypeStruct((frame + STAT, WIDTH), jnp.bfloat16),
        grid=(CHUNKS,),
        in_specs=[
            block(queries, 0),
            block(frame_kv, 0),
            block(frame_kv, CHUNKS),
            block(sink, 0),
            block(sink, CHUNKS),
        ],
        out_specs=pl.BlockSpec((frame + STAT, CW), lambda at: (0, at)),
        compiler_params=pltpu.CompilerParams(vmem_limit_bytes=VMEM),
        cost_estimate=pl.CostEstimate(
            flops=4 * WIDTH * frame * (frame + sink.shape[0]),
            bytes_accessed=6_000_000,
            transcendentals=HEADS * frame * (frame + sink.shape[0]),
        ),
        name="home",
    )(queries, frame_kv, frame_kv, sink, sink)


def cross(queries, shards, pick, prompt_rows):
    frame = queries.shape[0]
    step = 2 * prompt_rows

    def kernel(pick_ref, query, *refs):
        out = refs[-1]
        picked = pick_ref[0] * prompt_rows

        def chunk(at, carry):
            def rows(ref, which):
                start = pl.multiple_of(which * step + picked, 8)
                return ref.at[pl.ds(start, prompt_rows)]

            first = pl.multiple_of(at * CW, HDIM)
            for head in range(PER):
                cols = pl.ds(head * HDIM, HDIM)
                keys = stacked([rows(ref, at)[:, cols] for ref in refs[:-1]])
                values = stacked([rows(ref, CHUNKS + at)[:, cols] for ref in refs[:-1]])
                here = pl.ds(first + head * HDIM, HDIM)
                _, total, blended = fresh_state(query[:, here], keys, values)
                out[:, here] = (blended / total).astype(jnp.bfloat16)
            return carry

        lax.fori_loop(0, CHUNKS, chunk, 0)

    work = HEADS * frame * prompt_rows * len(shards)
    return pl.pallas_call(
        kernel,
        out_shape=jax.ShapeDtypeStruct(queries.shape, jnp.bfloat16),
        in_specs=[SCALAR] + [INSIDE] * (1 + len(shards)),
        out_specs=INSIDE,
        compiler_params=pltpu.CompilerParams(vmem_limit_bytes=VMEM),
        cost_estimate=pl.CostEstimate(
            flops=4 * work * HDIM, bytes_accessed=12_000_000, transcendentals=work
        ),
        name="cross",
    )(pick, queries, *shards)


def pack(place, rows, plans, onto=None, name="pack"):
    operands = Operands()
    located = {
        at: [(operands.index(block.array), block, first) for block, first in items]
        for at, items in plans.items()
    }
    most = max(len(items) for items in located.values())
    arrays = operands.arrays
    aliases = {}
    if onto is not None:
        aliases = {1 + len(arrays): 0}
        arrays = arrays + [onto]

    def kernel(place_ref, *refs):
        out, sems = refs[-2], refs[-1]
        for at, items in located.items():

            @pl.when(place_ref[0] == at)
            def _():
                copies = [
                    pltpu.make_async_copy(
                        refs[which].at[
                            pl.ds(block.row, block.rows), pl.ds(block.col, CW)
                        ],
                        out.at[pl.ds(first, block.rows), :],
                        sems.at[n],
                    )
                    for n, (which, block, first) in enumerate(items)
                ]
                for copy in copies:
                    copy.start()
                for copy in copies:
                    copy.wait()

    return pl.pallas_call(
        kernel,
        out_shape=jax.ShapeDtypeStruct((rows, CW), jnp.bfloat16),
        in_specs=[SCALAR] + [ANYWHERE] * len(arrays),
        out_specs=ANYWHERE,
        scratch_shapes=[pltpu.SemaphoreType.DMA((most,))],
        input_output_aliases=aliases,
        cost_estimate=pl.CostEstimate(flops=0, bytes_accessed=2_000_000, transcendentals=0),
        name=name,
    )(place, *arrays)


def unused(rows):
    return pl.pallas_call(
        lambda out: None,
        out_shape=jax.ShapeDtypeStruct((rows, CW), jnp.bfloat16),
        out_specs=ANYWHERE,
        name="unused",
    )()


def shards(queries, cross_queries, frame_kv, sink_kv, prompt_kv, switch):
    streams = lax.axis_size("span") // WIN
    device = lax.axis_index("span")
    place = device // streams
    stream = device % streams
    frame = queries.shape[0]
    sink = sink_kv.reshape(sink_kv.shape[1], sink_kv.shape[2])
    sink_rows = sink.shape[0]
    prompt_rows = prompt_kv.shape[1]
    prompt_both = prompt_kv.reshape(2 * prompt_rows, prompt_kv.shape[2])
    part_rows = frame + STAT
    place_ref = place.reshape(1).astype(jnp.int32)

    def move(value, *pairs):
        both = [(a * streams + s, b * streams + s) for a, b in pairs for s in range(streams)]
        return lax.ppermute(value, "span", both)

    def across(value, flip):
        pairs = [(at, at - at % streams + ((at % streams) ^ flip)) for at in range(WIN * streams)]
        return lax.ppermute(value, "span", pairs)

    def choose(branches, *operands):
        return lax.switch(place, branches, *operands)

    def columns(array, height):
        count = array.shape[1] // CW
        return [(Block(array, 0, height, at * CW), at * height) for at in range(count)]

    def query_chunks(array, *chunks):
        return [
            (Block(array, 0, frame, chunk * CW), at * frame) for at, chunk in enumerate(chunks)
        ]

    def kvs(frame_array, sink_array, chunk):
        low = chunk * CW
        return [
            (Block(frame_array, 0, frame, low), 0),
            (Block(frame_array, 0, frame, WIDTH + low), frame),
            (Block(sink_array, 0, sink_rows, low), 2 * frame),
            (Block(sink_array, 0, sink_rows, WIDTH + low), 2 * frame + sink_rows),
        ]

    def whole(array, rows):
        return [(Block(array, 0, rows), 0)]

    def own_pairs(frame_array, sink_array, chunk):
        low = chunk * CW
        return [
            (Block(frame_array, 0, frame, low), Block(frame_array, 0, frame, WIDTH + low)),
            (Block(sink_array, 0, sink_rows, low), Block(sink_array, 0, sink_rows, WIDTH + low)),
        ]

    def kvs_pairs(array):
        return [
            (Block(array, 0, frame), Block(array, frame, frame)),
            (
                Block(array, 2 * frame, sink_rows),
                Block(array, 2 * frame + sink_rows, sink_rows),
            ),
        ]

    def sink_pair(array, chunk):
        return (
            Block(array, chunk * sink_rows, sink_rows),
            Block(array, (CHUNKS + chunk) * sink_rows, sink_rows),
        )

    def part(array, index=0, col=0):
        return Block(array, index * part_rows, part_rows, col)

    def spread(shard):
        held = [shard]
        flip = streams // 2
        while flip > 0:
            held = held + [across(each, flip) for each in held]
            flip //= 2
        return held

    stream_ids = jnp.arange(switch.shape[0], dtype=jnp.int32)
    switch_at = jnp.sum(jnp.where(stream_ids == stream, switch, 0))
    pick = (place >= switch_at).astype(jnp.int32).reshape(1)

    prompt_size = 4 * CHUNKS * prompt_rows
    sink_size = 2 * CHUNKS * sink_rows
    same = max(prompt_size, 2 * frame, sink_size)
    kvs_rows = 2 * frame + 2 * sink_rows
    wide = max(kvs_rows, prompt_size, 2 * part_rows)
    two = 2 * part_rows

    prompt = pack(
        place_ref, prompt_size, {p: columns(prompt_both, 2 * prompt_rows) for p in range(WIN)}, name="prompt"
    )
    up_a = move(prompt, (0, 1), (1, 2), (2, 3))
    down_b = move(
        pack(
            place_ref,
            same,
            {1: whole(prompt, prompt_size), 2: query_chunks(queries, 0, 1), 3: whole(prompt, prompt_size)},
            name="down_b",
        ),
        (3, 2),
        (2, 1),
        (1, 0),
    )
    up_c = move(
        pack(
            place_ref,
            kvs_rows,
            {0: kvs(frame_kv, sink, 3), 1: kvs(frame_kv, sink, 3)},
            name="up_c",
        ),
        (0, 1),
        (1, 2),
    )
    down_d = move(
        pack(
            place_ref,
            same,
            {1: columns(sink, sink_rows), 3: query_chunks(queries, 0, 1)},
            name="down_d",
        ),
        (3, 1),
        (1, 0),
    )
    stages = spread(prompt)
    at_home = home(queries, frame_kv, sink)

    up_a = pack(place_ref, prompt_size, {0: whole(down_b, prompt_size)}, onto=up_a, name="first_shard")
    up_e = move(
        pack(
            place_ref,
            wide,
            {
                0: kvs(frame_kv, sink, 0),
                1: whole(up_a, prompt_size),
                2: whole(up_a, prompt_size),
            },
            name="up_e",
        ),
        (0, 1),
        (1, 2),
        (2, 3),
    )
    down_f = move(
        pack(
            place_ref,
            same,
            {2: whole(prompt, prompt_size), 3: query_chunks(queries, 2, 3)},
            name="down_f",
        ),
        (3, 2),
        (2, 1),
    )
    stages += spread(up_a)

    up_c = pack(place_ref, kvs_rows, {0: kvs(frame_kv, sink, 1)}, onto=up_c, name="up_g")
    up_g = move(up_c, (0, 1), (1, 2))
    down_b = pack(place_ref, same, {3: query_chunks(queries, 0, 1)}, onto=down_b, name="down_g")
    down_g = move(down_b, (3, 2), (2, 1))

    def visit(q2, q3, came, frame_array, sink_array, chunk, rows, after=()):
        return attend(
            [([q2, q3], own_pairs(frame_array, sink_array, chunk) + kvs_pairs(came), [], None)],
            (rows, CW),
            "visit",
            after,
        )

    def join(query, came, frame_array, sink_array, chunk, rows):
        return attend(
            [([query], own_pairs(frame_array, sink_array, chunk), [part(came, 1)], None)],
            (rows, CW),
            "join",
        )

    def branch_pack(rows, items):
        return pack(jnp.zeros((1,), jnp.int32), rows, {0: items}, name="branch")

    up_h = move(
        choose(
            [
                lambda f, s, e, b, d, h: branch_pack(wide, kvs(f, s, 2)),
                lambda f, s, e, b, d, h: visit(
                    Block(b, 0, frame), Block(d, 0, frame), e, f, s, 0, wide, (h,)
                ),
                lambda f, s, e, b, d, h: branch_pack(wide, whole(e, prompt_size)),
                lambda f, s, e, b, d, h: unused(wide),
            ],
            frame_kv,
            sink,
            up_e,
            down_b,
            down_d,
            at_home,
        ),
        (0, 1),
        (1, 2),
        (2, 3),
    )
    down_k = move(
        pack(
            place_ref,
            same,
            {
                1: whole(down_f, prompt_size),
                2: [(Block(queries, 0, frame, 2 * CW), 0), (Block(down_f, 0, frame), frame)],
                3: columns(sink, sink_rows),
            },
            name="down_k",
        ),
        (3, 2),
        (2, 1),
        (1, 0),
    )
    stages += spread(
        pack(
            place_ref,
            prompt_size,
            {
                0: whole(down_k, prompt_size),
                1: whole(down_f, prompt_size),
                2: whole(down_b, prompt_size),
                3: whole(up_e, prompt_size),
            },
            name="third_shard",
        )
    )

    up_j = move(
        choose(
            [
                lambda f, s, c, g, b, d, fd: unused(two),
                lambda f, s, c, g, b, d, fd: visit(
                    Block(b, frame, frame), Block(d, frame, frame), g, f, s, 1, two
                ),
                lambda f, s, c, g, b, d, fd: attend(
                    [
                        (
                            [Block(fd, frame, frame)],
                            own_pairs(f, s, 3) + kvs_pairs(c) + kvs_pairs(g),
                            [],
                            None,
                        )
                    ],
                    (two, CW),
                    "all_d",
                ),
                lambda f, s, c, g, b, d, fd: unused(two),
            ],
            frame_kv,
            sink,
            up_c,
            up_g,
            down_b,
            down_d,
            down_f,
        ),
        (1, 2),
        (2, 3),
    )
    down_l = move(
        pack(
            place_ref,
            same,
            {1: whole(down_g, same), 2: columns(sink, sink_rows)},
            name="down_l",
        ),
        (2, 1),
        (1, 0),
    )
    stages += spread(
        pack(
            place_ref,
            prompt_size,
            {
                0: whole(down_l, prompt_size),
                1: whole(down_g, prompt_size),
                2: whole(up_e, prompt_size),
                3: whole(up_h, prompt_size),
            },
            name="last_shard",
        )
    )

    up_n = move(
        choose(
            [
                lambda f, s, h, k, g: unused(two),
                lambda f, s, h, k, g: visit(
                    Block(k, 0, frame), Block(k, frame, frame), h, f, s, 2, two
                ),
                lambda f, s, h, k, g: join(Block(g, 0, frame), h, f, s, 0, two),
                lambda f, s, h, k, g: unused(two),
            ],
            frame_kv,
            sink,
            up_h,
            down_k,
            down_g,
        ),
        (1, 2),
        (2, 3),
    )
    down_m = move(down_k, (2, 1))
    last_o = move(
        choose(
            [
                lambda f, s, j, g, l: unused(same),
                lambda f, s, j, g, l: branch_pack(same, whole(l, sink_size)),
                lambda f, s, j, g, l: join(Block(g, frame, frame), j, f, s, 1, same),
                lambda f, s, j, g, l: unused(same),
            ],
            frame_kv,
            sink,
            up_j,
            down_g,
            down_l,
        ),
        (2, 3),
        (1, 0),
    )
    down_r = move(down_m, (1, 0))
    up_q = move(
        choose(
            [
                lambda f, s, n, d: unused(part_rows),
                lambda f, s, n, d: unused(part_rows),
                lambda f, s, n, d: join(Block(d, 0, frame), n, f, s, 2, part_rows),
                lambda f, s, n, d: unused(part_rows),
            ],
            frame_kv,
            sink,
            up_n,
            down_f,
        ),
        (2, 3),
    )

    cross_out = cross(cross_queries, stages, pick, prompt_rows)

    def finish(q, h, cross_done, pairs_of, parts_of):
        return attend(
            [
                (
                    [Block(q, 0, frame, chunk * CW)],
                    pairs_of(chunk),
                    [part(h, 0, chunk * CW)] + parts_of(chunk),
                    chunk * CW,
                )
                for chunk in range(CHUNKS)
            ],
            q.shape,
            "finish",
            (cross_done,),
        )

    def finish0(q, h, x, u, d):
        late = [d["d"], d["o"], d["r"]]
        return finish(q, h, x, lambda c: [sink_pair(each, c) for each in late], lambda c: [])

    def finish1(q, h, x, u, d):
        late = [d["l"], d["m"]]
        came = [u["e"], u["g"], u["h"], u["c"]]
        return finish(
            q,
            h,
            x,
            lambda c: kvs_pairs(came[c]) + [sink_pair(each, c) for each in late],
            lambda c: [],
        )

    def finish2(q, h, x, u, d):
        came = [u["h"], u["j"], u["n"]]
        return finish(
            q,
            h,
            x,
            lambda c: [sink_pair(d["k"], c)]
            + ((kvs_pairs(u["c"]) + kvs_pairs(u["g"])) if c == 3 else []),
            lambda c: [part(came[c])] if c < 3 else [],
        )

    def finish3(q, h, x, u, d):
        came = [u["n"], d["o"], u["q"], u["j"]]
        return finish(q, h, x, lambda c: [], lambda c: [part(came[c])])

    ups = {"c": up_c, "e": up_e, "g": up_g, "h": up_h, "j": up_j, "n": up_n, "q": up_q}
    downs = {"d": down_d, "k": down_k, "l": down_l, "m": down_m, "o": last_o, "r": down_r}
    self_out = choose(
        [finish0, finish1, finish2, finish3], queries, at_home, cross_out, ups, downs
    )
    return (self_out, cross_out)


def solution(mesh):
    in_specs = (
        P(("groups", "span"), None),
        P(("groups", "span"), None),
        P(("groups", "span"), None),
        P(("groups", "span"), None, None),
        P("groups", "span", None),
        P("groups"),
    )
    out_specs = (P(("groups", "span"), None), P(("groups", "span"), None))
    return jax.shard_map(shards, mesh=mesh, in_specs=in_specs, out_specs=out_specs, check_vma=False)
```

```python
import math

import jax
import jax.numpy as jnp
from jax import lax
from jax.experimental import pallas as pl
from jax.experimental.pallas import tpu as pltpu
from jax.sharding import PartitionSpec as P

HEADS = 20
HDIM = 128
WIN = 4
CHUNKS = 4
PER = HEADS // CHUNKS
CW = PER * HDIM
WIDTH = HEADS * HDIM
STAT = 16
LOG_SCALE = math.log2(math.e) / math.sqrt(HDIM)
VMEM = 48 * 1024 * 1024
ANYWHERE = pl.BlockSpec(memory_space=pl.ANY)
SCALAR = pl.BlockSpec(memory_space=pltpu.SMEM)
INSIDE = pl.BlockSpec(memory_space=pltpu.VMEM)


def diagonal():
    rows = lax.broadcasted_iota(jnp.int32, (HDIM, HDIM), 0)
    cols = lax.broadcasted_iota(jnp.int32, (HDIM, HDIM), 1)
    return rows == cols


def stat_rows(column):
    eye = diagonal()
    groups = column.shape[0] // HDIM
    tops, mids, lows = [], [], []
    for group in range(groups):
        part = column[group * HDIM : (group + 1) * HDIM]
        row = jnp.sum(jnp.where(eye, part, 0.0), axis=0, keepdims=True)
        top = row.astype(jnp.bfloat16).astype(jnp.float32)
        mid = (row - top).astype(jnp.bfloat16).astype(jnp.float32)
        tops.append(top)
        mids.append(mid)
        lows.append(row - top - mid)
    used = tops + mids + lows
    used.append(jnp.zeros((STAT - len(used), HDIM), jnp.float32))
    return jnp.concatenate(used, axis=0).astype(jnp.bfloat16)


def stat_column(tile, groups):
    eye = diagonal()
    tile = tile.astype(jnp.float32)
    columns = []
    for group in range(groups):
        row = (
            tile[group : group + 1]
            + tile[groups + group : groups + group + 1]
            + tile[2 * groups + group : 2 * groups + group + 1]
        )
        columns.append(jnp.sum(jnp.where(eye, row, 0.0), axis=1, keepdims=True))
    return jnp.concatenate(columns, axis=0)


def fresh_state(query, keys, values):
    scores = lax.dot_general(
        query, keys, (((1,), (1,)), ((), ())), preferred_element_type=jnp.float32
    )
    top = jnp.max(scores, axis=1, keepdims=True)
    weights = jnp.exp2((scores - top) * LOG_SCALE).astype(jnp.bfloat16)
    beside = jnp.concatenate([values, jnp.ones_like(values)], axis=1)
    both = jnp.dot(weights, beside, preferred_element_type=jnp.float32)
    return top * LOG_SCALE, both[:, HDIM:], both[:, :HDIM]


def merge_states(states):
    if len(states) == 1:
        return states[0]
    top = states[0][0]
    for state in states[1:]:
        top = jnp.maximum(top, state[0])
    total, blended = 0.0, 0.0
    for state in states:
        factor = jnp.exp2(state[0] - top)
        total = total + state[1] * factor
        blended = blended + state[2] * factor
    return top, total, blended


def stacked(pieces):
    return pieces[0] if len(pieces) == 1 else jnp.concatenate(pieces, axis=0)


class Block:
    def __init__(self, array, row, rows, col=0):
        self.array, self.row, self.rows, self.col = array, row, rows, col


class Operands:
    def __init__(self):
        self.arrays = []

    def index(self, array):
        for at, each in enumerate(self.arrays):
            if each is array:
                return at
        self.arrays.append(array)
        return len(self.arrays) - 1


def attend(jobs, out_shape, name, after=()):
    operands = Operands()

    def located(block):
        return (operands.index(block.array), block.row, block.rows, block.col)

    plan = [
        (
            [located(q) for q in queries],
            [(located(k), located(v)) for k, v in pairs],
            [located(p) for p in parts],
            out_col,
        )
        for queries, pairs, parts, out_col in jobs
    ]
    count = len(operands.arrays)

    def kernel(*refs):
        out = refs[-1]

        def read(where, head):
            at, row, rows, col = where
            return refs[at][row : row + rows, col + head * HDIM : col + (head + 1) * HDIM]

        for queries, pairs, parts, out_col in plan:
            for head in range(PER):
                if pairs:
                    keys = stacked([read(k, head) for k, _ in pairs])
                    values = stacked([read(v, head) for _, v in pairs])
                cols = slice(head * HDIM, (head + 1) * HDIM)
                for at, query in enumerate(queries):
                    frame = query[2]
                    states = []
                    if pairs:
                        states.append(fresh_state(read(query, head), keys, values))
                    for part in parts:
                        rows = read(part, head)
                        states.append(
                            (
                                stat_column(rows[frame : frame + STAT], frame // HDIM),
                                1.0,
                                rows[:frame].astype(jnp.float32),
                            )
                        )
                    top, total, blended = merge_states(states)
                    done = (blended / total).astype(jnp.bfloat16)
                    if out_col is None:
                        start = at * (frame + STAT)
                        out[start : start + frame, cols] = done
                        out[start + frame : start + frame + STAT, cols] = stat_rows(
                            top + jnp.log2(total)
                        )
                    else:
                        out[:, out_col + head * HDIM : out_col + (head + 1) * HDIM] = done

    work = sum(
        PER * len(queries) * queries[0].rows * sum(k.rows for k, _ in pairs)
        for queries, pairs, _, _ in jobs
    )
    return pl.pallas_call(
        kernel,
        out_shape=jax.ShapeDtypeStruct(out_shape, jnp.bfloat16),
        in_specs=[INSIDE] * count + [ANYWHERE] * len(after),
        out_specs=INSIDE,
        compiler_params=pltpu.CompilerParams(vmem_limit_bytes=VMEM),
        cost_estimate=pl.CostEstimate(
            flops=4 * work * HDIM, bytes_accessed=4_000_000, transcendentals=work
        ),
        name=name,
    )(*operands.arrays, *after)


def home(queries, frame_kv, sink):
    frame = queries.shape[0]

    def kernel(query, key, value, sink_key, sink_value, out):
        for head in range(PER):
            cols = slice(head * HDIM, (head + 1) * HDIM)
            keys = jnp.concatenate([key[:, cols], sink_key[:, cols]], axis=0)
            values = jnp.concatenate([value[:, cols], sink_value[:, cols]], axis=0)
            top, total, blended = fresh_state(query[:, cols], keys, values)
            out[:frame, cols] = (blended / total).astype(jnp.bfloat16)
            out[frame:, cols] = stat_rows(top + jnp.log2(total))

    def block(array, first):
        return pl.BlockSpec((array.shape[0], CW), lambda at: (0, first + at))

    return pl.pallas_call(
        kernel,
        out_shape=jax.ShapeDtypeStruct((frame + STAT, WIDTH), jnp.bfloat16),
        grid=(CHUNKS,),
        in_specs=[
            block(queries, 0),
            block(frame_kv, 0),
            block(frame_kv, CHUNKS),
            block(sink, 0),
            block(sink, CHUNKS),
        ],
        out_specs=pl.BlockSpec((frame + STAT, CW), lambda at: (0, at)),
        compiler_params=pltpu.CompilerParams(vmem_limit_bytes=VMEM),
        cost_estimate=pl.CostEstimate(
            flops=4 * WIDTH * frame * (frame + sink.shape[0]),
            bytes_accessed=6_000_000,
            transcendentals=HEADS * frame * (frame + sink.shape[0]),
        ),
        name="home",
    )(queries, frame_kv, frame_kv, sink, sink)


def cross(queries, shards, pick, prompt_rows):
    frame = queries.shape[0]
    step = 2 * prompt_rows

    def kernel(pick_ref, query, *refs):
        out = refs[-1]
        picked = pick_ref[0] * prompt_rows

        def chunk(at, carry):
            def rows(ref, which):
                start = pl.multiple_of(which * step + picked, 8)
                return ref.at[pl.ds(start, prompt_rows)]

            first = pl.multiple_of(at * CW, HDIM)
            for head in range(PER):
                cols = pl.ds(head * HDIM, HDIM)
                keys = stacked([rows(ref, at)[:, cols] for ref in refs[:-1]])
                values = stacked([rows(ref, CHUNKS + at)[:, cols] for ref in refs[:-1]])
                here = pl.ds(first + head * HDIM, HDIM)
                _, total, blended = fresh_state(query[:, here], keys, values)
                out[:, here] = (blended / total).astype(jnp.bfloat16)
            return carry

        lax.fori_loop(0, CHUNKS, chunk, 0)

    work = HEADS * frame * prompt_rows * len(shards)
    return pl.pallas_call(
        kernel,
        out_shape=jax.ShapeDtypeStruct(queries.shape, jnp.bfloat16),
        in_specs=[SCALAR] + [INSIDE] * (1 + len(shards)),
        out_specs=INSIDE,
        compiler_params=pltpu.CompilerParams(vmem_limit_bytes=VMEM),
        cost_estimate=pl.CostEstimate(
            flops=4 * work * HDIM, bytes_accessed=12_000_000, transcendentals=work
        ),
        name="cross",
    )(pick, queries, *shards)


def pack(place, rows, plans, name="pack"):
    operands = Operands()
    located = {
        at: [(operands.index(block.array), block, first) for block, first in items]
        for at, items in plans.items()
    }
    most = max(len(items) for items in located.values())

    def kernel(place_ref, *refs):
        out, sems = refs[-2], refs[-1]
        for at, items in located.items():

            @pl.when(place_ref[0] == at)
            def _():
                copies = [
                    pltpu.make_async_copy(
                        refs[which].at[pl.ds(block.row, block.rows), pl.ds(block.col, CW)],
                        out.at[pl.ds(first, block.rows), :],
                        sems.at[n],
                    )
                    for n, (which, block, first) in enumerate(items)
                ]
                for copy in copies:
                    copy.start()
                for copy in copies:
                    copy.wait()

    return pl.pallas_call(
        kernel,
        out_shape=jax.ShapeDtypeStruct((rows, CW), jnp.bfloat16),
        in_specs=[SCALAR] + [ANYWHERE] * len(operands.arrays),
        out_specs=INSIDE,
        scratch_shapes=[pltpu.SemaphoreType.DMA((most,))],
        cost_estimate=pl.CostEstimate(flops=0, bytes_accessed=2_000_000, transcendentals=0),
        name=name,
    )(place, *operands.arrays)


def unused(rows):
    return pl.pallas_call(
        lambda out: None,
        out_shape=jax.ShapeDtypeStruct((rows, CW), jnp.bfloat16),
        out_specs=INSIDE,
        name="unused",
    )()


def shards(queries, cross_queries, frame_kv, sink_kv, prompt_kv, switch):
    streams = lax.axis_size("span") // WIN
    device = lax.axis_index("span")
    place = device // streams
    stream = device % streams
    frame = queries.shape[0]
    sink = sink_kv.reshape(sink_kv.shape[1], sink_kv.shape[2])
    sink_rows = sink.shape[0]
    prompt_rows = prompt_kv.shape[1]
    prompt_both = prompt_kv.reshape(2 * prompt_rows, prompt_kv.shape[2])
    part_rows = frame + STAT
    place_ref = place.reshape(1).astype(jnp.int32)

    def move(value, *pairs):
        both = [(a * streams + s, b * streams + s) for a, b in pairs for s in range(streams)]
        return lax.ppermute(value, "span", both)

    def across(value, flip):
        pairs = [(at, at - at % streams + ((at % streams) ^ flip)) for at in range(WIN * streams)]
        return lax.ppermute(value, "span", pairs)

    def choose(branches, *operands):
        return lax.switch(place, branches, *operands)

    def columns(array, height):
        count = array.shape[1] // CW
        return [(Block(array, 0, height, at * CW), at * height) for at in range(count)]

    def query_chunks(array, *chunks):
        return [
            (Block(array, 0, frame, chunk * CW), at * frame) for at, chunk in enumerate(chunks)
        ]

    def kvs(frame_array, sink_array, chunk):
        low = chunk * CW
        return [
            (Block(frame_array, 0, frame, low), 0),
            (Block(frame_array, 0, frame, WIDTH + low), frame),
            (Block(sink_array, 0, sink_rows, low), 2 * frame),
            (Block(sink_array, 0, sink_rows, WIDTH + low), 2 * frame + sink_rows),
        ]

    def whole(array, rows):
        return [(Block(array, 0, rows), 0)]

    def own_pairs(frame_array, sink_array, chunk):
        low = chunk * CW
        return [
            (Block(frame_array, 0, frame, low), Block(frame_array, 0, frame, WIDTH + low)),
            (Block(sink_array, 0, sink_rows, low), Block(sink_array, 0, sink_rows, WIDTH + low)),
        ]

    def kvs_pairs(array):
        return [
            (Block(array, 0, frame), Block(array, frame, frame)),
            (
                Block(array, 2 * frame, sink_rows),
                Block(array, 2 * frame + sink_rows, sink_rows),
            ),
        ]

    def sink_pair(array, chunk):
        return (
            Block(array, chunk * sink_rows, sink_rows),
            Block(array, (CHUNKS + chunk) * sink_rows, sink_rows),
        )

    def part(array, index=0, col=0):
        return Block(array, index * part_rows, part_rows, col)

    def spread(shard):
        held = [shard]
        flip = streams // 2
        while flip > 0:
            held = held + [across(each, flip) for each in held]
            flip //= 2
        return held

    stream_ids = jnp.arange(switch.shape[0], dtype=jnp.int32)
    switch_at = jnp.sum(jnp.where(stream_ids == stream, switch, 0))
    pick = (place >= switch_at).astype(jnp.int32).reshape(1)

    prompt_size = 4 * CHUNKS * prompt_rows
    sink_size = 2 * CHUNKS * sink_rows
    same = max(prompt_size, 2 * frame, sink_size)
    kvs_rows = 2 * frame + 2 * sink_rows
    wide = max(kvs_rows, prompt_size, 2 * part_rows)
    two = 2 * part_rows

    prompt = pack(
        place_ref, prompt_size, {p: columns(prompt_both, 2 * prompt_rows) for p in range(WIN)}, name="prompt"
    )
    up_a = move(prompt, (0, 1), (1, 2), (2, 3))
    down_b = move(
        pack(
            place_ref,
            same,
            {1: whole(prompt, prompt_size), 2: query_chunks(queries, 0, 1), 3: whole(prompt, prompt_size)},
            name="down_b",
        ),
        (3, 2),
        (2, 1),
        (1, 0),
    )
    up_c = move(
        pack(
            place_ref,
            kvs_rows,
            {0: kvs(frame_kv, sink, 3), 1: kvs(frame_kv, sink, 3)},
            name="up_c",
        ),
        (0, 1),
        (1, 2),
    )
    down_d = move(
        pack(
            place_ref,
            same,
            {1: columns(sink, sink_rows), 3: query_chunks(queries, 0, 1)},
            name="down_d",
        ),
        (3, 1),
        (1, 0),
    )
    stages = spread(prompt)
    at_home = home(queries, frame_kv, sink)

    second = pack(
        place_ref,
        prompt_size,
        {p: whole(down_b if p == 0 else up_a, prompt_size) for p in range(WIN)},
        name="second_shard",
    )
    up_e = move(
        pack(
            place_ref,
            wide,
            {
                0: kvs(frame_kv, sink, 0),
                1: whole(second, prompt_size),
                2: whole(second, prompt_size),
            },
            name="up_e",
        ),
        (0, 1),
        (1, 2),
        (2, 3),
    )
    down_f = move(
        pack(
            place_ref,
            same,
            {2: whole(prompt, prompt_size), 3: query_chunks(queries, 2, 3)},
            name="down_f",
        ),
        (3, 2),
        (2, 1),
    )
    stages += spread(second)

    up_g = move(
        pack(
            place_ref,
            kvs_rows,
            {0: kvs(frame_kv, sink, 1), 1: whole(up_c, kvs_rows)},
            name="up_g",
        ),
        (0, 1),
        (1, 2),
    )
    down_g = move(
        pack(
            place_ref,
            same,
            {2: whole(down_b, same), 3: query_chunks(queries, 0, 1)},
            name="down_g",
        ),
        (3, 2),
        (2, 1),
    )

    def visit(q2, q3, came, frame_array, sink_array, chunk, rows, after=()):
        return attend(
            [([q2, q3], own_pairs(frame_array, sink_array, chunk) + kvs_pairs(came), [], None)],
            (rows, CW),
            "visit",
            after,
        )

    def join(query, came, frame_array, sink_array, chunk, rows):
        return attend(
            [([query], own_pairs(frame_array, sink_array, chunk), [part(came, 1)], None)],
            (rows, CW),
            "join",
        )

    def branch_pack(rows, items):
        return pack(jnp.zeros((1,), jnp.int32), rows, {0: items}, name="branch")

    up_h = move(
        choose(
            [
                lambda f, s, e, b, d, h: branch_pack(wide, kvs(f, s, 2)),
                lambda f, s, e, b, d, h: visit(
                    Block(b, 0, frame), Block(d, 0, frame), e, f, s, 0, wide, (h,)
                ),
                lambda f, s, e, b, d, h: branch_pack(wide, whole(e, prompt_size)),
                lambda f, s, e, b, d, h: unused(wide),
            ],
            frame_kv,
            sink,
            up_e,
            down_b,
            down_d,
            at_home,
        ),
        (0, 1),
        (1, 2),
        (2, 3),
    )
    down_k = move(
        pack(
            place_ref,
            same,
            {
                1: whole(down_f, prompt_size),
                2: [(Block(queries, 0, frame, 2 * CW), 0), (Block(down_f, 0, frame), frame)],
                3: columns(sink, sink_rows),
            },
            name="down_k",
        ),
        (3, 2),
        (2, 1),
        (1, 0),
    )
    stages += spread(
        pack(
            place_ref,
            prompt_size,
            {
                0: whole(down_k, prompt_size),
                1: whole(down_f, prompt_size),
                2: whole(down_b, prompt_size),
                3: whole(up_e, prompt_size),
            },
            name="third_shard",
        )
    )

    up_j = move(
        choose(
            [
                lambda f, s, c, g, b, d, fd: unused(two),
                lambda f, s, c, g, b, d, fd: visit(
                    Block(b, frame, frame), Block(d, frame, frame), g, f, s, 1, two
                ),
                lambda f, s, c, g, b, d, fd: attend(
                    [
                        (
                            [Block(fd, frame, frame)],
                            own_pairs(f, s, 3) + kvs_pairs(c) + kvs_pairs(g),
                            [],
                            None,
                        )
                    ],
                    (two, CW),
                    "all_d",
                ),
                lambda f, s, c, g, b, d, fd: unused(two),
            ],
            frame_kv,
            sink,
            up_c,
            up_g,
            down_b,
            down_d,
            down_f,
        ),
        (1, 2),
        (2, 3),
    )
    down_l = move(
        pack(
            place_ref,
            same,
            {1: whole(down_g, same), 2: columns(sink, sink_rows)},
            name="down_l",
        ),
        (2, 1),
        (1, 0),
    )
    stages += spread(
        pack(
            place_ref,
            prompt_size,
            {
                0: whole(down_l, prompt_size),
                1: whole(down_g, prompt_size),
                2: whole(up_e, prompt_size),
                3: whole(up_h, prompt_size),
            },
            name="last_shard",
        )
    )

    up_n = move(
        choose(
            [
                lambda f, s, h, k, g: unused(two),
                lambda f, s, h, k, g: visit(
                    Block(k, 0, frame), Block(k, frame, frame), h, f, s, 2, two
                ),
                lambda f, s, h, k, g: join(Block(g, 0, frame), h, f, s, 0, two),
                lambda f, s, h, k, g: unused(two),
            ],
            frame_kv,
            sink,
            up_h,
            down_k,
            down_g,
        ),
        (1, 2),
        (2, 3),
    )
    down_m = move(down_k, (2, 1))
    last_o = move(
        choose(
            [
                lambda f, s, j, g, l: unused(same),
                lambda f, s, j, g, l: branch_pack(same, whole(l, sink_size)),
                lambda f, s, j, g, l: join(Block(g, frame, frame), j, f, s, 1, same),
                lambda f, s, j, g, l: unused(same),
            ],
            frame_kv,
            sink,
            up_j,
            down_g,
            down_l,
        ),
        (2, 3),
        (1, 0),
    )
    down_r = move(down_m, (1, 0))
    up_q = move(
        choose(
            [
                lambda f, s, n, d: unused(part_rows),
                lambda f, s, n, d: unused(part_rows),
                lambda f, s, n, d: join(Block(d, 0, frame), n, f, s, 2, part_rows),
                lambda f, s, n, d: unused(part_rows),
            ],
            frame_kv,
            sink,
            up_n,
            down_f,
        ),
        (2, 3),
    )

    cross_out = cross(cross_queries, stages, pick, prompt_rows)

    def finish(q, h, cross_done, pairs_of, parts_of):
        return attend(
            [
                (
                    [Block(q, 0, frame, chunk * CW)],
                    pairs_of(chunk),
                    [part(h, 0, chunk * CW)] + parts_of(chunk),
                    chunk * CW,
                )
                for chunk in range(CHUNKS)
            ],
            q.shape,
            "finish",
            (cross_done,),
        )

    def finish0(q, h, x, u, d):
        late = [d["d"], d["o"], d["r"]]
        return finish(q, h, x, lambda c: [sink_pair(each, c) for each in late], lambda c: [])

    def finish1(q, h, x, u, d):
        late = [d["l"], d["m"]]
        came = [u["e"], u["g"], u["h"], u["c"]]
        return finish(
            q,
            h,
            x,
            lambda c: kvs_pairs(came[c]) + [sink_pair(each, c) for each in late],
            lambda c: [],
        )

    def finish2(q, h, x, u, d):
        came = [u["h"], u["j"], u["n"]]
        return finish(
            q,
            h,
            x,
            lambda c: [sink_pair(d["k"], c)]
            + ((kvs_pairs(u["c"]) + kvs_pairs(u["g"])) if c == 3 else []),
            lambda c: [part(came[c])] if c < 3 else [],
        )

    def finish3(q, h, x, u, d):
        came = [u["n"], d["o"], u["q"], u["j"]]
        return finish(q, h, x, lambda c: [], lambda c: [part(came[c])])

    ups = {"c": up_c, "e": up_e, "g": up_g, "h": up_h, "j": up_j, "n": up_n, "q": up_q}
    downs = {"d": down_d, "k": down_k, "l": down_l, "m": down_m, "o": last_o, "r": down_r}
    self_out = choose(
        [finish0, finish1, finish2, finish3], queries, at_home, cross_out, ups, downs
    )
    return (self_out, cross_out)


def solution(mesh):
    in_specs = (
        P(("groups", "span"), None),
        P(("groups", "span"), None),
        P(("groups", "span"), None),
        P(("groups", "span"), None, None),
        P("groups", "span", None),
        P("groups"),
    )
    out_specs = (P(("groups", "span"), None), P(("groups", "span"), None))
    return jax.shard_map(shards, mesh=mesh, in_specs=in_specs, out_specs=out_specs, check_vma=False)
```

```python
import math

import jax
import jax.numpy as jnp
from jax import lax
from jax.experimental import pallas as pl
from jax.experimental.pallas import tpu as pltpu
from jax.sharding import PartitionSpec as P

HEADS = 20
HDIM = 128
WIN = 4
CHUNKS = 4
PER = HEADS // CHUNKS
CW = PER * HDIM
WIDTH = HEADS * HDIM
STAT = 16
LOG_SCALE = math.log2(math.e) / math.sqrt(HDIM)
VMEM = 48 * 1024 * 1024
ANYWHERE = pl.BlockSpec(memory_space=pl.ANY)
SCALAR = pl.BlockSpec(memory_space=pltpu.SMEM)
INSIDE = pl.BlockSpec(memory_space=pltpu.VMEM)


def diagonal():
    rows = lax.broadcasted_iota(jnp.int32, (HDIM, HDIM), 0)
    cols = lax.broadcasted_iota(jnp.int32, (HDIM, HDIM), 1)
    return rows == cols


def stat_rows(column):
    eye = diagonal()
    groups = column.shape[0] // HDIM
    tops, mids, lows = [], [], []
    for group in range(groups):
        part = column[group * HDIM : (group + 1) * HDIM]
        row = jnp.sum(jnp.where(eye, part, 0.0), axis=0, keepdims=True)
        top = row.astype(jnp.bfloat16).astype(jnp.float32)
        mid = (row - top).astype(jnp.bfloat16).astype(jnp.float32)
        tops.append(top)
        mids.append(mid)
        lows.append(row - top - mid)
    used = tops + mids + lows
    used.append(jnp.zeros((STAT - len(used), HDIM), jnp.float32))
    return jnp.concatenate(used, axis=0).astype(jnp.bfloat16)


def stat_column(tile, groups):
    eye = diagonal()
    tile = tile.astype(jnp.float32)
    columns = []
    for group in range(groups):
        row = (
            tile[group : group + 1]
            + tile[groups + group : groups + group + 1]
            + tile[2 * groups + group : 2 * groups + group + 1]
        )
        columns.append(jnp.sum(jnp.where(eye, row, 0.0), axis=1, keepdims=True))
    return jnp.concatenate(columns, axis=0)


def fresh_state(query, keys, values):
    scores = lax.dot_general(
        query, keys, (((1,), (1,)), ((), ())), preferred_element_type=jnp.float32
    )
    top = jnp.max(scores, axis=1, keepdims=True)
    weights = jnp.exp2((scores - top) * LOG_SCALE).astype(jnp.bfloat16)
    beside = jnp.concatenate([values, jnp.ones_like(values)], axis=1)
    both = jnp.dot(weights, beside, preferred_element_type=jnp.float32)
    return top * LOG_SCALE, both[:, HDIM:], both[:, :HDIM]


def merge_states(states):
    if len(states) == 1:
        return states[0]
    top = states[0][0]
    for state in states[1:]:
        top = jnp.maximum(top, state[0])
    total, blended = 0.0, 0.0
    for state in states:
        factor = jnp.exp2(state[0] - top)
        total = total + state[1] * factor
        blended = blended + state[2] * factor
    return top, total, blended


def stacked(pieces):
    return pieces[0] if len(pieces) == 1 else jnp.concatenate(pieces, axis=0)


class Block:
    def __init__(self, array, row, rows, col=0):
        self.array, self.row, self.rows, self.col = array, row, rows, col


class Operands:
    def __init__(self):
        self.arrays = []

    def index(self, array):
        for at, each in enumerate(self.arrays):
            if each is array:
                return at
        self.arrays.append(array)
        return len(self.arrays) - 1


def attend(jobs, out_shape, name, after=()):
    operands = Operands()

    def located(block):
        return (operands.index(block.array), block.row, block.rows, block.col)

    plan = [
        (
            [located(q) for q in queries],
            [(located(k), located(v)) for k, v in pairs],
            [located(p) for p in parts],
            out_col,
        )
        for queries, pairs, parts, out_col in jobs
    ]
    count = len(operands.arrays)

    def kernel(*refs):
        out = refs[-1]

        def read(where, head):
            at, row, rows, col = where
            left = pl.multiple_of(col + head * HDIM, HDIM)
            return refs[at][row : row + rows, pl.ds(left, HDIM)]

        def one_job(queries, pairs, parts, out_col):
            def one_head(head, carry):
                if pairs:
                    keys = stacked([read(k, head) for k, _ in pairs])
                    values = stacked([read(v, head) for _, v in pairs])
                cols = pl.ds(pl.multiple_of((out_col or 0) + head * HDIM, HDIM), HDIM)
                for at, query in enumerate(queries):
                    frame = query[2]
                    states = []
                    if pairs:
                        states.append(fresh_state(read(query, head), keys, values))
                    for part in parts:
                        rows = read(part, head)
                        states.append(
                            (
                                stat_column(rows[frame : frame + STAT], frame // HDIM),
                                1.0,
                                rows[:frame].astype(jnp.float32),
                            )
                        )
                    top, total, blended = merge_states(states)
                    done = (blended / total).astype(jnp.bfloat16)
                    if out_col is None:
                        start = at * (frame + STAT)
                        out[start : start + frame, cols] = done
                        out[start + frame : start + frame + STAT, cols] = stat_rows(
                            top + jnp.log2(total)
                        )
                    else:
                        out[:, cols] = done
                return carry

            lax.fori_loop(0, PER, one_head, 0)

        for job in plan:
            one_job(*job)

    work = sum(
        PER * len(queries) * queries[0].rows * sum(k.rows for k, _ in pairs)
        for queries, pairs, _, _ in jobs
    )
    return pl.pallas_call(
        kernel,
        out_shape=jax.ShapeDtypeStruct(out_shape, jnp.bfloat16),
        in_specs=[INSIDE] * count + [ANYWHERE] * len(after),
        out_specs=INSIDE,
        compiler_params=pltpu.CompilerParams(vmem_limit_bytes=VMEM),
        cost_estimate=pl.CostEstimate(
            flops=4 * work * HDIM, bytes_accessed=4_000_000, transcendentals=work
        ),
        name=name,
    )(*operands.arrays, *after)


def home(queries, frame_kv, sink, after):
    frame = queries.shape[0]

    def kernel(query, key, value, sink_key, sink_value, _, out):
        for head in range(PER):
            cols = slice(head * HDIM, (head + 1) * HDIM)
            keys = jnp.concatenate([key[:, cols], sink_key[:, cols]], axis=0)
            values = jnp.concatenate([value[:, cols], sink_value[:, cols]], axis=0)
            top, total, blended = fresh_state(query[:, cols], keys, values)
            out[:frame, cols] = (blended / total).astype(jnp.bfloat16)
            out[frame:, cols] = stat_rows(top + jnp.log2(total))

    def block(array, first):
        return pl.BlockSpec((array.shape[0], CW), lambda at: (0, first + at))

    return pl.pallas_call(
        kernel,
        out_shape=jax.ShapeDtypeStruct((frame + STAT, WIDTH), jnp.bfloat16),
        grid=(CHUNKS,),
        in_specs=[
            block(queries, 0),
            block(frame_kv, 0),
            block(frame_kv, CHUNKS),
            block(sink, 0),
            block(sink, CHUNKS),
            ANYWHERE,
        ],
        out_specs=pl.BlockSpec((frame + STAT, CW), lambda at: (0, at)),
        compiler_params=pltpu.CompilerParams(vmem_limit_bytes=VMEM),
        cost_estimate=pl.CostEstimate(
            flops=4 * WIDTH * frame * (frame + sink.shape[0]),
            bytes_accessed=6_000_000,
            transcendentals=HEADS * frame * (frame + sink.shape[0]),
        ),
        name="home",
    )(queries, frame_kv, frame_kv, sink, sink, after)


def finish(queries, at_home, sinks, came, extra, sink_rows):
    frame = queries.shape[0]
    as_keys = bool(came) and len(came) == CHUNKS and bool(sinks)
    rows = 2 * frame + 2 * sink_rows
    came_rows = rows if as_keys else frame + STAT
    moved = [(each, came_rows) for each in came] + [(each, rows) for each in extra]

    def kernel(*refs):
        query, home_ref = refs[:2]
        sink_refs = refs[2 : 2 + 2 * len(sinks)]
        sources = refs[2 + 2 * len(sinks) : 2 + 2 * len(sinks) + len(moved)]
        out = refs[2 + 2 * len(sinks) + len(moved)]
        held = refs[3 + 2 * len(sinks) + len(moved) : -1]
        sems = refs[-1]
        step = pl.program_id(0)

        def copy(at):
            return pltpu.make_async_copy(
                sources[at].at[pl.ds(0, moved[at][1])],
                held[0].at[at] if at < len(came) else held[-1].at[at - len(came)],
                sems.at[at],
            )

        if moved:

            @pl.when(step == 0)
            def _():
                for at in range(len(moved)):
                    copy(at).start()

        for at in range(len(came)):

            @pl.when(step == at)
            def _():
                copy(at).wait()

        def chunk(key_places, part_place):
            for head in range(PER):
                cols = slice(head * HDIM, (head + 1) * HDIM)
                keys = [ref[:, cols] for ref in sink_refs[::2]]
                values = [ref[:, cols] for ref in sink_refs[1::2]]
                for buffer, which in key_places:
                    keys += [buffer[which, :frame, cols], buffer[which, 2 * frame : 2 * frame + sink_rows, cols]]
                    values += [buffer[which, frame : 2 * frame, cols], buffer[which, 2 * frame + sink_rows :, cols]]
                parts = [home_ref[:, cols]]
                if part_place is not None:
                    parts.append(part_place[0][part_place[1], :, cols])
                states = [fresh_state(query[:, cols], stacked(keys), stacked(values))] if keys else []
                for part in parts:
                    states.append(
                        (
                            stat_column(part[frame:], frame // HDIM),
                            1.0,
                            part[:frame].astype(jnp.float32),
                        )
                    )
                _, total, blended = merge_states(states)
                out[:, cols] = (blended / total).astype(jnp.bfloat16)

        if extra:

            @pl.when(step < len(came))
            def _():
                chunk([], (held[0], step))

            @pl.when(step == len(came))
            def _():
                for at in range(len(came), len(moved)):
                    copy(at).wait()
                chunk([(held[-1], at) for at in range(len(extra))], None)

        elif as_keys:
            chunk([(held[0], step)], None)
        elif came:
            chunk([], (held[0], step))
        else:
            chunk([], None)

    in_specs = [
        pl.BlockSpec((frame, CW), lambda at: (0, at)),
        pl.BlockSpec((frame + STAT, CW), lambda at: (0, at)),
    ]
    for _ in sinks:
        in_specs += [
            pl.BlockSpec((sink_rows, CW), lambda at: (at, 0)),
            pl.BlockSpec((sink_rows, CW), lambda at: (CHUNKS + at, 0)),
        ]
    scratch = []
    if came:
        scratch.append(pltpu.VMEM((len(came), came_rows, CW), jnp.bfloat16))
    if extra:
        scratch.append(pltpu.VMEM((len(extra), rows, CW), jnp.bfloat16))
    return pl.pallas_call(
        kernel,
        out_shape=jax.ShapeDtypeStruct(queries.shape, jnp.bfloat16),
        grid=(CHUNKS,),
        in_specs=in_specs + [ANYWHERE] * len(moved),
        out_specs=pl.BlockSpec((frame, CW), lambda at: (0, at)),
        scratch_shapes=scratch + [pltpu.SemaphoreType.DMA((max(len(moved), 1),))],
        compiler_params=pltpu.CompilerParams(vmem_limit_bytes=VMEM),
        name="finish",
    )(queries, at_home, *[each for sink in sinks for each in (sink, sink)], *[each for each, _ in moved])


def cross(queries, shards, pick, prompt_rows, after):
    frame = queries.shape[0]
    step = 2 * prompt_rows

    def kernel(pick_ref, query, *refs):
        out = refs[-1]
        picked = pick_ref[0] * prompt_rows

        def chunk(at, carry):
            def rows(ref, which):
                start = pl.multiple_of(which * step + picked, 8)
                return ref.at[pl.ds(start, prompt_rows)]

            first = pl.multiple_of(at * CW, HDIM)
            for head in range(PER):
                cols = pl.ds(head * HDIM, HDIM)
                keys = stacked([rows(ref, at)[:, cols] for ref in refs[:-2]])
                values = stacked([rows(ref, CHUNKS + at)[:, cols] for ref in refs[:-2]])
                here = pl.ds(first + head * HDIM, HDIM)
                _, total, blended = fresh_state(query[:, here], keys, values)
                out[:, here] = (blended / total).astype(jnp.bfloat16)
            return carry

        lax.fori_loop(0, CHUNKS, chunk, 0)

    work = HEADS * frame * prompt_rows * len(shards)
    return pl.pallas_call(
        kernel,
        out_shape=jax.ShapeDtypeStruct(queries.shape, jnp.bfloat16),
        in_specs=[SCALAR] + [INSIDE] * (1 + len(shards)) + [ANYWHERE],
        out_specs=INSIDE,
        compiler_params=pltpu.CompilerParams(vmem_limit_bytes=VMEM),
        cost_estimate=pl.CostEstimate(
            flops=4 * work * HDIM, bytes_accessed=12_000_000, transcendentals=work
        ),
        name="cross",
    )(pick, queries, *shards, after)


def pack(place, rows, plans, name="pack", after=()):
    operands = Operands()
    located = {
        at: [(operands.index(block.array), block, first) for block, first in items]
        for at, items in plans.items()
    }
    most = max(len(items) for items in located.values())

    def kernel(place_ref, *refs):
        out, sems = refs[-2:]
        for at, items in located.items():

            @pl.when(place_ref[0] == at)
            def _():
                copies = [
                    pltpu.make_async_copy(
                        refs[which].at[pl.ds(block.row, block.rows), pl.ds(block.col, CW)],
                        out.at[pl.ds(first, block.rows), :],
                        sems.at[n],
                    )
                    for n, (which, block, first) in enumerate(items)
                ]
                for copy in copies:
                    copy.start()
                for copy in copies:
                    copy.wait()

    return pl.pallas_call(
        kernel,
        out_shape=jax.ShapeDtypeStruct((rows, CW), jnp.bfloat16),
        in_specs=[SCALAR] + [ANYWHERE] * (len(operands.arrays) + len(after)),
        out_specs=INSIDE,
        scratch_shapes=[pltpu.SemaphoreType.DMA((most,))],
        cost_estimate=pl.CostEstimate(flops=0, bytes_accessed=2_000_000, transcendentals=0),
        name=name,
    )(place, *operands.arrays, *after)


def unused(rows, after):
    return pl.pallas_call(
        lambda _, out: None,
        out_shape=jax.ShapeDtypeStruct((rows, CW), jnp.bfloat16),
        in_specs=[ANYWHERE],
        out_specs=ANYWHERE,
        name="unused",
    )(after)


def shards(queries, cross_queries, frame_kv, sink_kv, prompt_kv, switch):
    streams = lax.axis_size("span") // WIN
    device = lax.axis_index("span")
    place = device // streams
    stream = device % streams
    frame = queries.shape[0]
    sink = sink_kv.reshape(sink_kv.shape[1], sink_kv.shape[2])
    sink_rows = sink.shape[0]
    prompt_rows = prompt_kv.shape[1]
    prompt_both = prompt_kv.reshape(2 * prompt_rows, prompt_kv.shape[2])
    part_rows = frame + STAT
    place_ref = place.reshape(1).astype(jnp.int32)

    def move(value, *pairs):
        both = [(a * streams + s, b * streams + s) for a, b in pairs for s in range(streams)]
        return lax.ppermute(value, "span", both)

    def across(value, flip):
        pairs = [(at, at - at % streams + ((at % streams) ^ flip)) for at in range(WIN * streams)]
        return lax.ppermute(value, "span", pairs)

    def choose(branches, *operands):
        return lax.switch(place, branches, *operands)

    def columns(array, height):
        count = array.shape[1] // CW
        return [(Block(array, 0, height, at * CW), at * height) for at in range(count)]

    def cut(row, rows, first, array, col=0):
        size = rows // 4 if rows % 64 == 0 else rows
        return [
            (Block(array, row + at, size, col), first + at) for at in range(0, rows, size)
        ]

    def query_chunks(array, *chunks):
        return [
            each
            for at, chunk in enumerate(chunks)
            for each in cut(0, frame, at * frame, array, chunk * CW)
        ]

    def kvs(frame_array, sink_array, chunk):
        low = chunk * CW
        return [
            (Block(frame_array, 0, frame, low), 0),
            (Block(frame_array, 0, frame, WIDTH + low), frame),
            (Block(sink_array, 0, sink_rows, low), 2 * frame),
            (Block(sink_array, 0, sink_rows, WIDTH + low), 2 * frame + sink_rows),
        ]

    def whole(array, rows):
        return cut(0, rows, 0, array)

    def own_pairs(frame_array, sink_array, chunk):
        low = chunk * CW
        return [
            (Block(frame_array, 0, frame, low), Block(frame_array, 0, frame, WIDTH + low)),
            (Block(sink_array, 0, sink_rows, low), Block(sink_array, 0, sink_rows, WIDTH + low)),
        ]

    def kvs_pairs(array):
        return [
            (Block(array, 0, frame), Block(array, frame, frame)),
            (
                Block(array, 2 * frame, sink_rows),
                Block(array, 2 * frame + sink_rows, sink_rows),
            ),
        ]

    def sink_pair(array, chunk):
        return (
            Block(array, chunk * sink_rows, sink_rows),
            Block(array, (CHUNKS + chunk) * sink_rows, sink_rows),
        )

    def part(array, index=0, col=0):
        return Block(array, index * part_rows, part_rows, col)

    def spread(shard):
        held = [shard]
        flip = streams // 2
        while flip > 0:
            held = held + [across(each, flip) for each in held]
            flip //= 2
        return held

    stream_ids = jnp.arange(switch.shape[0], dtype=jnp.int32)
    switch_at = jnp.sum(jnp.where(stream_ids == stream, switch, 0))
    pick = (place >= switch_at).astype(jnp.int32).reshape(1)

    prompt_size = 4 * CHUNKS * prompt_rows
    sink_size = 2 * CHUNKS * sink_rows
    same = max(prompt_size, 2 * frame, sink_size)
    kvs_rows = 2 * frame + 2 * sink_rows
    wide = max(kvs_rows, prompt_size, 2 * part_rows)
    two = 2 * part_rows

    prompt = pack(
        place_ref,
        prompt_size,
        {p: columns(prompt_both, 2 * prompt_rows) for p in range(WIN)},
        name="prompt",
    )
    up_a = move(prompt, (0, 1), (1, 2), (2, 3))
    send_b = pack(
        place_ref,
        same,
        {1: whole(prompt, prompt_size), 2: query_chunks(queries, 0, 1), 3: whole(prompt, prompt_size)},
        name="send_b",
    )
    down_b = move(send_b, (3, 2), (2, 1), (1, 0))
    send_c = pack(
        place_ref,
        kvs_rows,
        {0: kvs(frame_kv, sink, 3), 1: kvs(frame_kv, sink, 3)},
        name="send_c",
        after=(send_b,),
    )
    up_c = move(send_c, (0, 1), (1, 2))
    send_d = pack(
        place_ref,
        same,
        {1: columns(sink, sink_rows), 3: query_chunks(queries, 0, 1)},
        name="send_d",
        after=(send_c,),
    )
    down_d = move(send_d, (3, 1), (1, 0))
    stages = spread(prompt)
    at_home = home(queries, frame_kv, sink, send_d)

    send_e = pack(
        place_ref,
        wide,
        {
            0: kvs(frame_kv, sink, 0),
            1: whole(up_a, prompt_size),
            2: whole(up_a, prompt_size),
        },
        name="send_e",
        after=(at_home,),
    )
    up_e = move(send_e, (0, 1), (1, 2), (2, 3))
    send_f = pack(
        place_ref,
        same,
        {2: whole(prompt, prompt_size), 3: query_chunks(queries, 2, 3)},
        name="send_f",
        after=(send_e,),
    )
    down_f = move(send_f, (3, 2), (2, 1))
    second = pack(
        place_ref,
        prompt_size,
        {p: whole(down_b if p == 0 else up_a, prompt_size) for p in range(WIN)},
        name="second_shard",
        after=(send_f,),
    )
    stages += spread(second)
    send_g = pack(
        place_ref,
        kvs_rows,
        {0: kvs(frame_kv, sink, 1), 1: whole(up_c, kvs_rows)},
        name="send_g",
        after=(second,),
    )
    up_g = move(send_g, (0, 1), (1, 2))
    send_i = pack(
        place_ref,
        same,
        {2: whole(down_b, same), 3: query_chunks(queries, 0, 1)},
        name="send_i",
        after=(send_g,),
    )
    down_i = move(send_i, (3, 2), (2, 1))
    send_k = pack(
        place_ref,
        same,
        {
            1: whole(down_f, prompt_size),
            2: cut(0, frame, 0, queries, 2 * CW) + cut(0, frame, frame, down_f),
            3: columns(sink, sink_rows),
        },
        name="send_k",
        after=(send_i,),
    )
    down_k = move(send_k, (3, 2), (2, 1), (1, 0))

    def visit(q2, q3, came, frame_array, sink_array, chunk, rows):
        return attend(
            [([q2, q3], own_pairs(frame_array, sink_array, chunk) + kvs_pairs(came), [], None)],
            (rows, CW),
            "visit",
        )

    def join(query, came, frame_array, sink_array, chunk, rows):
        return attend(
            [([query], own_pairs(frame_array, sink_array, chunk), [part(came, 1)], None)],
            (rows, CW),
            "join",
        )

    def branch_pack(rows, items):
        return pack(jnp.zeros((1,), jnp.int32), rows, {0: items}, name="branch")

    send_h = choose(
        [
            lambda t, f, s, e, b, d: branch_pack(wide, kvs(f, s, 2)),
            lambda t, f, s, e, b, d: visit(
                Block(b, 0, frame), Block(d, 0, frame), e, f, s, 0, wide
            ),
            lambda t, f, s, e, b, d: branch_pack(wide, whole(e, prompt_size)),
            lambda t, f, s, e, b, d: unused(wide, t),
        ],
        send_k,
        frame_kv,
        sink,
        up_e,
        down_b,
        down_d,
    )
    up_h = move(send_h, (0, 1), (1, 2), (2, 3))
    send_l = pack(
        place_ref,
        same,
        {1: whole(down_i, same), 2: columns(sink, sink_rows)},
        name="send_l",
        after=(send_h,),
    )
    down_l = move(send_l, (2, 1), (1, 0))
    third = pack(
        place_ref,
        prompt_size,
        {
            0: whole(down_k, prompt_size),
            1: whole(down_f, prompt_size),
            2: whole(down_b, prompt_size),
            3: whole(up_e, prompt_size),
        },
        name="third_shard",
        after=(send_l,),
    )
    stages += spread(third)
    send_j = choose(
        [
            lambda t, f, s, c, g, b, d, fd: unused(two, t),
            lambda t, f, s, c, g, b, d, fd: visit(
                Block(b, frame, frame), Block(d, frame, frame), g, f, s, 1, two
            ),
            lambda t, f, s, c, g, b, d, fd: attend(
                [([Block(fd, frame, frame)], own_pairs(f, s, 3) + kvs_pairs(c) + kvs_pairs(g), [], None)],
                (two, CW),
                "all_d",
            ),
            lambda t, f, s, c, g, b, d, fd: unused(two, t),
        ],
        third,
        frame_kv,
        sink,
        up_c,
        up_g,
        down_b,
        down_d,
        down_f,
    )
    up_j = move(send_j, (1, 2), (2, 3))
    down_m = move(down_k, (2, 1))
    last = pack(
        place_ref,
        prompt_size,
        {
            0: whole(down_l, prompt_size),
            1: whole(down_i, prompt_size),
            2: whole(up_e, prompt_size),
            3: whole(up_h, prompt_size),
        },
        name="last_shard",
        after=(send_j,),
    )
    stages += spread(last)
    down_o = move(down_l, (1, 0))
    send_n = choose(
        [
            lambda t, f, s, h, k, i: unused(two, t),
            lambda t, f, s, h, k, i: visit(
                Block(k, 0, frame), Block(k, frame, frame), h, f, s, 2, two
            ),
            lambda t, f, s, h, k, i: join(Block(i, 0, frame), h, f, s, 0, two),
            lambda t, f, s, h, k, i: unused(two, t),
        ],
        last,
        frame_kv,
        sink,
        up_h,
        down_k,
        down_i,
    )
    up_n = move(send_n, (1, 2), (2, 3))
    send_o = choose(
        [
            lambda t, f, s, j, i: unused(part_rows, t),
            lambda t, f, s, j, i: unused(part_rows, t),
            lambda t, f, s, j, i: join(Block(i, frame, frame), j, f, s, 1, part_rows),
            lambda t, f, s, j, i: unused(part_rows, t),
        ],
        send_n,
        frame_kv,
        sink,
        up_j,
        down_i,
    )
    up_o = move(send_o, (2, 3))
    down_r = move(down_m, (1, 0))
    send_q = choose(
        [
            lambda t, f, s, n, d: unused(part_rows, t),
            lambda t, f, s, n, d: unused(part_rows, t),
            lambda t, f, s, n, d: join(Block(d, 0, frame), n, f, s, 2, part_rows),
            lambda t, f, s, n, d: unused(part_rows, t),
        ],
        send_o,
        frame_kv,
        sink,
        up_n,
        down_f,
    )
    up_q = move(send_q, (2, 3))

    cross_out = cross(cross_queries, stages, pick, prompt_rows, send_q)

    def finish0(q, h, x, u, d):
        return finish(q, h, [d["d"], d["o"], d["r"]], [], [], sink_rows)

    def finish1(q, h, x, u, d):
        return finish(q, h, [d["l"], d["m"]], [u["e"], u["g"], u["h"], u["c"]], [], sink_rows)

    def finish2(q, h, x, u, d):
        return finish(q, h, [d["k"]], [u["h"], u["j"], u["n"]], [u["c"], u["g"]], sink_rows)

    def finish3(q, h, x, u, d):
        return finish(q, h, [], [u["n"], u["o"], u["q"], u["j"]], [], sink_rows)

    ups = {"c": up_c, "e": up_e, "g": up_g, "h": up_h, "j": up_j, "n": up_n, "o": up_o, "q": up_q}
    downs = {"d": down_d, "k": down_k, "l": down_l, "m": down_m, "o": down_o, "r": down_r}
    self_out = choose(
        [finish0, finish1, finish2, finish3], queries, at_home, cross_out, ups, downs
    )
    return (self_out, cross_out)


def solution(mesh):
    in_specs = (
        P(("groups", "span"), None),
        P(("groups", "span"), None),
        P(("groups", "span"), None),
        P(("groups", "span"), None, None),
        P("groups", "span", None),
        P("groups"),
    )
    out_specs = (P(("groups", "span"), None), P(("groups", "span"), None))
    return jax.shard_map(shards, mesh=mesh, in_specs=in_specs, out_specs=out_specs, check_vma=False)
```

```python
import math

import jax
import jax.numpy as jnp
from jax import lax
from jax.experimental import pallas as pl
from jax.experimental.pallas import tpu as pltpu
from jax.sharding import PartitionSpec as P

HEADS = 20
HDIM = 128
WIN = 4
CHUNKS = 4
PER = HEADS // CHUNKS
CW = PER * HDIM
WIDTH = HEADS * HDIM
STAT = 16
LOG_SCALE = math.log2(math.e) / math.sqrt(HDIM)
VMEM = 48 * 1024 * 1024
ANYWHERE = pl.BlockSpec(memory_space=pl.ANY)
SCALAR = pl.BlockSpec(memory_space=pltpu.SMEM)
INSIDE = pl.BlockSpec(memory_space=pltpu.VMEM)


def diagonal():
    rows = lax.broadcasted_iota(jnp.int32, (HDIM, HDIM), 0)
    cols = lax.broadcasted_iota(jnp.int32, (HDIM, HDIM), 1)
    return rows == cols


def stat_rows(column):
    eye = diagonal()
    groups = column.shape[0] // HDIM
    tops, mids, lows = [], [], []
    for group in range(groups):
        part = column[group * HDIM : (group + 1) * HDIM]
        row = jnp.sum(jnp.where(eye, part, 0.0), axis=0, keepdims=True)
        top = row.astype(jnp.bfloat16).astype(jnp.float32)
        mid = (row - top).astype(jnp.bfloat16).astype(jnp.float32)
        tops.append(top)
        mids.append(mid)
        lows.append(row - top - mid)
    used = tops + mids + lows
    used.append(jnp.zeros((STAT - len(used), HDIM), jnp.float32))
    return jnp.concatenate(used, axis=0).astype(jnp.bfloat16)


def stat_column(tile, groups):
    eye = diagonal()
    tile = tile.astype(jnp.float32)
    columns = []
    for group in range(groups):
        row = (
            tile[group : group + 1]
            + tile[groups + group : groups + group + 1]
            + tile[2 * groups + group : 2 * groups + group + 1]
        )
        columns.append(jnp.sum(jnp.where(eye, row, 0.0), axis=1, keepdims=True))
    return jnp.concatenate(columns, axis=0)


def fresh_state(query, keys, values):
    scores = lax.dot_general(
        query, keys, (((1,), (1,)), ((), ())), preferred_element_type=jnp.float32
    )
    top = jnp.max(scores, axis=1, keepdims=True)
    weights = jnp.exp2((scores - top) * LOG_SCALE).astype(jnp.bfloat16)
    beside = jnp.concatenate([values, jnp.ones_like(values)], axis=1)
    both = jnp.dot(weights, beside, preferred_element_type=jnp.float32)
    return top * LOG_SCALE, both[:, HDIM:], both[:, :HDIM]


def merge_states(states):
    if len(states) == 1:
        return states[0]
    top = states[0][0]
    for state in states[1:]:
        top = jnp.maximum(top, state[0])
    total, blended = 0.0, 0.0
    for state in states:
        factor = jnp.exp2(state[0] - top)
        total = total + state[1] * factor
        blended = blended + state[2] * factor
    return top, total, blended


def stacked(pieces):
    return pieces[0] if len(pieces) == 1 else jnp.concatenate(pieces, axis=0)


class Block:
    def __init__(self, array, row, rows, col=0):
        self.array, self.row, self.rows, self.col = array, row, rows, col


class Operands:
    def __init__(self):
        self.arrays = []

    def index(self, array):
        for at, each in enumerate(self.arrays):
            if each is array:
                return at
        self.arrays.append(array)
        return len(self.arrays) - 1


def attend(jobs, out_shape, name, after=()):
    operands = Operands()

    def located(block):
        return (operands.index(block.array), block.row, block.rows, block.col)

    plan = [
        (
            [located(q) for q in queries],
            [(located(k), located(v)) for k, v in pairs],
            [located(p) for p in parts],
            out_col,
        )
        for queries, pairs, parts, out_col in jobs
    ]
    count = len(operands.arrays)

    def kernel(*refs):
        out = refs[-1]

        def read(where, head):
            at, row, rows, col = where
            left = pl.multiple_of(col + head * HDIM, HDIM)
            return refs[at][row : row + rows, pl.ds(left, HDIM)]

        def one_job(queries, pairs, parts, out_col):
            def one_head(head, carry):
                if pairs:
                    keys = stacked([read(k, head) for k, _ in pairs])
                    values = stacked([read(v, head) for _, v in pairs])
                cols = pl.ds(pl.multiple_of((out_col or 0) + head * HDIM, HDIM), HDIM)
                for at, query in enumerate(queries):
                    frame = query[2]
                    states = []
                    if pairs:
                        states.append(fresh_state(read(query, head), keys, values))
                    for part in parts:
                        rows = read(part, head)
                        states.append(
                            (
                                stat_column(rows[frame : frame + STAT], frame // HDIM),
                                1.0,
                                rows[:frame].astype(jnp.float32),
                            )
                        )
                    top, total, blended = merge_states(states)
                    done = (blended / total).astype(jnp.bfloat16)
                    if out_col is None:
                        start = at * (frame + STAT)
                        out[start : start + frame, cols] = done
                        out[start + frame : start + frame + STAT, cols] = stat_rows(
                            top + jnp.log2(total)
                        )
                    else:
                        out[:, cols] = done
                return carry

            lax.fori_loop(0, PER, one_head, 0)

        for job in plan:
            one_job(*job)

    work = sum(
        PER * len(queries) * queries[0].rows * sum(k.rows for k, _ in pairs)
        for queries, pairs, _, _ in jobs
    )
    return pl.pallas_call(
        kernel,
        out_shape=jax.ShapeDtypeStruct(out_shape, jnp.bfloat16),
        in_specs=[INSIDE] * count + [ANYWHERE] * len(after),
        out_specs=INSIDE,
        compiler_params=pltpu.CompilerParams(vmem_limit_bytes=VMEM),
        cost_estimate=pl.CostEstimate(
            flops=4 * work * HDIM, bytes_accessed=4_000_000, transcendentals=work
        ),
        name=name,
    )(*operands.arrays, *after)


def home(queries, frame_kv, sink, after):
    frame = queries.shape[0]

    def kernel(query, key, value, sink_key, sink_value, _, out):
        for head in range(PER):
            cols = slice(head * HDIM, (head + 1) * HDIM)
            keys = jnp.concatenate([key[:, cols], sink_key[:, cols]], axis=0)
            values = jnp.concatenate([value[:, cols], sink_value[:, cols]], axis=0)
            top, total, blended = fresh_state(query[:, cols], keys, values)
            out[:frame, cols] = (blended / total).astype(jnp.bfloat16)
            out[frame:, cols] = stat_rows(top + jnp.log2(total))

    def block(array, first):
        return pl.BlockSpec((array.shape[0], CW), lambda at: (0, first + at))

    return pl.pallas_call(
        kernel,
        out_shape=jax.ShapeDtypeStruct((frame + STAT, WIDTH), jnp.bfloat16),
        grid=(CHUNKS,),
        in_specs=[
            block(queries, 0),
            block(frame_kv, 0),
            block(frame_kv, CHUNKS),
            block(sink, 0),
            block(sink, CHUNKS),
            ANYWHERE,
        ],
        out_specs=pl.BlockSpec((frame + STAT, CW), lambda at: (0, at)),
        compiler_params=pltpu.CompilerParams(vmem_limit_bytes=VMEM),
        cost_estimate=pl.CostEstimate(
            flops=4 * WIDTH * frame * (frame + sink.shape[0]),
            bytes_accessed=6_000_000,
            transcendentals=HEADS * frame * (frame + sink.shape[0]),
        ),
        name="home",
    )(queries, frame_kv, frame_kv, sink, sink, after)


def finish(queries, at_home, sinks, came, extra, sink_rows):
    frame = queries.shape[0]
    as_keys = bool(came) and len(came) == CHUNKS and bool(sinks)
    rows = 2 * frame + 2 * sink_rows
    came_rows = rows if as_keys else frame + STAT
    moved = [(each, came_rows) for each in came] + [(each, rows) for each in extra]

    def kernel(*refs):
        query, home_ref = refs[:2]
        sink_refs = refs[2 : 2 + 2 * len(sinks)]
        sources = refs[2 + 2 * len(sinks) : 2 + 2 * len(sinks) + len(moved)]
        out = refs[2 + 2 * len(sinks) + len(moved)]
        held = refs[3 + 2 * len(sinks) + len(moved) : -1]
        sems = refs[-1]
        step = pl.program_id(0)

        def copy(at):
            return pltpu.make_async_copy(
                sources[at].at[pl.ds(0, moved[at][1])],
                held[0].at[at] if at < len(came) else held[-1].at[at - len(came)],
                sems.at[at],
            )

        if moved:

            @pl.when(step == 0)
            def _():
                for at in range(len(moved)):
                    copy(at).start()

        for at in range(len(came)):

            @pl.when(step == at)
            def _():
                copy(at).wait()

        def chunk(key_places, part_place):
            for head in range(PER):
                cols = slice(head * HDIM, (head + 1) * HDIM)
                keys = [ref[:, cols] for ref in sink_refs[::2]]
                values = [ref[:, cols] for ref in sink_refs[1::2]]
                for buffer, which in key_places:
                    keys += [buffer[which, :frame, cols], buffer[which, 2 * frame : 2 * frame + sink_rows, cols]]
                    values += [buffer[which, frame : 2 * frame, cols], buffer[which, 2 * frame + sink_rows :, cols]]
                parts = [home_ref[:, cols]]
                if part_place is not None:
                    parts.append(part_place[0][part_place[1], :, cols])
                states = [fresh_state(query[:, cols], stacked(keys), stacked(values))] if keys else []
                for part in parts:
                    states.append(
                        (
                            stat_column(part[frame:], frame // HDIM),
                            1.0,
                            part[:frame].astype(jnp.float32),
                        )
                    )
                _, total, blended = merge_states(states)
                out[:, cols] = (blended / total).astype(jnp.bfloat16)

        if extra:

            @pl.when(step < len(came))
            def _():
                chunk([], (held[0], step))

            @pl.when(step == len(came))
            def _():
                for at in range(len(came), len(moved)):
                    copy(at).wait()
                chunk([(held[-1], at) for at in range(len(extra))], None)

        elif as_keys:
            chunk([(held[0], step)], None)
        elif came:
            chunk([], (held[0], step))
        else:
            chunk([], None)

    in_specs = [
        pl.BlockSpec((frame, CW), lambda at: (0, at)),
        pl.BlockSpec((frame + STAT, CW), lambda at: (0, at)),
    ]
    for _ in sinks:
        in_specs += [
            pl.BlockSpec((sink_rows, CW), lambda at: (at, 0)),
            pl.BlockSpec((sink_rows, CW), lambda at: (CHUNKS + at, 0)),
        ]
    scratch = []
    if came:
        scratch.append(pltpu.VMEM((len(came), came_rows, CW), jnp.bfloat16))
    if extra:
        scratch.append(pltpu.VMEM((len(extra), rows, CW), jnp.bfloat16))
    return pl.pallas_call(
        kernel,
        out_shape=jax.ShapeDtypeStruct(queries.shape, jnp.bfloat16),
        grid=(CHUNKS,),
        in_specs=in_specs + [ANYWHERE] * len(moved),
        out_specs=pl.BlockSpec((frame, CW), lambda at: (0, at)),
        scratch_shapes=scratch + [pltpu.SemaphoreType.DMA((max(len(moved), 1),))],
        compiler_params=pltpu.CompilerParams(vmem_limit_bytes=VMEM),
        name="finish",
    )(queries, at_home, *[each for sink in sinks for each in (sink, sink)], *[each for each, _ in moved])


def cross(queries, shards, pick, prompt_rows, after):
    frame = queries.shape[0]
    step = 2 * prompt_rows
    size = 2 * CHUNKS * step
    count = sum(each.shape[0] for each in shards) // size

    def kernel(pick_ref, query, *refs):
        out = refs[-1]
        picked = pick_ref[0] * prompt_rows

        def chunk(at, carry):
            def pieces(which, cols):
                return stacked(
                    [
                        ref[pl.ds(pl.multiple_of(first + which * step + picked, 8), prompt_rows), cols]
                        for ref in refs[: len(shards)]
                        for first in range(0, ref.shape[0], size)
                    ]
                )

            left = pl.multiple_of(at * CW, HDIM)
            for head in range(PER):
                cols = pl.ds(head * HDIM, HDIM)
                keys, values = pieces(at, cols), pieces(CHUNKS + at, cols)
                here = pl.ds(left + head * HDIM, HDIM)
                _, total, blended = fresh_state(query[:, here], keys, values)
                out[:, here] = (blended / total).astype(jnp.bfloat16)
            return carry

        lax.fori_loop(0, CHUNKS, chunk, 0)

    work = HEADS * frame * prompt_rows * count
    return pl.pallas_call(
        kernel,
        out_shape=jax.ShapeDtypeStruct(queries.shape, jnp.bfloat16),
        in_specs=[SCALAR] + [INSIDE] * (1 + len(shards)) + [ANYWHERE],
        out_specs=INSIDE,
        compiler_params=pltpu.CompilerParams(vmem_limit_bytes=VMEM),
        cost_estimate=pl.CostEstimate(
            flops=4 * work * HDIM, bytes_accessed=12_000_000, transcendentals=work
        ),
        name="cross",
    )(pick, queries, *shards, after)


def pack(place, rows, plans, name="pack", after=()):
    operands = Operands()
    located = {
        at: [(operands.index(block.array), block, first) for block, first in items]
        for at, items in plans.items()
    }
    most = max(len(items) for items in located.values())

    def kernel(place_ref, *refs):
        out, sems = refs[-2:]
        for at, items in located.items():

            @pl.when(place_ref[0] == at)
            def _():
                copies = [
                    pltpu.make_async_copy(
                        refs[which].at[pl.ds(block.row, block.rows), pl.ds(block.col, CW)],
                        out.at[pl.ds(first, block.rows), :],
                        sems.at[n],
                    )
                    for n, (which, block, first) in enumerate(items)
                ]
                for copy in copies:
                    copy.start()
                for copy in copies:
                    copy.wait()

    return pl.pallas_call(
        kernel,
        out_shape=jax.ShapeDtypeStruct((rows, CW), jnp.bfloat16),
        in_specs=[SCALAR] + [ANYWHERE] * (len(operands.arrays) + len(after)),
        out_specs=INSIDE,
        scratch_shapes=[pltpu.SemaphoreType.DMA((most,))],
        cost_estimate=pl.CostEstimate(flops=0, bytes_accessed=2_000_000, transcendentals=0),
        name=name,
    )(place, *operands.arrays, *after)


def unused(rows, after):
    return pl.pallas_call(
        lambda _, out: None,
        out_shape=jax.ShapeDtypeStruct((rows, CW), jnp.bfloat16),
        in_specs=[ANYWHERE],
        out_specs=ANYWHERE,
        name="unused",
    )(after)


def shards(queries, cross_queries, frame_kv, sink_kv, prompt_kv, switch):
    streams = lax.axis_size("span") // WIN
    device = lax.axis_index("span")
    place = device // streams
    stream = device % streams
    frame = queries.shape[0]
    sink = sink_kv.reshape(sink_kv.shape[1], sink_kv.shape[2])
    sink_rows = sink.shape[0]
    prompt_rows = prompt_kv.shape[1]
    prompt_both = prompt_kv.reshape(2 * prompt_rows, prompt_kv.shape[2])
    part_rows = frame + STAT
    place_ref = place.reshape(1).astype(jnp.int32)

    def move(value, *pairs):
        both = [(a * streams + s, b * streams + s) for a, b in pairs for s in range(streams)]
        return lax.ppermute(value, "span", both)

    def across(value, flip):
        pairs = [(at, at - at % streams + ((at % streams) ^ flip)) for at in range(WIN * streams)]
        return lax.ppermute(value, "span", pairs)

    def choose(branches, *operands):
        return lax.switch(place, branches, *operands)

    def columns(array, height):
        count = array.shape[1] // CW
        return [(Block(array, 0, height, at * CW), at * height) for at in range(count)]

    def cut(row, rows, first, array, col=0):
        size = rows // 4 if rows % 64 == 0 else rows
        return [
            (Block(array, row + at, size, col), first + at) for at in range(0, rows, size)
        ]

    def query_chunks(array, *chunks):
        return [
            each
            for at, chunk in enumerate(chunks)
            for each in cut(0, frame, at * frame, array, chunk * CW)
        ]

    def kvs(frame_array, sink_array, chunk):
        low = chunk * CW
        return [
            (Block(frame_array, 0, frame, low), 0),
            (Block(frame_array, 0, frame, WIDTH + low), frame),
            (Block(sink_array, 0, sink_rows, low), 2 * frame),
            (Block(sink_array, 0, sink_rows, WIDTH + low), 2 * frame + sink_rows),
        ]

    def whole(array, rows):
        return cut(0, rows, 0, array)

    def own_pairs(frame_array, sink_array, chunk):
        low = chunk * CW
        return [
            (Block(frame_array, 0, frame, low), Block(frame_array, 0, frame, WIDTH + low)),
            (Block(sink_array, 0, sink_rows, low), Block(sink_array, 0, sink_rows, WIDTH + low)),
        ]

    def kvs_pairs(array):
        return [
            (Block(array, 0, frame), Block(array, frame, frame)),
            (
                Block(array, 2 * frame, sink_rows),
                Block(array, 2 * frame + sink_rows, sink_rows),
            ),
        ]

    def sink_pair(array, chunk):
        return (
            Block(array, chunk * sink_rows, sink_rows),
            Block(array, (CHUNKS + chunk) * sink_rows, sink_rows),
        )

    def part(array, index=0, col=0):
        return Block(array, index * part_rows, part_rows, col)

    def spread(shard):
        held = [shard]
        flip = streams // 2
        while flip > 0:
            held = held + [across(each, flip) for each in held]
            flip //= 2
        return held

    planes = [[at * streams + s for s in range(streams)] for at in range(WIN)]

    def gathered(shard):
        return [lax.all_gather(shard, "span", axis_index_groups=planes, axis=0, tiled=True)]

    stream_ids = jnp.arange(switch.shape[0], dtype=jnp.int32)
    switch_at = jnp.sum(jnp.where(stream_ids == stream, switch, 0))
    pick = (place >= switch_at).astype(jnp.int32).reshape(1)

    prompt_size = 4 * CHUNKS * prompt_rows
    sink_size = 2 * CHUNKS * sink_rows
    same = max(prompt_size, 2 * frame, sink_size)
    kvs_rows = 2 * frame + 2 * sink_rows
    wide = max(kvs_rows, prompt_size, 2 * part_rows)
    two = 2 * part_rows

    prompt = pack(
        place_ref,
        prompt_size,
        {p: columns(prompt_both, 2 * prompt_rows) for p in range(WIN)},
        name="prompt",
    )
    up_a = move(prompt, (0, 1), (1, 2), (2, 3))
    send_b = pack(
        place_ref,
        same,
        {1: whole(prompt, prompt_size), 2: query_chunks(queries, 0, 1), 3: whole(prompt, prompt_size)},
        name="send_b",
    )
    down_b = move(send_b, (3, 2), (2, 1), (1, 0))
    send_c = pack(
        place_ref,
        kvs_rows,
        {0: kvs(frame_kv, sink, 3), 1: kvs(frame_kv, sink, 3)},
        name="send_c",
        after=(send_b,),
    )
    up_c = move(send_c, (0, 1), (1, 2))
    send_d = pack(
        place_ref,
        same,
        {1: columns(sink, sink_rows), 3: query_chunks(queries, 0, 1)},
        name="send_d",
        after=(send_c,),
    )
    down_d = move(send_d, (3, 1), (1, 0))
    stages = spread(prompt)
    at_home = home(queries, frame_kv, sink, send_d)

    send_e = pack(
        place_ref,
        wide,
        {
            0: kvs(frame_kv, sink, 0),
            1: whole(up_a, prompt_size),
            2: whole(up_a, prompt_size),
        },
        name="send_e",
        after=(at_home,),
    )
    up_e = move(send_e, (0, 1), (1, 2), (2, 3))
    send_f = pack(
        place_ref,
        same,
        {2: whole(prompt, prompt_size), 3: query_chunks(queries, 2, 3)},
        name="send_f",
        after=(send_e,),
    )
    down_f = move(send_f, (3, 2), (2, 1))
    second = pack(
        place_ref,
        prompt_size,
        {p: whole(down_b if p == 0 else up_a, prompt_size) for p in range(WIN)},
        name="second_shard",
        after=(send_f,),
    )
    stages += spread(second)
    send_g = pack(
        place_ref,
        kvs_rows,
        {0: kvs(frame_kv, sink, 1), 1: whole(up_c, kvs_rows)},
        name="send_g",
        after=(second,),
    )
    up_g = move(send_g, (0, 1), (1, 2))
    send_i = pack(
        place_ref,
        same,
        {2: whole(down_b, same), 3: query_chunks(queries, 0, 1)},
        name="send_i",
        after=(send_g,),
    )
    down_i = move(send_i, (3, 2), (2, 1))
    send_k = pack(
        place_ref,
        same,
        {
            1: whole(down_f, prompt_size),
            2: cut(0, frame, 0, queries, 2 * CW) + cut(0, frame, frame, down_f),
            3: columns(sink, sink_rows),
        },
        name="send_k",
        after=(send_i,),
    )
    down_k = move(send_k, (3, 2), (2, 1), (1, 0))

    def visit(q2, q3, came, frame_array, sink_array, chunk, rows):
        return attend(
            [([q2, q3], own_pairs(frame_array, sink_array, chunk) + kvs_pairs(came), [], None)],
            (rows, CW),
            "visit",
        )

    def join(query, came, frame_array, sink_array, chunk, rows):
        return attend(
            [([query], own_pairs(frame_array, sink_array, chunk), [part(came, 1)], None)],
            (rows, CW),
            "join",
        )

    def branch_pack(rows, items):
        return pack(jnp.zeros((1,), jnp.int32), rows, {0: items}, name="branch")

    send_h = choose(
        [
            lambda t, f, s, e, b, d: branch_pack(wide, kvs(f, s, 2)),
            lambda t, f, s, e, b, d: visit(
                Block(b, 0, frame), Block(d, 0, frame), e, f, s, 0, wide
            ),
            lambda t, f, s, e, b, d: branch_pack(wide, whole(e, prompt_size)),
            lambda t, f, s, e, b, d: unused(wide, t),
        ],
        send_k,
        frame_kv,
        sink,
        up_e,
        down_b,
        down_d,
    )
    up_h = move(send_h, (0, 1), (1, 2), (2, 3))
    send_l = pack(
        place_ref,
        same,
        {1: whole(down_i, same), 2: columns(sink, sink_rows)},
        name="send_l",
        after=(send_h,),
    )
    down_l = move(send_l, (2, 1), (1, 0))
    send_j = choose(
        [
            lambda t, f, s, c, g, b, d, fd: unused(two, t),
            lambda t, f, s, c, g, b, d, fd: visit(
                Block(b, frame, frame), Block(d, frame, frame), g, f, s, 1, two
            ),
            lambda t, f, s, c, g, b, d, fd: attend(
                [([Block(fd, frame, frame)], own_pairs(f, s, 3) + kvs_pairs(c) + kvs_pairs(g), [], None)],
                (two, CW),
                "all_d",
            ),
            lambda t, f, s, c, g, b, d, fd: unused(two, t),
        ],
        send_l,
        frame_kv,
        sink,
        up_c,
        up_g,
        down_b,
        down_d,
        down_f,
    )
    up_j = move(send_j, (1, 2), (2, 3))
    third = pack(
        place_ref,
        prompt_size,
        {
            0: whole(down_k, prompt_size),
            1: whole(down_f, prompt_size),
            2: whole(down_b, prompt_size),
            3: whole(up_e, prompt_size),
        },
        name="third_shard",
        after=(send_j,),
    )
    stages += spread(third)
    down_m = move(down_k, (2, 1))
    down_o = move(down_l, (1, 0))
    send_n = choose(
        [
            lambda t, f, s, h, k, i: unused(two, t),
            lambda t, f, s, h, k, i: visit(
                Block(k, 0, frame), Block(k, frame, frame), h, f, s, 2, two
            ),
            lambda t, f, s, h, k, i: join(Block(i, 0, frame), h, f, s, 0, two),
            lambda t, f, s, h, k, i: unused(two, t),
        ],
        third,
        frame_kv,
        sink,
        up_h,
        down_k,
        down_i,
    )
    up_n = move(send_n, (1, 2), (2, 3))
    last = pack(
        place_ref,
        prompt_size,
        {
            0: whole(down_l, prompt_size),
            1: whole(down_i, prompt_size),
            2: whole(up_e, prompt_size),
            3: whole(up_h, prompt_size),
        },
        name="last_shard",
        after=(send_n,),
    )
    stages += spread(last)
    send_o = choose(
        [
            lambda t, f, s, j, i: unused(part_rows, t),
            lambda t, f, s, j, i: unused(part_rows, t),
            lambda t, f, s, j, i: join(Block(i, frame, frame), j, f, s, 1, part_rows),
            lambda t, f, s, j, i: unused(part_rows, t),
        ],
        last,
        frame_kv,
        sink,
        up_j,
        down_i,
    )
    up_o = move(send_o, (2, 3))
    down_r = move(down_m, (1, 0))
    cross_out = cross(cross_queries, stages, pick, prompt_rows, send_o)
    send_q = choose(
        [
            lambda t, f, s, n, d: unused(part_rows, t),
            lambda t, f, s, n, d: unused(part_rows, t),
            lambda t, f, s, n, d: join(Block(d, 0, frame), n, f, s, 2, part_rows),
            lambda t, f, s, n, d: unused(part_rows, t),
        ],
        send_o,
        frame_kv,
        sink,
        up_n,
        down_f,
    )
    up_q = move(send_q, (2, 3))


    def finish0(q, h, x, u, d):
        return finish(q, h, [d["d"], d["o"], d["r"]], [], [], sink_rows)

    def finish1(q, h, x, u, d):
        return finish(q, h, [d["l"], d["m"]], [u["e"], u["g"], u["h"], u["c"]], [], sink_rows)

    def finish2(q, h, x, u, d):
        return finish(q, h, [d["k"]], [u["h"], u["j"], u["n"]], [u["c"], u["g"]], sink_rows)

    def finish3(q, h, x, u, d):
        return finish(q, h, [], [u["n"], u["o"], u["q"], u["j"]], [], sink_rows)

    ups = {"c": up_c, "e": up_e, "g": up_g, "h": up_h, "j": up_j, "n": up_n, "o": up_o, "q": up_q}
    downs = {"d": down_d, "k": down_k, "l": down_l, "m": down_m, "o": down_o, "r": down_r}
    self_out = choose(
        [finish0, finish1, finish2, finish3], queries, at_home, cross_out, ups, downs
    )
    return (self_out, cross_out)


def solution(mesh):
    in_specs = (
        P(("groups", "span"), None),
        P(("groups", "span"), None),
        P(("groups", "span"), None),
        P(("groups", "span"), None, None),
        P("groups", "span", None),
        P("groups"),
    )
    out_specs = (P(("groups", "span"), None), P(("groups", "span"), None))
    return jax.shard_map(shards, mesh=mesh, in_specs=in_specs, out_specs=out_specs, check_vma=False)
```

```python
import math

import jax
import jax.numpy as jnp
from jax import lax
from jax.experimental import pallas as pl
from jax.experimental.pallas import tpu as pltpu
from jax.sharding import PartitionSpec as P

HEADS = 20
HDIM = 128
WIN = 4
CHUNKS = 4
PER = HEADS // CHUNKS
CW = PER * HDIM
WIDTH = HEADS * HDIM
STAT = 16
LOG_SCALE = math.log2(math.e) / math.sqrt(HDIM)
VMEM = 48 * 1024 * 1024
ANYWHERE = pl.BlockSpec(memory_space=pl.ANY)
SCALAR = pl.BlockSpec(memory_space=pltpu.SMEM)
INSIDE = pl.BlockSpec(memory_space=pltpu.VMEM)


def diagonal():
    rows = lax.broadcasted_iota(jnp.int32, (HDIM, HDIM), 0)
    cols = lax.broadcasted_iota(jnp.int32, (HDIM, HDIM), 1)
    return rows == cols


def stat_rows(column):
    eye = diagonal()
    groups = column.shape[0] // HDIM
    tops, mids, lows = [], [], []
    for group in range(groups):
        part = column[group * HDIM : (group + 1) * HDIM]
        row = jnp.sum(jnp.where(eye, part, 0.0), axis=0, keepdims=True)
        top = row.astype(jnp.bfloat16).astype(jnp.float32)
        mid = (row - top).astype(jnp.bfloat16).astype(jnp.float32)
        tops.append(top)
        mids.append(mid)
        lows.append(row - top - mid)
    used = tops + mids + lows
    used.append(jnp.zeros((STAT - len(used), HDIM), jnp.float32))
    return jnp.concatenate(used, axis=0).astype(jnp.bfloat16)


def stat_column(tile, groups):
    eye = diagonal()
    tile = tile.astype(jnp.float32)
    columns = []
    for group in range(groups):
        row = (
            tile[group : group + 1]
            + tile[groups + group : groups + group + 1]
            + tile[2 * groups + group : 2 * groups + group + 1]
        )
        columns.append(jnp.sum(jnp.where(eye, row, 0.0), axis=1, keepdims=True))
    return jnp.concatenate(columns, axis=0)


def fresh_state(query, keys, values):
    scores = lax.dot_general(
        query, keys, (((1,), (1,)), ((), ())), preferred_element_type=jnp.float32
    )
    top = jnp.max(scores, axis=1, keepdims=True)
    weights = jnp.exp2((scores - top) * LOG_SCALE).astype(jnp.bfloat16)
    beside = jnp.concatenate([values, jnp.ones_like(values)], axis=1)
    both = jnp.dot(weights, beside, preferred_element_type=jnp.float32)
    return top * LOG_SCALE, both[:, HDIM:], both[:, :HDIM]


def merge_rows(parts, frame):
    eye = diagonal()
    groups = frame // HDIM
    logs = []
    for part in parts:
        tile = part[frame : frame + 3 * groups].astype(jnp.float32)
        logs.append(
            tile[:groups] + tile[groups : 2 * groups] + tile[2 * groups : 3 * groups]
        )
    top = logs[0]
    for each in logs[1:]:
        top = jnp.maximum(top, each)
    shares = [jnp.exp2(each - top) for each in logs]
    total = shares[0]
    for each in shares[1:]:
        total = total + each
    merged = []
    for group in range(groups):
        rows = 0.0
        for part, share in zip(parts, shares):
            row = (share / total)[group : group + 1]
            column = jnp.sum(jnp.where(eye, row, 0.0), axis=1, keepdims=True)
            rows = rows + column * part[group * HDIM : (group + 1) * HDIM].astype(jnp.float32)
        merged.append(rows)
    return jnp.concatenate(merged, axis=0)


def merge_states(states):
    if len(states) == 1:
        return states[0]
    top = states[0][0]
    for state in states[1:]:
        top = jnp.maximum(top, state[0])
    total, blended = 0.0, 0.0
    for state in states:
        factor = jnp.exp2(state[0] - top)
        total = total + state[1] * factor
        blended = blended + state[2] * factor
    return top, total, blended


def stacked(pieces):
    return pieces[0] if len(pieces) == 1 else jnp.concatenate(pieces, axis=0)


class Block:
    def __init__(self, array, row, rows, col=0):
        self.array, self.row, self.rows, self.col = array, row, rows, col


class Operands:
    def __init__(self):
        self.arrays = []

    def index(self, array):
        for at, each in enumerate(self.arrays):
            if each is array:
                return at
        self.arrays.append(array)
        return len(self.arrays) - 1


def attend(jobs, out_shape, name, after=()):
    operands = Operands()

    def located(block):
        return (operands.index(block.array), block.row, block.rows, block.col)

    plan = [
        (
            [located(q) for q in queries],
            [(located(k), located(v)) for k, v in pairs],
            [located(p) for p in parts],
            out_col,
        )
        for queries, pairs, parts, out_col in jobs
    ]
    count = len(operands.arrays)

    def kernel(*refs):
        out = refs[-1]

        def read(where, head):
            at, row, rows, col = where
            left = pl.multiple_of(col + head * HDIM, HDIM)
            return refs[at][row : row + rows, pl.ds(left, HDIM)]

        def one_job(queries, pairs, parts, out_col):
            def one_head(head, carry):
                if pairs:
                    keys = stacked([read(k, head) for k, _ in pairs])
                    values = stacked([read(v, head) for _, v in pairs])
                cols = pl.ds(pl.multiple_of((out_col or 0) + head * HDIM, HDIM), HDIM)
                for at, query in enumerate(queries):
                    frame = query[2]
                    states = []
                    if pairs:
                        states.append(fresh_state(read(query, head), keys, values))
                    for part in parts:
                        rows = read(part, head)
                        states.append(
                            (
                                stat_column(rows[frame : frame + STAT], frame // HDIM),
                                1.0,
                                rows[:frame].astype(jnp.float32),
                            )
                        )
                    top, total, blended = merge_states(states)
                    done = (blended / total).astype(jnp.bfloat16)
                    if out_col is None:
                        start = at * (frame + STAT)
                        out[start : start + frame, cols] = done
                        out[start + frame : start + frame + STAT, cols] = stat_rows(
                            top + jnp.log2(total)
                        )
                    else:
                        out[:, cols] = done
                return carry

            lax.fori_loop(0, PER, one_head, 0)

        for job in plan:
            one_job(*job)

    work = sum(
        PER * len(queries) * queries[0].rows * sum(k.rows for k, _ in pairs)
        for queries, pairs, _, _ in jobs
    )
    return pl.pallas_call(
        kernel,
        out_shape=jax.ShapeDtypeStruct(out_shape, jnp.bfloat16),
        in_specs=[INSIDE] * count + [ANYWHERE] * len(after),
        out_specs=INSIDE,
        compiler_params=pltpu.CompilerParams(vmem_limit_bytes=VMEM),
        cost_estimate=pl.CostEstimate(
            flops=4 * work * HDIM, bytes_accessed=4_000_000, transcendentals=work
        ),
        name=name,
    )(*operands.arrays, *after)


def home(queries, frame_kv, sink, after):
    frame = queries.shape[0]

    def kernel(query, key, value, sink_key, sink_value, _, out):
        for head in range(PER):
            cols = slice(head * HDIM, (head + 1) * HDIM)
            keys = jnp.concatenate([key[:, cols], sink_key[:, cols]], axis=0)
            values = jnp.concatenate([value[:, cols], sink_value[:, cols]], axis=0)
            top, total, blended = fresh_state(query[:, cols], keys, values)
            out[:frame, cols] = (blended / total).astype(jnp.bfloat16)
            out[frame:, cols] = stat_rows(top + jnp.log2(total))

    def block(array, first):
        return pl.BlockSpec((array.shape[0], CW), lambda at: (0, first + at))

    return pl.pallas_call(
        kernel,
        out_shape=jax.ShapeDtypeStruct((frame + STAT, WIDTH), jnp.bfloat16),
        grid=(CHUNKS,),
        in_specs=[
            block(queries, 0),
            block(frame_kv, 0),
            block(frame_kv, CHUNKS),
            block(sink, 0),
            block(sink, CHUNKS),
            ANYWHERE,
        ],
        out_specs=pl.BlockSpec((frame + STAT, CW), lambda at: (0, at)),
        compiler_params=pltpu.CompilerParams(vmem_limit_bytes=VMEM),
        cost_estimate=pl.CostEstimate(
            flops=4 * WIDTH * frame * (frame + sink.shape[0]),
            bytes_accessed=6_000_000,
            transcendentals=HEADS * frame * (frame + sink.shape[0]),
        ),
        name="home",
    )(queries, frame_kv, frame_kv, sink, sink, after)


def finish(queries, at_home, sinks, came, extra, sink_rows, own=None):
    frame = queries.shape[0]
    as_keys = bool(came) and len(came) == CHUNKS and bool(sinks)
    rows = 2 * frame + 2 * sink_rows
    came_rows = rows if as_keys else frame + STAT
    moved = [(each, came_rows) for each in came] + [(each, rows) for each in extra]
    pairs = 2 * len(sinks) + (4 if own else 0)

    def kernel(*refs):
        query, home_ref = refs[:2]
        sink_refs = refs[2 : 2 + pairs]
        sources = refs[2 + pairs : 2 + pairs + len(moved)]
        out = refs[2 + pairs + len(moved)]
        held = refs[3 + pairs + len(moved) : -1]
        sems = refs[-1]
        step = pl.program_id(0)

        def copy(at):
            return pltpu.make_async_copy(
                sources[at].at[pl.ds(0, moved[at][1])],
                held[0].at[at] if at < len(came) else held[-1].at[at - len(came)],
                sems.at[at],
            )

        if moved:

            @pl.when(step == 0)
            def _():
                for at in range(len(moved)):
                    copy(at).start()

        for at in range(len(came)):

            @pl.when(step == at)
            def _():
                copy(at).wait()

        def chunk(key_places, part_place):
            for head in range(PER):
                cols = slice(head * HDIM, (head + 1) * HDIM)
                keys = [ref[:, cols] for ref in sink_refs[::2]]
                values = [ref[:, cols] for ref in sink_refs[1::2]]
                for buffer, which in key_places:
                    keys += [buffer[which, :frame, cols], buffer[which, 2 * frame : 2 * frame + sink_rows, cols]]
                    values += [buffer[which, frame : 2 * frame, cols], buffer[which, 2 * frame + sink_rows :, cols]]
                parts = [] if own else [home_ref[:, cols]]
                if part_place is not None:
                    parts.append(part_place[0][part_place[1], :, cols])
                if not keys:
                    out[:, cols] = merge_rows(parts, frame).astype(jnp.bfloat16)
                    continue
                states = [fresh_state(query[:, cols], stacked(keys), stacked(values))]
                for part in parts:
                    states.append(
                        (
                            stat_column(part[frame:], frame // HDIM),
                            1.0,
                            part[:frame].astype(jnp.float32),
                        )
                    )
                _, total, blended = merge_states(states)
                out[:, cols] = (blended / total).astype(jnp.bfloat16)

        if extra:

            @pl.when(step < len(came))
            def _():
                chunk([], (held[0], step))

            @pl.when(step == len(came))
            def _():
                for at in range(len(came), len(moved)):
                    copy(at).wait()
                chunk([(held[-1], at) for at in range(len(extra))], None)

        elif as_keys:
            chunk([(held[0], step)], None)
        elif came:
            chunk([], (held[0], step))
        else:
            chunk([], None)

    in_specs = [
        pl.BlockSpec((frame, CW), lambda at: (0, at)),
        pl.BlockSpec((frame + STAT, CW), lambda at: (0, at)),
    ]
    for _ in sinks:
        in_specs += [
            pl.BlockSpec((sink_rows, CW), lambda at: (at, 0)),
            pl.BlockSpec((sink_rows, CW), lambda at: (CHUNKS + at, 0)),
        ]
    own_arrays = []
    if own:
        for array in own:
            for first in (0, CHUNKS):
                own_arrays.append(array)
                in_specs.append(
                    pl.BlockSpec((array.shape[0], CW), lambda at, first=first: (0, first + at))
                )
    scratch = []
    if came:
        scratch.append(pltpu.VMEM((len(came), came_rows, CW), jnp.bfloat16))
    if extra:
        scratch.append(pltpu.VMEM((len(extra), rows, CW), jnp.bfloat16))
    return pl.pallas_call(
        kernel,
        out_shape=jax.ShapeDtypeStruct(queries.shape, jnp.bfloat16),
        grid=(CHUNKS,),
        in_specs=in_specs + [ANYWHERE] * len(moved),
        out_specs=pl.BlockSpec((frame, CW), lambda at: (0, at)),
        scratch_shapes=scratch + [pltpu.SemaphoreType.DMA((max(len(moved), 1),))],
        compiler_params=pltpu.CompilerParams(vmem_limit_bytes=VMEM),
        name="finish",
    )(
        queries,
        at_home,
        *[each for sink in sinks for each in (sink, sink)],
        *own_arrays,
        *[each for each, _ in moved],
    )


def cross(queries, shards, pick, prompt_rows, after):
    frame = queries.shape[0]
    blocks = 2 * CHUNKS
    parts = [each.reshape(blocks, 2, prompt_rows, CW) for each in shards]
    while parts[0].shape[2] % 16:
        half = len(parts) // 2
        parts = [
            jnp.concatenate([one, other], axis=2) for one, other in zip(parts[:half], parts[half:])
        ]
    rows = parts[0].shape[2]
    tokens = rows * len(parts)

    def kernel(pick_ref, query, *refs):
        out, held, sems = refs[-3:]
        copies = [
            pltpu.make_async_copy(
                refs[n].at[:, pick_ref[0]], held.at[:, pl.ds(n * rows, rows)], sems.at[n]
            )
            for n in range(len(parts))
        ]
        for copy in copies:
            copy.start()
        for copy in copies:
            copy.wait()

        def chunk(at, carry):
            left = pl.multiple_of(at * CW, HDIM)
            for head in range(PER):
                cols = pl.ds(head * HDIM, HDIM)
                here = pl.ds(left + head * HDIM, HDIM)
                _, total, blended = fresh_state(
                    query[:, here], held[at, :, cols], held[CHUNKS + at, :, cols]
                )
                out[:, here] = (blended / total).astype(jnp.bfloat16)
            return carry

        lax.fori_loop(0, CHUNKS, chunk, 0)

    work = HEADS * frame * tokens
    return pl.pallas_call(
        kernel,
        out_shape=jax.ShapeDtypeStruct(queries.shape, jnp.bfloat16),
        in_specs=[SCALAR, INSIDE] + [ANYWHERE] * (len(parts) + 1),
        out_specs=INSIDE,
        scratch_shapes=[
            pltpu.VMEM((blocks, tokens, CW), jnp.bfloat16),
            pltpu.SemaphoreType.DMA((len(parts),)),
        ],
        compiler_params=pltpu.CompilerParams(vmem_limit_bytes=VMEM),
        cost_estimate=pl.CostEstimate(
            flops=4 * work * HDIM, bytes_accessed=12_000_000, transcendentals=work
        ),
        name="cross",
    )(pick, queries, *parts, after)


def pack(place, rows, plans, name="pack", after=()):
    operands = Operands()
    located = {
        at: [(operands.index(block.array), block, first) for block, first in items]
        for at, items in plans.items()
    }
    most = max(len(items) for items in located.values())

    def kernel(place_ref, *refs):
        out, sems = refs[-2:]
        for at, items in located.items():

            @pl.when(place_ref[0] == at)
            def _():
                copies = [
                    pltpu.make_async_copy(
                        refs[which].at[pl.ds(block.row, block.rows), pl.ds(block.col, CW)],
                        out.at[pl.ds(first, block.rows), :],
                        sems.at[n],
                    )
                    for n, (which, block, first) in enumerate(items)
                ]
                for copy in copies:
                    copy.start()
                for copy in copies:
                    copy.wait()

    return pl.pallas_call(
        kernel,
        out_shape=jax.ShapeDtypeStruct((rows, CW), jnp.bfloat16),
        in_specs=[SCALAR] + [ANYWHERE] * (len(operands.arrays) + len(after)),
        out_specs=INSIDE,
        scratch_shapes=[pltpu.SemaphoreType.DMA((most,))],
        cost_estimate=pl.CostEstimate(flops=0, bytes_accessed=2_000_000, transcendentals=0),
        name=name,
    )(place, *operands.arrays, *after)


def unused(rows, after):
    return pl.pallas_call(
        lambda _, out: None,
        out_shape=jax.ShapeDtypeStruct((rows, CW), jnp.bfloat16),
        in_specs=[ANYWHERE],
        out_specs=ANYWHERE,
        name="unused",
    )(after)


def shards(queries, cross_queries, frame_kv, sink_kv, prompt_kv, switch):
    streams = lax.axis_size("span") // WIN
    device = lax.axis_index("span")
    place = device // streams
    stream = device % streams
    frame = queries.shape[0]
    sink = sink_kv.reshape(sink_kv.shape[1], sink_kv.shape[2])
    sink_rows = sink.shape[0]
    prompt_rows = prompt_kv.shape[1]
    prompt_both = prompt_kv.reshape(2 * prompt_rows, prompt_kv.shape[2])
    part_rows = frame + STAT
    place_ref = place.reshape(1).astype(jnp.int32)

    def move(value, *pairs):
        both = [(a * streams + s, b * streams + s) for a, b in pairs for s in range(streams)]
        return lax.ppermute(value, "span", both)

    def across(value, flip):
        pairs = [(at, at - at % streams + ((at % streams) ^ flip)) for at in range(WIN * streams)]
        return lax.ppermute(value, "span", pairs)

    def choose(branches, *operands):
        return lax.switch(place, branches, *operands)

    def columns(array, height):
        count = array.shape[1] // CW
        return [(Block(array, 0, height, at * CW), at * height) for at in range(count)]

    def cut(row, rows, first, array, col=0):
        size = rows // 4 if rows % 64 == 0 else rows
        return [
            (Block(array, row + at, size, col), first + at) for at in range(0, rows, size)
        ]

    def query_chunks(array, *chunks):
        return [
            each
            for at, chunk in enumerate(chunks)
            for each in cut(0, frame, at * frame, array, chunk * CW)
        ]

    def kvs(frame_array, sink_array, chunk):
        low = chunk * CW
        return [
            (Block(frame_array, 0, frame, low), 0),
            (Block(frame_array, 0, frame, WIDTH + low), frame),
            (Block(sink_array, 0, sink_rows, low), 2 * frame),
            (Block(sink_array, 0, sink_rows, WIDTH + low), 2 * frame + sink_rows),
        ]

    def whole(array, rows):
        return cut(0, rows, 0, array)

    def own_pairs(frame_array, sink_array, chunk):
        low = chunk * CW
        return [
            (Block(frame_array, 0, frame, low), Block(frame_array, 0, frame, WIDTH + low)),
            (Block(sink_array, 0, sink_rows, low), Block(sink_array, 0, sink_rows, WIDTH + low)),
        ]

    def kvs_pairs(array):
        return [
            (Block(array, 0, frame), Block(array, frame, frame)),
            (
                Block(array, 2 * frame, sink_rows),
                Block(array, 2 * frame + sink_rows, sink_rows),
            ),
        ]

    def sink_pair(array, chunk):
        return (
            Block(array, chunk * sink_rows, sink_rows),
            Block(array, (CHUNKS + chunk) * sink_rows, sink_rows),
        )

    def part(array, index=0, col=0):
        return Block(array, index * part_rows, part_rows, col)

    def spread(shard):
        held = [shard]
        flip = streams // 2
        while flip > 0:
            held = held + [across(each, flip) for each in held]
            flip //= 2
        return held

    stream_ids = jnp.arange(switch.shape[0], dtype=jnp.int32)
    switch_at = jnp.sum(jnp.where(stream_ids == stream, switch, 0))
    pick = (place >= switch_at).astype(jnp.int32).reshape(1)

    prompt_size = 4 * CHUNKS * prompt_rows
    sink_size = 2 * CHUNKS * sink_rows
    same = max(prompt_size, 2 * frame, sink_size)
    kvs_rows = 2 * frame + 2 * sink_rows
    wide = max(kvs_rows, prompt_size, 2 * part_rows)
    two = 2 * part_rows

    prompt = pack(
        place_ref,
        prompt_size,
        {p: columns(prompt_both, 2 * prompt_rows) for p in range(WIN)},
        name="prompt",
    )
    up_a = move(prompt, (0, 1), (1, 2), (2, 3))
    send_b = pack(
        place_ref,
        same,
        {1: whole(prompt, prompt_size), 2: query_chunks(queries, 0, 1), 3: whole(prompt, prompt_size)},
        name="send_b",
    )
    down_b = move(send_b, (3, 2), (2, 1), (1, 0))
    send_c = pack(
        place_ref,
        kvs_rows,
        {0: kvs(frame_kv, sink, 3), 1: kvs(frame_kv, sink, 3)},
        name="send_c",
        after=(send_b,),
    )
    up_c = move(send_c, (0, 1), (1, 2))
    send_d = pack(
        place_ref,
        same,
        {1: columns(sink, sink_rows), 3: query_chunks(queries, 0, 1)},
        name="send_d",
        after=(send_c,),
    )
    down_d = move(send_d, (3, 1), (1, 0))
    stages = spread(prompt)
    at_home = home(queries, frame_kv, sink, send_d)

    send_e = pack(
        place_ref,
        wide,
        {
            0: kvs(frame_kv, sink, 0),
            1: whole(up_a, prompt_size),
            2: whole(up_a, prompt_size),
        },
        name="send_e",
        after=(at_home,),
    )
    up_e = move(send_e, (0, 1), (1, 2), (2, 3))
    send_f = pack(
        place_ref,
        same,
        {2: whole(prompt, prompt_size), 3: query_chunks(queries, 2, 3)},
        name="send_f",
        after=(send_e,),
    )
    down_f = move(send_f, (3, 2), (2, 1))
    second = pack(
        place_ref,
        prompt_size,
        {p: whole(down_b if p == 0 else up_a, prompt_size) for p in range(WIN)},
        name="second_shard",
        after=(send_f,),
    )
    stages += spread(second)
    send_g = pack(
        place_ref,
        kvs_rows,
        {0: kvs(frame_kv, sink, 1), 1: whole(up_c, kvs_rows)},
        name="send_g",
        after=(second,),
    )
    up_g = move(send_g, (0, 1), (1, 2))
    send_i = pack(
        place_ref,
        same,
        {2: whole(down_b, same), 3: query_chunks(queries, 0, 1)},
        name="send_i",
        after=(send_g,),
    )
    down_i = move(send_i, (3, 2), (2, 1))
    send_k = pack(
        place_ref,
        same,
        {
            1: whole(down_f, prompt_size),
            2: cut(0, frame, 0, queries, 2 * CW) + cut(0, frame, frame, down_f),
            3: columns(sink, sink_rows),
        },
        name="send_k",
        after=(send_i,),
    )
    down_k = move(send_k, (3, 2), (2, 1), (1, 0))

    def visit(q2, q3, came, frame_array, sink_array, chunk, rows):
        return attend(
            [([q2, q3], own_pairs(frame_array, sink_array, chunk) + kvs_pairs(came), [], None)],
            (rows, CW),
            "visit",
        )

    def join(query, came, frame_array, sink_array, chunk, rows):
        return attend(
            [([query], own_pairs(frame_array, sink_array, chunk), [part(came, 1)], None)],
            (rows, CW),
            "join",
        )

    def branch_pack(rows, items):
        return pack(jnp.zeros((1,), jnp.int32), rows, {0: items}, name="branch")

    send_h = choose(
        [
            lambda t, f, s, e, b, d: branch_pack(wide, kvs(f, s, 2)),
            lambda t, f, s, e, b, d: visit(
                Block(b, 0, frame), Block(d, 0, frame), e, f, s, 0, wide
            ),
            lambda t, f, s, e, b, d: branch_pack(wide, whole(e, prompt_size)),
            lambda t, f, s, e, b, d: unused(wide, t),
        ],
        send_k,
        frame_kv,
        sink,
        up_e,
        down_b,
        down_d,
    )
    up_h = move(send_h, (0, 1), (1, 2), (2, 3))
    send_l = pack(
        place_ref,
        same,
        {1: whole(down_i, same), 2: columns(sink, sink_rows)},
        name="send_l",
        after=(send_h,),
    )
    down_l = move(send_l, (2, 1), (1, 0))
    send_j = choose(
        [
            lambda t, f, s, c, g, b, d, fd: unused(two, t),
            lambda t, f, s, c, g, b, d, fd: visit(
                Block(b, frame, frame), Block(d, frame, frame), g, f, s, 1, two
            ),
            lambda t, f, s, c, g, b, d, fd: attend(
                [([Block(fd, frame, frame)], own_pairs(f, s, 3) + kvs_pairs(c) + kvs_pairs(g), [], None)],
                (two, CW),
                "all_d",
            ),
            lambda t, f, s, c, g, b, d, fd: unused(two, t),
        ],
        send_l,
        frame_kv,
        sink,
        up_c,
        up_g,
        down_b,
        down_d,
        down_f,
    )
    up_j = move(send_j, (1, 2), (2, 3))
    third = pack(
        place_ref,
        prompt_size,
        {
            0: whole(down_k, prompt_size),
            1: whole(down_f, prompt_size),
            2: whole(down_b, prompt_size),
            3: whole(up_e, prompt_size),
        },
        name="third_shard",
        after=(send_j,),
    )
    stages += spread(third)
    down_m = move(down_k, (2, 1))
    down_o = move(down_l, (1, 0))
    send_n = choose(
        [
            lambda t, f, s, h, k, i: unused(two, t),
            lambda t, f, s, h, k, i: visit(
                Block(k, 0, frame), Block(k, frame, frame), h, f, s, 2, two
            ),
            lambda t, f, s, h, k, i: join(Block(i, 0, frame), h, f, s, 0, two),
            lambda t, f, s, h, k, i: unused(two, t),
        ],
        third,
        frame_kv,
        sink,
        up_h,
        down_k,
        down_i,
    )
    up_n = move(send_n, (1, 2), (2, 3))
    last = pack(
        place_ref,
        prompt_size,
        {
            0: whole(down_l, prompt_size),
            1: whole(down_i, prompt_size),
            2: whole(up_e, prompt_size),
            3: whole(up_h, prompt_size),
        },
        name="last_shard",
        after=(stages[6], send_n,),
    )
    stages += spread(last)
    send_o = choose(
        [
            lambda t, f, s, j, i: unused(part_rows, t),
            lambda t, f, s, j, i: unused(part_rows, t),
            lambda t, f, s, j, i: join(Block(i, frame, frame), j, f, s, 1, part_rows),
            lambda t, f, s, j, i: unused(part_rows, t),
        ],
        last,
        frame_kv,
        sink,
        up_j,
        down_i,
    )
    up_o = move(send_o, (2, 3))
    down_r = move(down_m, (1, 0))
    cross_out = cross(cross_queries, stages, pick, prompt_rows, send_o)
    send_q = choose(
        [
            lambda t, f, s, n, d: unused(part_rows, t),
            lambda t, f, s, n, d: unused(part_rows, t),
            lambda t, f, s, n, d: join(Block(d, 0, frame), n, f, s, 2, part_rows),
            lambda t, f, s, n, d: unused(part_rows, t),
        ],
        send_o,
        frame_kv,
        sink,
        up_n,
        down_f,
    )
    up_q = move(send_q, (2, 3))


    def finish0(q, h, f, s, x, u, d):
        return finish(q, h, [d["d"], d["o"], d["r"]], [], [], sink_rows, (f, s))

    def finish1(q, h, f, s, x, u, d):
        return finish(q, h, [d["l"], d["m"]], [u["e"], u["g"], u["h"], u["c"]], [], sink_rows)

    def finish2(q, h, f, s, x, u, d):
        return finish(q, h, [d["k"]], [u["h"], u["j"], u["n"]], [u["c"], u["g"]], sink_rows)

    def finish3(q, h, f, s, x, u, d):
        return finish(q, h, [], [u["n"], u["o"], u["q"], u["j"]], [], sink_rows)

    ups = {"c": up_c, "e": up_e, "g": up_g, "h": up_h, "j": up_j, "n": up_n, "o": up_o, "q": up_q}
    downs = {"d": down_d, "k": down_k, "l": down_l, "m": down_m, "o": down_o, "r": down_r}
    self_out = choose(
        [finish0, finish1, finish2, finish3], queries, at_home, frame_kv, sink, cross_out, ups, downs
    )
    return (self_out, cross_out)


def solution(mesh):
    in_specs = (
        P(("groups", "span"), None),
        P(("groups", "span"), None),
        P(("groups", "span"), None),
        P(("groups", "span"), None, None),
        P("groups", "span", None),
        P("groups"),
    )
    out_specs = (P(("groups", "span"), None), P(("groups", "span"), None))
    return jax.shard_map(shards, mesh=mesh, in_specs=in_specs, out_specs=out_specs, check_vma=False)
```

```python
import math

import jax
import jax.numpy as jnp
from jax import lax
from jax.experimental import pallas as pl
from jax.experimental.pallas import tpu as pltpu
from jax.sharding import PartitionSpec as P

HEADS = 20
HDIM = 128
WIN = 4
CHUNKS = 4
PER = HEADS // CHUNKS
CW = PER * HDIM
WIDTH = HEADS * HDIM
STAT = 16
LOG_SCALE = math.log2(math.e) / math.sqrt(HDIM)
VMEM = 48 * 1024 * 1024
ANYWHERE = pl.BlockSpec(memory_space=pl.ANY)
SCALAR = pl.BlockSpec(memory_space=pltpu.SMEM)
INSIDE = pl.BlockSpec(memory_space=pltpu.VMEM)


def diagonal():
    rows = lax.broadcasted_iota(jnp.int32, (HDIM, HDIM), 0)
    cols = lax.broadcasted_iota(jnp.int32, (HDIM, HDIM), 1)
    return rows == cols


def stat_rows(column):
    eye = diagonal()
    groups = column.shape[0] // HDIM
    tops, mids, lows = [], [], []
    for group in range(groups):
        part = column[group * HDIM : (group + 1) * HDIM]
        row = jnp.sum(jnp.where(eye, part, 0.0), axis=0, keepdims=True)
        top = row.astype(jnp.bfloat16).astype(jnp.float32)
        mid = (row - top).astype(jnp.bfloat16).astype(jnp.float32)
        tops.append(top)
        mids.append(mid)
        lows.append(row - top - mid)
    used = tops + mids + lows
    used.append(jnp.zeros((STAT - len(used), HDIM), jnp.float32))
    return jnp.concatenate(used, axis=0).astype(jnp.bfloat16)


def stat_column(tile, groups):
    eye = diagonal()
    tile = tile.astype(jnp.float32)
    columns = []
    for group in range(groups):
        row = (
            tile[group : group + 1]
            + tile[groups + group : groups + group + 1]
            + tile[2 * groups + group : 2 * groups + group + 1]
        )
        columns.append(jnp.sum(jnp.where(eye, row, 0.0), axis=1, keepdims=True))
    return jnp.concatenate(columns, axis=0)


def fresh_state(query, keys, values):
    scores = lax.dot_general(
        query, keys, (((1,), (1,)), ((), ())), preferred_element_type=jnp.float32
    )
    top = jnp.max(scores, axis=1, keepdims=True)
    weights = jnp.exp2((scores - top) * LOG_SCALE).astype(jnp.bfloat16)
    beside = jnp.concatenate([values, jnp.ones_like(values)], axis=1)
    both = jnp.dot(weights, beside, preferred_element_type=jnp.float32)
    return top * LOG_SCALE, both[:, HDIM:], both[:, :HDIM]


def merge_rows(parts, frame):
    eye = diagonal()
    groups = frame // HDIM
    logs = []
    for part in parts:
        tile = part[frame : frame + 3 * groups].astype(jnp.float32)
        logs.append(
            tile[:groups] + tile[groups : 2 * groups] + tile[2 * groups : 3 * groups]
        )
    top = logs[0]
    for each in logs[1:]:
        top = jnp.maximum(top, each)
    shares = [jnp.exp2(each - top) for each in logs]
    total = shares[0]
    for each in shares[1:]:
        total = total + each
    merged = []
    for group in range(groups):
        rows = 0.0
        for part, share in zip(parts, shares):
            row = (share / total)[group : group + 1]
            column = jnp.sum(jnp.where(eye, row, 0.0), axis=1, keepdims=True)
            rows = rows + column * part[group * HDIM : (group + 1) * HDIM].astype(jnp.float32)
        merged.append(rows)
    return jnp.concatenate(merged, axis=0)


def merge_states(states):
    if len(states) == 1:
        return states[0]
    top = states[0][0]
    for state in states[1:]:
        top = jnp.maximum(top, state[0])
    total, blended = 0.0, 0.0
    for state in states:
        factor = jnp.exp2(state[0] - top)
        total = total + state[1] * factor
        blended = blended + state[2] * factor
    return top, total, blended


def stacked(pieces):
    return pieces[0] if len(pieces) == 1 else jnp.concatenate(pieces, axis=0)


class Block:
    def __init__(self, array, row, rows, col=0):
        self.array, self.row, self.rows, self.col = array, row, rows, col


class Operands:
    def __init__(self):
        self.arrays = []

    def index(self, array):
        for at, each in enumerate(self.arrays):
            if each is array:
                return at
        self.arrays.append(array)
        return len(self.arrays) - 1


def attend(jobs, out_shape, name, after=()):
    operands = Operands()

    def located(block):
        return (operands.index(block.array), block.row, block.rows, block.col)

    plan = [
        (
            [located(q) for q in queries],
            [(located(k), located(v)) for k, v in pairs],
            [located(p) for p in parts],
            out_col,
        )
        for queries, pairs, parts, out_col in jobs
    ]
    count = len(operands.arrays)

    def kernel(*refs):
        out = refs[-1]

        def read(where, head):
            at, row, rows, col = where
            left = pl.multiple_of(col + head * HDIM, HDIM)
            return refs[at][row : row + rows, pl.ds(left, HDIM)]

        def one_job(queries, pairs, parts, out_col):
            def one_head(head, carry):
                if pairs:
                    keys = stacked([read(k, head) for k, _ in pairs])
                    values = stacked([read(v, head) for _, v in pairs])
                cols = pl.ds(pl.multiple_of((out_col or 0) + head * HDIM, HDIM), HDIM)
                for at, query in enumerate(queries):
                    frame = query[2]
                    states = []
                    if pairs:
                        states.append(fresh_state(read(query, head), keys, values))
                    for part in parts:
                        rows = read(part, head)
                        states.append(
                            (
                                stat_column(rows[frame : frame + STAT], frame // HDIM),
                                1.0,
                                rows[:frame].astype(jnp.float32),
                            )
                        )
                    top, total, blended = merge_states(states)
                    done = (blended / total).astype(jnp.bfloat16)
                    if out_col is None:
                        start = at * (frame + STAT)
                        out[start : start + frame, cols] = done
                        out[start + frame : start + frame + STAT, cols] = stat_rows(
                            top + jnp.log2(total)
                        )
                    else:
                        out[:, cols] = done
                return carry

            lax.fori_loop(0, PER, one_head, 0)

        for job in plan:
            one_job(*job)

    work = sum(
        PER * len(queries) * queries[0].rows * sum(k.rows for k, _ in pairs)
        for queries, pairs, _, _ in jobs
    )
    return pl.pallas_call(
        kernel,
        out_shape=jax.ShapeDtypeStruct(out_shape, jnp.bfloat16),
        in_specs=[INSIDE] * count + [ANYWHERE] * len(after),
        out_specs=INSIDE,
        compiler_params=pltpu.CompilerParams(vmem_limit_bytes=VMEM),
        cost_estimate=pl.CostEstimate(
            flops=4 * work * HDIM, bytes_accessed=4_000_000, transcendentals=work
        ),
        name=name,
    )(*operands.arrays, *after)


def home(queries, frame_kv, sink, after):
    frame = queries.shape[0]

    def kernel(query, key, value, sink_key, sink_value, _, out):
        for head in range(PER):
            cols = slice(head * HDIM, (head + 1) * HDIM)
            keys = jnp.concatenate([key[:, cols], sink_key[:, cols]], axis=0)
            values = jnp.concatenate([value[:, cols], sink_value[:, cols]], axis=0)
            top, total, blended = fresh_state(query[:, cols], keys, values)
            out[:frame, cols] = (blended / total).astype(jnp.bfloat16)
            out[frame:, cols] = stat_rows(top + jnp.log2(total))

    def block(array, first):
        return pl.BlockSpec((array.shape[0], CW), lambda at: (0, first + at))

    return pl.pallas_call(
        kernel,
        out_shape=jax.ShapeDtypeStruct((frame + STAT, WIDTH), jnp.bfloat16),
        grid=(CHUNKS,),
        in_specs=[
            block(queries, 0),
            block(frame_kv, 0),
            block(frame_kv, CHUNKS),
            block(sink, 0),
            block(sink, CHUNKS),
            ANYWHERE,
        ],
        out_specs=pl.BlockSpec((frame + STAT, CW), lambda at: (0, at)),
        compiler_params=pltpu.CompilerParams(vmem_limit_bytes=VMEM),
        cost_estimate=pl.CostEstimate(
            flops=4 * WIDTH * frame * (frame + sink.shape[0]),
            bytes_accessed=6_000_000,
            transcendentals=HEADS * frame * (frame + sink.shape[0]),
        ),
        name="home",
    )(queries, frame_kv, frame_kv, sink, sink, after)


def finish(queries, at_home, sinks, came, extra, sink_rows, own=None):
    frame = queries.shape[0]
    as_keys = bool(came) and len(came) == CHUNKS and bool(sinks)
    rows = 2 * frame + 2 * sink_rows
    came_rows = rows if as_keys else frame + STAT
    moved = [(each, came_rows) for each in came] + [(each, rows) for each in extra]
    pairs = 2 * len(sinks) + (4 if own else 0)

    def kernel(*refs):
        query, home_ref = refs[:2]
        sink_refs = refs[2 : 2 + pairs]
        sources = refs[2 + pairs : 2 + pairs + len(moved)]
        out = refs[2 + pairs + len(moved)]
        held = refs[3 + pairs + len(moved) : -1]
        sems = refs[-1]
        step = pl.program_id(0)

        def copy(at):
            return pltpu.make_async_copy(
                sources[at].at[pl.ds(0, moved[at][1])],
                held[0].at[at] if at < len(came) else held[-1].at[at - len(came)],
                sems.at[at],
            )

        if moved:

            @pl.when(step == 0)
            def _():
                for at in range(len(moved)):
                    copy(at).start()

        for at in range(len(came)):

            @pl.when(step == at)
            def _():
                copy(at).wait()

        def chunk(key_places, part_place):
            for head in range(PER):
                cols = slice(head * HDIM, (head + 1) * HDIM)
                keys = [ref[:, cols] for ref in sink_refs[::2]]
                values = [ref[:, cols] for ref in sink_refs[1::2]]
                for buffer, which in key_places:
                    keys += [buffer[which, :frame, cols], buffer[which, 2 * frame : 2 * frame + sink_rows, cols]]
                    values += [buffer[which, frame : 2 * frame, cols], buffer[which, 2 * frame + sink_rows :, cols]]
                parts = [] if own else [home_ref[:, cols]]
                if part_place is not None:
                    parts.append(part_place[0][part_place[1], :, cols])
                if not keys:
                    out[:, cols] = merge_rows(parts, frame).astype(jnp.bfloat16)
                    continue
                states = [fresh_state(query[:, cols], stacked(keys), stacked(values))]
                for part in parts:
                    states.append(
                        (
                            stat_column(part[frame:], frame // HDIM),
                            1.0,
                            part[:frame].astype(jnp.float32),
                        )
                    )
                _, total, blended = merge_states(states)
                out[:, cols] = (blended / total).astype(jnp.bfloat16)

        if extra:

            @pl.when(step < len(came))
            def _():
                chunk([], (held[0], step))

            @pl.when(step == len(came))
            def _():
                for at in range(len(came), len(moved)):
                    copy(at).wait()
                chunk([(held[-1], at) for at in range(len(extra))], None)

        elif as_keys:
            chunk([(held[0], step)], None)
        elif came:
            chunk([], (held[0], step))
        else:
            chunk([], None)

    in_specs = [
        pl.BlockSpec((frame, CW), lambda at: (0, at)),
        pl.BlockSpec((frame + STAT, CW), lambda at: (0, at)),
    ]
    for _ in sinks:
        in_specs += [
            pl.BlockSpec((sink_rows, CW), lambda at: (at, 0)),
            pl.BlockSpec((sink_rows, CW), lambda at: (CHUNKS + at, 0)),
        ]
    own_arrays = []
    if own:
        for array in own:
            for first in (0, CHUNKS):
                own_arrays.append(array)
                in_specs.append(
                    pl.BlockSpec((array.shape[0], CW), lambda at, first=first: (0, first + at))
                )
    scratch = []
    if came:
        scratch.append(pltpu.VMEM((len(came), came_rows, CW), jnp.bfloat16))
    if extra:
        scratch.append(pltpu.VMEM((len(extra), rows, CW), jnp.bfloat16))
    return pl.pallas_call(
        kernel,
        out_shape=jax.ShapeDtypeStruct(queries.shape, jnp.bfloat16),
        grid=(CHUNKS,),
        in_specs=in_specs + [ANYWHERE] * len(moved),
        out_specs=pl.BlockSpec((frame, CW), lambda at: (0, at)),
        scratch_shapes=scratch + [pltpu.SemaphoreType.DMA((max(len(moved), 1),))],
        compiler_params=pltpu.CompilerParams(vmem_limit_bytes=VMEM),
        name="finish",
    )(
        queries,
        at_home,
        *[each for sink in sinks for each in (sink, sink)],
        *own_arrays,
        *[each for each, _ in moved],
    )


def cross(queries, shards, pick, prompt_rows, after):
    frame = queries.shape[0]
    blocks = 2 * CHUNKS
    parts = [each.reshape(blocks, 2, prompt_rows, CW) for each in shards]
    while parts[0].shape[2] % 16:
        half = len(parts) // 2
        parts = [
            jnp.concatenate([one, other], axis=2) for one, other in zip(parts[:half], parts[half:])
        ]
    rows = parts[0].shape[2]
    tokens = rows * len(parts)

    def kernel(pick_ref, query, *refs):
        out, held, sems = refs[-3:]
        copies = [
            pltpu.make_async_copy(
                refs[n].at[:, pick_ref[0]], held.at[:, pl.ds(n * rows, rows)], sems.at[n]
            )
            for n in range(len(parts))
        ]
        for copy in copies:
            copy.start()
        for copy in copies:
            copy.wait()

        def chunk(step, carry):
            for head in range(2 * PER):
                at = 2 * step + head // PER
                cols = pl.ds(head % PER * HDIM, HDIM)
                here = pl.ds(pl.multiple_of(2 * step * CW, HDIM) + head * HDIM, HDIM)
                keys, values = held[at, :, cols], held[CHUNKS + at, :, cols]
                for row in range(0, frame, frame // 2):
                    some = pl.ds(row, frame // 2)
                    _, total, blended = fresh_state(query[some, here], keys, values)
                    out[some, here] = (blended / total).astype(jnp.bfloat16)
            return carry

        lax.fori_loop(0, CHUNKS // 2, chunk, 0)

    work = HEADS * frame * tokens
    return pl.pallas_call(
        kernel,
        out_shape=jax.ShapeDtypeStruct(queries.shape, jnp.bfloat16),
        in_specs=[SCALAR, INSIDE] + [ANYWHERE] * (len(parts) + 1),
        out_specs=INSIDE,
        scratch_shapes=[
            pltpu.VMEM((blocks, tokens, CW), jnp.bfloat16),
            pltpu.SemaphoreType.DMA((len(parts),)),
        ],
        compiler_params=pltpu.CompilerParams(vmem_limit_bytes=VMEM),
        cost_estimate=pl.CostEstimate(
            flops=4 * work * HDIM, bytes_accessed=12_000_000, transcendentals=work
        ),
        name="cross",
    )(pick, queries, *parts, after)


def pack(place, rows, plans, name="pack", after=()):
    operands = Operands()
    located = {
        at: [(operands.index(block.array), block, first) for block, first in items]
        for at, items in plans.items()
    }
    most = max(len(items) for items in located.values())

    def kernel(place_ref, *refs):
        out, sems = refs[-2:]
        for at, items in located.items():

            @pl.when(place_ref[0] == at)
            def _():
                copies = [
                    pltpu.make_async_copy(
                        refs[which].at[pl.ds(block.row, block.rows), pl.ds(block.col, CW)],
                        out.at[pl.ds(first, block.rows), :],
                        sems.at[n],
                    )
                    for n, (which, block, first) in enumerate(items)
                ]
                for copy in copies:
                    copy.start()
                for copy in copies:
                    copy.wait()

    return pl.pallas_call(
        kernel,
        out_shape=jax.ShapeDtypeStruct((rows, CW), jnp.bfloat16),
        in_specs=[SCALAR] + [ANYWHERE] * (len(operands.arrays) + len(after)),
        out_specs=INSIDE,
        scratch_shapes=[pltpu.SemaphoreType.DMA((most,))],
        cost_estimate=pl.CostEstimate(flops=0, bytes_accessed=2_000_000, transcendentals=0),
        name=name,
    )(place, *operands.arrays, *after)


def unused(rows, after):
    return pl.pallas_call(
        lambda _, out: None,
        out_shape=jax.ShapeDtypeStruct((rows, CW), jnp.bfloat16),
        in_specs=[ANYWHERE],
        out_specs=ANYWHERE,
        name="unused",
    )(after)


def shards(queries, cross_queries, frame_kv, sink_kv, prompt_kv, switch):
    streams = lax.axis_size("span") // WIN
    device = lax.axis_index("span")
    place = device // streams
    stream = device % streams
    frame = queries.shape[0]
    sink = sink_kv.reshape(sink_kv.shape[1], sink_kv.shape[2])
    sink_rows = sink.shape[0]
    prompt_rows = prompt_kv.shape[1]
    prompt_both = prompt_kv.reshape(2 * prompt_rows, prompt_kv.shape[2])
    part_rows = frame + STAT
    place_ref = place.reshape(1).astype(jnp.int32)

    def move(value, *pairs):
        both = [(a * streams + s, b * streams + s) for a, b in pairs for s in range(streams)]
        return lax.ppermute(value, "span", both)

    def across(value, flip):
        pairs = [(at, at - at % streams + ((at % streams) ^ flip)) for at in range(WIN * streams)]
        return lax.ppermute(value, "span", pairs)

    def choose(branches, *operands):
        return lax.switch(place, branches, *operands)

    def columns(array, height):
        count = array.shape[1] // CW
        return [(Block(array, 0, height, at * CW), at * height) for at in range(count)]

    def cut(row, rows, first, array, col=0):
        size = rows // 4 if rows % 64 == 0 else rows
        return [
            (Block(array, row + at, size, col), first + at) for at in range(0, rows, size)
        ]

    def query_chunks(array, *chunks):
        return [
            each
            for at, chunk in enumerate(chunks)
            for each in cut(0, frame, at * frame, array, chunk * CW)
        ]

    def kvs(frame_array, sink_array, chunk):
        low = chunk * CW
        return [
            (Block(frame_array, 0, frame, low), 0),
            (Block(frame_array, 0, frame, WIDTH + low), frame),
            (Block(sink_array, 0, sink_rows, low), 2 * frame),
            (Block(sink_array, 0, sink_rows, WIDTH + low), 2 * frame + sink_rows),
        ]

    def whole(array, rows):
        return cut(0, rows, 0, array)

    def own_pairs(frame_array, sink_array, chunk):
        low = chunk * CW
        return [
            (Block(frame_array, 0, frame, low), Block(frame_array, 0, frame, WIDTH + low)),
            (Block(sink_array, 0, sink_rows, low), Block(sink_array, 0, sink_rows, WIDTH + low)),
        ]

    def kvs_pairs(array):
        return [
            (Block(array, 0, frame), Block(array, frame, frame)),
            (
                Block(array, 2 * frame, sink_rows),
                Block(array, 2 * frame + sink_rows, sink_rows),
            ),
        ]

    def sink_pair(array, chunk):
        return (
            Block(array, chunk * sink_rows, sink_rows),
            Block(array, (CHUNKS + chunk) * sink_rows, sink_rows),
        )

    def part(array, index=0, col=0):
        return Block(array, index * part_rows, part_rows, col)

    def spread(shard):
        held = [shard]
        flip = streams // 2
        while flip > 0:
            held = held + [across(each, flip) for each in held]
            flip //= 2
        return held

    stream_ids = jnp.arange(switch.shape[0], dtype=jnp.int32)
    switch_at = jnp.sum(jnp.where(stream_ids == stream, switch, 0))
    pick = (place >= switch_at).astype(jnp.int32).reshape(1)

    prompt_size = 4 * CHUNKS * prompt_rows
    sink_size = 2 * CHUNKS * sink_rows
    same = max(prompt_size, 2 * frame, sink_size)
    kvs_rows = 2 * frame + 2 * sink_rows
    wide = max(kvs_rows, prompt_size, 2 * part_rows)
    two = 2 * part_rows

    prompt = pack(
        place_ref,
        prompt_size,
        {p: columns(prompt_both, 2 * prompt_rows) for p in range(WIN)},
        name="prompt",
    )
    up_a = move(prompt, (0, 1), (1, 2), (2, 3))
    send_b = pack(
        place_ref,
        same,
        {1: whole(prompt, prompt_size), 2: query_chunks(queries, 0, 1), 3: whole(prompt, prompt_size)},
        name="send_b",
    )
    down_b = move(send_b, (3, 2), (2, 1), (1, 0))
    send_c = pack(
        place_ref,
        kvs_rows,
        {0: kvs(frame_kv, sink, 3), 1: kvs(frame_kv, sink, 3)},
        name="send_c",
        after=(send_b,),
    )
    up_c = move(send_c, (0, 1), (1, 2))
    send_d = pack(
        place_ref,
        same,
        {1: columns(sink, sink_rows), 3: query_chunks(queries, 0, 1)},
        name="send_d",
        after=(send_c,),
    )
    down_d = move(send_d, (3, 1), (1, 0))
    stages = spread(prompt)
    at_home = home(queries, frame_kv, sink, send_d)

    send_e = pack(
        place_ref,
        wide,
        {
            0: kvs(frame_kv, sink, 0),
            1: whole(up_a, prompt_size),
            2: whole(up_a, prompt_size),
        },
        name="send_e",
        after=(at_home,),
    )
    up_e = move(send_e, (0, 1), (1, 2), (2, 3))
    send_f = pack(
        place_ref,
        same,
        {2: whole(prompt, prompt_size), 3: query_chunks(queries, 2, 3)},
        name="send_f",
        after=(send_e,),
    )
    down_f = move(send_f, (3, 2), (2, 1))
    second = pack(
        place_ref,
        prompt_size,
        {p: whole(down_b if p == 0 else up_a, prompt_size) for p in range(WIN)},
        name="second_shard",
        after=(send_f,),
    )
    stages += spread(second)
    send_g = pack(
        place_ref,
        kvs_rows,
        {0: kvs(frame_kv, sink, 1), 1: whole(up_c, kvs_rows)},
        name="send_g",
        after=(second,),
    )
    up_g = move(send_g, (0, 1), (1, 2))
    send_i = pack(
        place_ref,
        same,
        {2: whole(down_b, same), 3: query_chunks(queries, 0, 1)},
        name="send_i",
        after=(send_g,),
    )
    down_i = move(send_i, (3, 2), (2, 1))
    send_k = pack(
        place_ref,
        same,
        {
            1: whole(down_f, prompt_size),
            2: cut(0, frame, 0, queries, 2 * CW) + cut(0, frame, frame, down_f),
            3: columns(sink, sink_rows),
        },
        name="send_k",
        after=(send_i,),
    )
    down_k = move(send_k, (3, 2), (2, 1), (1, 0))

    def visit(q2, q3, came, frame_array, sink_array, chunk, rows):
        return attend(
            [([q2, q3], own_pairs(frame_array, sink_array, chunk) + kvs_pairs(came), [], None)],
            (rows, CW),
            "visit",
        )

    def join(query, came, frame_array, sink_array, chunk, rows):
        return attend(
            [([query], own_pairs(frame_array, sink_array, chunk), [part(came, 1)], None)],
            (rows, CW),
            "join",
        )

    def branch_pack(rows, items):
        return pack(jnp.zeros((1,), jnp.int32), rows, {0: items}, name="branch")

    send_h = choose(
        [
            lambda t, f, s, e, b, d: branch_pack(wide, kvs(f, s, 2)),
            lambda t, f, s, e, b, d: visit(
                Block(b, 0, frame), Block(d, 0, frame), e, f, s, 0, wide
            ),
            lambda t, f, s, e, b, d: branch_pack(wide, whole(e, prompt_size)),
            lambda t, f, s, e, b, d: unused(wide, t),
        ],
        send_k,
        frame_kv,
        sink,
        up_e,
        down_b,
        down_d,
    )
    up_h = move(send_h, (0, 1), (1, 2), (2, 3))
    send_l = pack(
        place_ref,
        same,
        {1: whole(down_i, same), 2: columns(sink, sink_rows)},
        name="send_l",
        after=(send_h,),
    )
    down_l = move(send_l, (2, 1), (1, 0))
    send_j = choose(
        [
            lambda t, f, s, c, g, b, d, fd: unused(two, t),
            lambda t, f, s, c, g, b, d, fd: visit(
                Block(b, frame, frame), Block(d, frame, frame), g, f, s, 1, two
            ),
            lambda t, f, s, c, g, b, d, fd: attend(
                [([Block(fd, frame, frame)], own_pairs(f, s, 3) + kvs_pairs(c) + kvs_pairs(g), [], None)],
                (two, CW),
                "all_d",
            ),
            lambda t, f, s, c, g, b, d, fd: unused(two, t),
        ],
        send_l,
        frame_kv,
        sink,
        up_c,
        up_g,
        down_b,
        down_d,
        down_f,
    )
    up_j = move(send_j, (1, 2), (2, 3))
    third = pack(
        place_ref,
        prompt_size,
        {
            0: whole(down_k, prompt_size),
            1: whole(down_f, prompt_size),
            2: whole(down_b, prompt_size),
            3: whole(up_e, prompt_size),
        },
        name="third_shard",
        after=(send_j,),
    )
    stages += spread(third)
    down_m = move(down_k, (2, 1))
    down_o = move(down_l, (1, 0))
    send_n = choose(
        [
            lambda t, f, s, h, k, i: unused(two, t),
            lambda t, f, s, h, k, i: visit(
                Block(k, 0, frame), Block(k, frame, frame), h, f, s, 2, two
            ),
            lambda t, f, s, h, k, i: join(Block(i, 0, frame), h, f, s, 0, two),
            lambda t, f, s, h, k, i: unused(two, t),
        ],
        third,
        frame_kv,
        sink,
        up_h,
        down_k,
        down_i,
    )
    up_n = move(send_n, (1, 2), (2, 3))
    last = pack(
        place_ref,
        prompt_size,
        {
            0: whole(down_l, prompt_size),
            1: whole(down_i, prompt_size),
            2: whole(up_e, prompt_size),
            3: whole(up_h, prompt_size),
        },
        name="last_shard",
        after=(stages[6], send_n,),
    )
    stages += spread(last)
    send_o = choose(
        [
            lambda t, f, s, j, i: unused(part_rows, t),
            lambda t, f, s, j, i: unused(part_rows, t),
            lambda t, f, s, j, i: join(Block(i, frame, frame), j, f, s, 1, part_rows),
            lambda t, f, s, j, i: unused(part_rows, t),
        ],
        last,
        frame_kv,
        sink,
        up_j,
        down_i,
    )
    up_o = move(send_o, (2, 3))
    down_r = move(down_m, (1, 0))
    cross_out = cross(cross_queries, stages, pick, prompt_rows, send_o)
    send_q = choose(
        [
            lambda t, f, s, n, d: unused(part_rows, t),
            lambda t, f, s, n, d: unused(part_rows, t),
            lambda t, f, s, n, d: join(Block(d, 0, frame), n, f, s, 2, part_rows),
            lambda t, f, s, n, d: unused(part_rows, t),
        ],
        send_o,
        frame_kv,
        sink,
        up_n,
        down_f,
    )
    up_q = move(send_q, (2, 3))


    def finish0(q, h, f, s, x, u, d):
        return finish(q, h, [d["d"], d["o"], d["r"]], [], [], sink_rows, (f, s))

    def finish1(q, h, f, s, x, u, d):
        return finish(q, h, [d["l"], d["m"]], [u["e"], u["g"], u["h"], u["c"]], [], sink_rows)

    def finish2(q, h, f, s, x, u, d):
        return finish(q, h, [d["k"]], [u["h"], u["j"], u["n"]], [u["c"], u["g"]], sink_rows)

    def finish3(q, h, f, s, x, u, d):
        return finish(q, h, [], [u["n"], u["o"], u["q"], u["j"]], [], sink_rows)

    ups = {"c": up_c, "e": up_e, "g": up_g, "h": up_h, "j": up_j, "n": up_n, "o": up_o, "q": up_q}
    downs = {"d": down_d, "k": down_k, "l": down_l, "m": down_m, "o": down_o, "r": down_r}
    self_out = choose(
        [finish0, finish1, finish2, finish3], queries, at_home, frame_kv, sink, cross_out, ups, downs
    )
    return (self_out, cross_out)


def solution(mesh):
    in_specs = (
        P(("groups", "span"), None),
        P(("groups", "span"), None),
        P(("groups", "span"), None),
        P(("groups", "span"), None, None),
        P("groups", "span", None),
        P("groups"),
    )
    out_specs = (P(("groups", "span"), None), P(("groups", "span"), None))
    return jax.shard_map(shards, mesh=mesh, in_specs=in_specs, out_specs=out_specs, check_vma=False)
```

```python
import math

import jax
import jax.numpy as jnp
from jax import lax
from jax.experimental import pallas as pl
from jax.experimental.pallas import tpu as pltpu
from jax.sharding import PartitionSpec as P

HEADS = 20
HDIM = 128
WIN = 4
CHUNKS = 4
PER = HEADS // CHUNKS
CW = PER * HDIM
WIDTH = HEADS * HDIM
STAT = 16
LOG_SCALE = math.log2(math.e) / math.sqrt(HDIM)
VMEM = 48 * 1024 * 1024
ANYWHERE = pl.BlockSpec(memory_space=pl.ANY)
SCALAR = pl.BlockSpec(memory_space=pltpu.SMEM)
INSIDE = pl.BlockSpec(memory_space=pltpu.VMEM)


def diagonal():
    rows = lax.broadcasted_iota(jnp.int32, (HDIM, HDIM), 0)
    cols = lax.broadcasted_iota(jnp.int32, (HDIM, HDIM), 1)
    return rows == cols


def stat_rows(column):
    eye = diagonal()
    groups = column.shape[0] // HDIM
    tops, mids, lows = [], [], []
    for group in range(groups):
        part = column[group * HDIM : (group + 1) * HDIM]
        row = jnp.sum(jnp.where(eye, part, 0.0), axis=0, keepdims=True)
        top = row.astype(jnp.bfloat16).astype(jnp.float32)
        mid = (row - top).astype(jnp.bfloat16).astype(jnp.float32)
        tops.append(top)
        mids.append(mid)
        lows.append(row - top - mid)
    used = tops + mids + lows
    used.append(jnp.zeros((STAT - len(used), HDIM), jnp.float32))
    return jnp.concatenate(used, axis=0).astype(jnp.bfloat16)


def stat_column(tile, groups):
    eye = diagonal()
    tile = tile.astype(jnp.float32)
    columns = []
    for group in range(groups):
        row = (
            tile[group : group + 1]
            + tile[groups + group : groups + group + 1]
            + tile[2 * groups + group : 2 * groups + group + 1]
        )
        columns.append(jnp.sum(jnp.where(eye, row, 0.0), axis=1, keepdims=True))
    return jnp.concatenate(columns, axis=0)


def fresh_state(query, keys, values):
    scores = lax.dot_general(
        query, keys, (((1,), (1,)), ((), ())), preferred_element_type=jnp.float32
    )
    top = jnp.max(scores, axis=1, keepdims=True)
    weights = jnp.exp2((scores - top) * LOG_SCALE).astype(jnp.bfloat16)
    beside = jnp.concatenate([values, jnp.ones_like(values)], axis=1)
    both = jnp.dot(weights, beside, preferred_element_type=jnp.float32)
    return top * LOG_SCALE, both[:, HDIM:], both[:, :HDIM]


def merge_rows(parts, frame):
    eye = diagonal()
    groups = frame // HDIM
    logs = []
    for part in parts:
        tile = part[frame : frame + 3 * groups].astype(jnp.float32)
        logs.append(
            tile[:groups] + tile[groups : 2 * groups] + tile[2 * groups : 3 * groups]
        )
    top = logs[0]
    for each in logs[1:]:
        top = jnp.maximum(top, each)
    shares = [jnp.exp2(each - top) for each in logs]
    total = shares[0]
    for each in shares[1:]:
        total = total + each
    merged = []
    for group in range(groups):
        rows = 0.0
        for part, share in zip(parts, shares):
            row = (share / total)[group : group + 1]
            column = jnp.sum(jnp.where(eye, row, 0.0), axis=1, keepdims=True)
            rows = rows + column * part[group * HDIM : (group + 1) * HDIM].astype(jnp.float32)
        merged.append(rows)
    return jnp.concatenate(merged, axis=0)


def merge_states(states):
    if len(states) == 1:
        return states[0]
    top = states[0][0]
    for state in states[1:]:
        top = jnp.maximum(top, state[0])
    total, blended = 0.0, 0.0
    for state in states:
        factor = jnp.exp2(state[0] - top)
        total = total + state[1] * factor
        blended = blended + state[2] * factor
    return top, total, blended


def stacked(pieces):
    return pieces[0] if len(pieces) == 1 else jnp.concatenate(pieces, axis=0)


class Block:
    def __init__(self, array, row, rows, col=0):
        self.array, self.row, self.rows, self.col = array, row, rows, col


class Operands:
    def __init__(self):
        self.arrays = []

    def index(self, array):
        for at, each in enumerate(self.arrays):
            if each is array:
                return at
        self.arrays.append(array)
        return len(self.arrays) - 1


def attend(jobs, out_shape, name, after=()):
    operands = Operands()

    def located(block):
        return (operands.index(block.array), block.row, block.rows, block.col)

    plan = [
        (
            [located(q) for q in queries],
            [(located(k), located(v)) for k, v in pairs],
            [located(p) for p in parts],
            out_col,
        )
        for queries, pairs, parts, out_col in jobs
    ]
    count = len(operands.arrays)

    def kernel(*refs):
        out = refs[-1]

        def read(where, head):
            at, row, rows, col = where
            left = pl.multiple_of(col + head * HDIM, HDIM)
            return refs[at][row : row + rows, pl.ds(left, HDIM)]

        def one_job(queries, pairs, parts, out_col):
            def one_head(head, carry):
                if pairs:
                    keys = stacked([read(k, head) for k, _ in pairs])
                    values = stacked([read(v, head) for _, v in pairs])
                cols = pl.ds(pl.multiple_of((out_col or 0) + head * HDIM, HDIM), HDIM)
                for at, query in enumerate(queries):
                    frame = query[2]
                    states = []
                    if pairs:
                        states.append(fresh_state(read(query, head), keys, values))
                    for part in parts:
                        rows = read(part, head)
                        states.append(
                            (
                                stat_column(rows[frame : frame + STAT], frame // HDIM),
                                1.0,
                                rows[:frame].astype(jnp.float32),
                            )
                        )
                    top, total, blended = merge_states(states)
                    done = (blended / total).astype(jnp.bfloat16)
                    if out_col is None:
                        start = at * (frame + STAT)
                        out[start : start + frame, cols] = done
                        out[start + frame : start + frame + STAT, cols] = stat_rows(
                            top + jnp.log2(total)
                        )
                    else:
                        out[:, cols] = done
                return carry

            lax.fori_loop(0, PER, one_head, 0)

        for job in plan:
            one_job(*job)

    work = sum(
        PER * len(queries) * queries[0].rows * sum(k.rows for k, _ in pairs)
        for queries, pairs, _, _ in jobs
    )
    return pl.pallas_call(
        kernel,
        out_shape=jax.ShapeDtypeStruct(out_shape, jnp.bfloat16),
        in_specs=[INSIDE] * count + [ANYWHERE] * len(after),
        out_specs=INSIDE,
        compiler_params=pltpu.CompilerParams(vmem_limit_bytes=VMEM),
        cost_estimate=pl.CostEstimate(
            flops=4 * work * HDIM, bytes_accessed=4_000_000, transcendentals=work
        ),
        name=name,
    )(*operands.arrays, *after)


def home(queries, frame_kv, sink, after):
    frame = queries.shape[0]

    def kernel(query, key, value, sink_key, sink_value, _, out):
        for head in range(PER):
            cols = slice(head * HDIM, (head + 1) * HDIM)
            keys = jnp.concatenate([key[:, cols], sink_key[:, cols]], axis=0)
            values = jnp.concatenate([value[:, cols], sink_value[:, cols]], axis=0)
            top, total, blended = fresh_state(query[:, cols], keys, values)
            out[:frame, cols] = (blended / total).astype(jnp.bfloat16)
            out[frame:, cols] = stat_rows(top + jnp.log2(total))

    def block(array, first):
        return pl.BlockSpec((array.shape[0], CW), lambda at: (0, first + at))

    return pl.pallas_call(
        kernel,
        out_shape=jax.ShapeDtypeStruct((frame + STAT, WIDTH), jnp.bfloat16),
        grid=(CHUNKS,),
        in_specs=[
            block(queries, 0),
            block(frame_kv, 0),
            block(frame_kv, CHUNKS),
            block(sink, 0),
            block(sink, CHUNKS),
            ANYWHERE,
        ],
        out_specs=pl.BlockSpec((frame + STAT, CW), lambda at: (0, at)),
        compiler_params=pltpu.CompilerParams(vmem_limit_bytes=VMEM),
        cost_estimate=pl.CostEstimate(
            flops=4 * WIDTH * frame * (frame + sink.shape[0]),
            bytes_accessed=6_000_000,
            transcendentals=HEADS * frame * (frame + sink.shape[0]),
        ),
        name="home",
    )(queries, frame_kv, frame_kv, sink, sink, after)


def finish(queries, at_home, sinks, came, extra, sink_rows, own=None):
    frame = queries.shape[0]
    as_keys = bool(came) and len(came) == CHUNKS and bool(sinks)
    rows = 2 * frame + 2 * sink_rows
    came_rows = rows if as_keys else frame + STAT
    moved = [(each, came_rows) for each in came] + [(each, rows) for each in extra]
    pairs = 2 * len(sinks) + (4 if own else 0)

    def kernel(*refs):
        query, home_ref = refs[:2]
        sink_refs = refs[2 : 2 + pairs]
        sources = refs[2 + pairs : 2 + pairs + len(moved)]
        out = refs[2 + pairs + len(moved)]
        held = refs[3 + pairs + len(moved) : -1]
        sems = refs[-1]
        step = pl.program_id(0)

        def copy(at):
            return pltpu.make_async_copy(
                sources[at].at[pl.ds(0, moved[at][1])],
                held[0].at[at] if at < len(came) else held[-1].at[at - len(came)],
                sems.at[at],
            )

        if moved:

            @pl.when(step == 0)
            def _():
                for at in range(len(moved)):
                    copy(at).start()

        for at in range(len(came)):

            @pl.when(step == at)
            def _():
                copy(at).wait()

        def chunk(key_places, part_place):
            for head in range(PER):
                cols = slice(head * HDIM, (head + 1) * HDIM)
                keys = [ref[:, cols] for ref in sink_refs[::2]]
                values = [ref[:, cols] for ref in sink_refs[1::2]]
                for buffer, which in key_places:
                    keys += [buffer[which, :frame, cols], buffer[which, 2 * frame : 2 * frame + sink_rows, cols]]
                    values += [buffer[which, frame : 2 * frame, cols], buffer[which, 2 * frame + sink_rows :, cols]]
                parts = [] if own else [home_ref[:, cols]]
                if part_place is not None:
                    parts.append(part_place[0][part_place[1], :, cols])
                if not keys:
                    out[:, cols] = merge_rows(parts, frame).astype(jnp.bfloat16)
                    continue
                both = [
                    fresh_state(query[row : row + frame // 2, cols], stacked(keys), stacked(values))
                    for row in (0, frame // 2)
                ]
                states = [tuple(jnp.concatenate(pair, axis=0) for pair in zip(*both))]
                for part in parts:
                    states.append(
                        (
                            stat_column(part[frame:], frame // HDIM),
                            1.0,
                            part[:frame].astype(jnp.float32),
                        )
                    )
                _, total, blended = merge_states(states)
                out[:, cols] = (blended / total).astype(jnp.bfloat16)

        if extra:

            @pl.when(step < len(came))
            def _():
                chunk([], (held[0], step))

            @pl.when(step == len(came))
            def _():
                for at in range(len(came), len(moved)):
                    copy(at).wait()
                chunk([(held[-1], at) for at in range(len(extra))], None)

        elif as_keys:
            chunk([(held[0], step)], None)
        elif came:
            chunk([], (held[0], step))
        else:
            chunk([], None)

    in_specs = [
        pl.BlockSpec((frame, CW), lambda at: (0, at)),
        pl.BlockSpec((frame + STAT, CW), lambda at: (0, at)),
    ]
    for _ in sinks:
        in_specs += [
            pl.BlockSpec((sink_rows, CW), lambda at: (at, 0)),
            pl.BlockSpec((sink_rows, CW), lambda at: (CHUNKS + at, 0)),
        ]
    own_arrays = []
    if own:
        for array in own:
            for first in (0, CHUNKS):
                own_arrays.append(array)
                in_specs.append(
                    pl.BlockSpec((array.shape[0], CW), lambda at, first=first: (0, first + at))
                )
    scratch = []
    if came:
        scratch.append(pltpu.VMEM((len(came), came_rows, CW), jnp.bfloat16))
    if extra:
        scratch.append(pltpu.VMEM((len(extra), rows, CW), jnp.bfloat16))
    return pl.pallas_call(
        kernel,
        out_shape=jax.ShapeDtypeStruct(queries.shape, jnp.bfloat16),
        grid=(CHUNKS,),
        in_specs=in_specs + [ANYWHERE] * len(moved),
        out_specs=pl.BlockSpec((frame, CW), lambda at: (0, at)),
        scratch_shapes=scratch + [pltpu.SemaphoreType.DMA((max(len(moved), 1),))],
        compiler_params=pltpu.CompilerParams(vmem_limit_bytes=VMEM),
        name="finish",
    )(
        queries,
        at_home,
        *[each for sink in sinks for each in (sink, sink)],
        *own_arrays,
        *[each for each, _ in moved],
    )


def cross(queries, shards, pick, prompt_rows, after):
    frame = queries.shape[0]
    blocks = 2 * CHUNKS
    parts = [each.reshape(blocks, 2, prompt_rows, CW) for each in shards]
    while parts[0].shape[2] % 16:
        half = len(parts) // 2
        parts = [
            jnp.concatenate([one, other], axis=2) for one, other in zip(parts[:half], parts[half:])
        ]
    rows = parts[0].shape[2]
    tokens = rows * len(parts)

    def kernel(pick_ref, query, *refs):
        out, held, sems = refs[-3:]
        copies = [
            pltpu.make_async_copy(
                refs[n].at[:, pick_ref[0]], held.at[:, pl.ds(n * rows, rows)], sems.at[n]
            )
            for n in range(len(parts))
        ]
        for copy in copies:
            copy.start()
        for copy in copies:
            copy.wait()

        def chunk(step, carry):
            for head in range(2 * PER):
                at = 2 * step + head // PER
                cols = pl.ds(head % PER * HDIM, HDIM)
                here = pl.ds(pl.multiple_of(2 * step * CW, HDIM) + head * HDIM, HDIM)
                keys, values = held[at, :, cols], held[CHUNKS + at, :, cols]
                for row in range(0, frame, frame // 2):
                    some = pl.ds(row, frame // 2)
                    _, total, blended = fresh_state(query[some, here], keys, values)
                    out[some, here] = (blended / total).astype(jnp.bfloat16)
            return carry

        lax.fori_loop(0, CHUNKS // 2, chunk, 0)

    work = HEADS * frame * tokens
    return pl.pallas_call(
        kernel,
        out_shape=jax.ShapeDtypeStruct(queries.shape, jnp.bfloat16),
        in_specs=[SCALAR, INSIDE] + [ANYWHERE] * (len(parts) + 1),
        out_specs=INSIDE,
        scratch_shapes=[
            pltpu.VMEM((blocks, tokens, CW), jnp.bfloat16),
            pltpu.SemaphoreType.DMA((len(parts),)),
        ],
        compiler_params=pltpu.CompilerParams(vmem_limit_bytes=VMEM),
        cost_estimate=pl.CostEstimate(
            flops=4 * work * HDIM, bytes_accessed=12_000_000, transcendentals=work
        ),
        name="cross",
    )(pick, queries, *parts, after)


def pack(place, rows, plans, name="pack", after=()):
    operands = Operands()
    located = {
        at: [(operands.index(block.array), block, first) for block, first in items]
        for at, items in plans.items()
    }
    most = max(len(items) for items in located.values())

    def kernel(place_ref, *refs):
        out, sems = refs[-2:]
        for at, items in located.items():

            @pl.when(place_ref[0] == at)
            def _():
                copies = [
                    pltpu.make_async_copy(
                        refs[which].at[pl.ds(block.row, block.rows), pl.ds(block.col, CW)],
                        out.at[pl.ds(first, block.rows), :],
                        sems.at[n],
                    )
                    for n, (which, block, first) in enumerate(items)
                ]
                for copy in copies:
                    copy.start()
                for copy in copies:
                    copy.wait()

    return pl.pallas_call(
        kernel,
        out_shape=jax.ShapeDtypeStruct((rows, CW), jnp.bfloat16),
        in_specs=[SCALAR] + [ANYWHERE] * (len(operands.arrays) + len(after)),
        out_specs=INSIDE,
        scratch_shapes=[pltpu.SemaphoreType.DMA((most,))],
        cost_estimate=pl.CostEstimate(flops=0, bytes_accessed=2_000_000, transcendentals=0),
        name=name,
    )(place, *operands.arrays, *after)


def unused(rows, after):
    return pl.pallas_call(
        lambda _, out: None,
        out_shape=jax.ShapeDtypeStruct((rows, CW), jnp.bfloat16),
        in_specs=[ANYWHERE],
        out_specs=ANYWHERE,
        name="unused",
    )(after)


def shards(queries, cross_queries, frame_kv, sink_kv, prompt_kv, switch):
    streams = lax.axis_size("span") // WIN
    device = lax.axis_index("span")
    place = device // streams
    stream = device % streams
    frame = queries.shape[0]
    sink = sink_kv.reshape(sink_kv.shape[1], sink_kv.shape[2])
    sink_rows = sink.shape[0]
    prompt_rows = prompt_kv.shape[1]
    prompt_both = prompt_kv.reshape(2 * prompt_rows, prompt_kv.shape[2])
    part_rows = frame + STAT
    place_ref = place.reshape(1).astype(jnp.int32)

    def move(value, *pairs):
        both = [(a * streams + s, b * streams + s) for a, b in pairs for s in range(streams)]
        return lax.ppermute(value, "span", both)

    def across(value, flip):
        pairs = [(at, at - at % streams + ((at % streams) ^ flip)) for at in range(WIN * streams)]
        return lax.ppermute(value, "span", pairs)

    def choose(branches, *operands):
        return lax.switch(place, branches, *operands)

    def columns(array, height):
        count = array.shape[1] // CW
        return [(Block(array, 0, height, at * CW), at * height) for at in range(count)]

    def cut(row, rows, first, array, col=0):
        size = rows // 4 if rows % 64 == 0 else rows
        return [
            (Block(array, row + at, size, col), first + at) for at in range(0, rows, size)
        ]

    def query_chunks(array, *chunks):
        return [
            each
            for at, chunk in enumerate(chunks)
            for each in cut(0, frame, at * frame, array, chunk * CW)
        ]

    def kvs(frame_array, sink_array, chunk):
        low = chunk * CW
        return [
            (Block(frame_array, 0, frame, low), 0),
            (Block(frame_array, 0, frame, WIDTH + low), frame),
            (Block(sink_array, 0, sink_rows, low), 2 * frame),
            (Block(sink_array, 0, sink_rows, WIDTH + low), 2 * frame + sink_rows),
        ]

    def whole(array, rows):
        return cut(0, rows, 0, array)

    def own_pairs(frame_array, sink_array, chunk):
        low = chunk * CW
        return [
            (Block(frame_array, 0, frame, low), Block(frame_array, 0, frame, WIDTH + low)),
            (Block(sink_array, 0, sink_rows, low), Block(sink_array, 0, sink_rows, WIDTH + low)),
        ]

    def kvs_pairs(array):
        return [
            (Block(array, 0, frame), Block(array, frame, frame)),
            (
                Block(array, 2 * frame, sink_rows),
                Block(array, 2 * frame + sink_rows, sink_rows),
            ),
        ]

    def sink_pair(array, chunk):
        return (
            Block(array, chunk * sink_rows, sink_rows),
            Block(array, (CHUNKS + chunk) * sink_rows, sink_rows),
        )

    def part(array, index=0, col=0):
        return Block(array, index * part_rows, part_rows, col)

    def spread(shard):
        held = [shard]
        flip = streams // 2
        while flip > 0:
            held = held + [across(each, flip) for each in held]
            flip //= 2
        return held

    stream_ids = jnp.arange(switch.shape[0], dtype=jnp.int32)
    switch_at = jnp.sum(jnp.where(stream_ids == stream, switch, 0))
    pick = (place >= switch_at).astype(jnp.int32).reshape(1)

    prompt_size = 4 * CHUNKS * prompt_rows
    sink_size = 2 * CHUNKS * sink_rows
    same = max(prompt_size, 2 * frame, sink_size)
    kvs_rows = 2 * frame + 2 * sink_rows
    wide = max(kvs_rows, prompt_size, 2 * part_rows)
    two = 2 * part_rows

    prompt = pack(
        place_ref,
        prompt_size,
        {p: columns(prompt_both, 2 * prompt_rows) for p in range(WIN)},
        name="prompt",
    )
    up_a = move(prompt, (0, 1), (1, 2), (2, 3))
    send_b = pack(
        place_ref,
        same,
        {1: whole(prompt, prompt_size), 2: query_chunks(queries, 0, 1), 3: whole(prompt, prompt_size)},
        name="send_b",
    )
    down_b = move(send_b, (3, 2), (2, 1), (1, 0))
    send_c = pack(
        place_ref,
        kvs_rows,
        {0: kvs(frame_kv, sink, 3), 1: kvs(frame_kv, sink, 3)},
        name="send_c",
        after=(send_b,),
    )
    up_c = move(send_c, (0, 1), (1, 2))
    send_d = pack(
        place_ref,
        same,
        {1: columns(sink, sink_rows), 3: query_chunks(queries, 0, 1)},
        name="send_d",
        after=(send_c,),
    )
    down_d = move(send_d, (3, 1), (1, 0))
    stages = spread(prompt)
    at_home = home(queries, frame_kv, sink, send_d)

    send_e = pack(
        place_ref,
        wide,
        {
            0: kvs(frame_kv, sink, 0),
            1: whole(up_a, prompt_size),
            2: whole(up_a, prompt_size),
        },
        name="send_e",
        after=(at_home,),
    )
    up_e = move(send_e, (0, 1), (1, 2), (2, 3))
    send_f = pack(
        place_ref,
        same,
        {2: whole(prompt, prompt_size), 3: query_chunks(queries, 2, 3)},
        name="send_f",
        after=(send_e,),
    )
    down_f = move(send_f, (3, 2), (2, 1))
    second = pack(
        place_ref,
        prompt_size,
        {p: whole(down_b if p == 0 else up_a, prompt_size) for p in range(WIN)},
        name="second_shard",
        after=(send_f,),
    )
    stages += spread(second)
    send_g = pack(
        place_ref,
        kvs_rows,
        {0: kvs(frame_kv, sink, 1), 1: whole(up_c, kvs_rows)},
        name="send_g",
        after=(second,),
    )
    up_g = move(send_g, (0, 1), (1, 2))
    send_i = pack(
        place_ref,
        same,
        {2: whole(down_b, same), 3: query_chunks(queries, 0, 1)},
        name="send_i",
        after=(send_g,),
    )
    down_i = move(send_i, (3, 2), (2, 1))
    send_k = pack(
        place_ref,
        same,
        {
            1: whole(down_f, prompt_size),
            2: cut(0, frame, 0, queries, 2 * CW) + cut(0, frame, frame, down_f),
            3: columns(sink, sink_rows),
        },
        name="send_k",
        after=(send_i,),
    )
    down_k = move(send_k, (3, 2), (2, 1), (1, 0))

    def visit(q2, q3, came, frame_array, sink_array, chunk, rows):
        return attend(
            [([q2, q3], own_pairs(frame_array, sink_array, chunk) + kvs_pairs(came), [], None)],
            (rows, CW),
            "visit",
        )

    def join(query, came, frame_array, sink_array, chunk, rows):
        return attend(
            [([query], own_pairs(frame_array, sink_array, chunk), [part(came, 1)], None)],
            (rows, CW),
            "join",
        )

    def branch_pack(rows, items):
        return pack(jnp.zeros((1,), jnp.int32), rows, {0: items}, name="branch")

    send_h = choose(
        [
            lambda t, f, s, e, b, d: branch_pack(wide, kvs(f, s, 2)),
            lambda t, f, s, e, b, d: visit(
                Block(b, 0, frame), Block(d, 0, frame), e, f, s, 0, wide
            ),
            lambda t, f, s, e, b, d: branch_pack(wide, whole(e, prompt_size)),
            lambda t, f, s, e, b, d: unused(wide, t),
        ],
        send_k,
        frame_kv,
        sink,
        up_e,
        down_b,
        down_d,
    )
    up_h = move(send_h, (0, 1), (1, 2), (2, 3))
    send_l = pack(
        place_ref,
        same,
        {1: whole(down_i, same), 2: columns(sink, sink_rows)},
        name="send_l",
        after=(send_h,),
    )
    down_l = move(send_l, (2, 1), (1, 0))
    send_j = choose(
        [
            lambda t, f, s, c, g, b, d, fd: unused(two, t),
            lambda t, f, s, c, g, b, d, fd: visit(
                Block(b, frame, frame), Block(d, frame, frame), g, f, s, 1, two
            ),
            lambda t, f, s, c, g, b, d, fd: attend(
                [([Block(fd, frame, frame)], own_pairs(f, s, 3) + kvs_pairs(c) + kvs_pairs(g), [], None)],
                (two, CW),
                "all_d",
            ),
            lambda t, f, s, c, g, b, d, fd: unused(two, t),
        ],
        send_l,
        frame_kv,
        sink,
        up_c,
        up_g,
        down_b,
        down_d,
        down_f,
    )
    up_j = move(send_j, (1, 2), (2, 3))
    third = pack(
        place_ref,
        prompt_size,
        {
            0: whole(down_k, prompt_size),
            1: whole(down_f, prompt_size),
            2: whole(down_b, prompt_size),
            3: whole(up_e, prompt_size),
        },
        name="third_shard",
        after=(send_j,),
    )
    stages += spread(third)
    down_m = move(down_k, (2, 1))
    down_o = move(down_l, (1, 0))
    send_n = choose(
        [
            lambda t, f, s, h, k, i: unused(two, t),
            lambda t, f, s, h, k, i: visit(
                Block(k, 0, frame), Block(k, frame, frame), h, f, s, 2, two
            ),
            lambda t, f, s, h, k, i: join(Block(i, 0, frame), h, f, s, 0, two),
            lambda t, f, s, h, k, i: unused(two, t),
        ],
        third,
        frame_kv,
        sink,
        up_h,
        down_k,
        down_i,
    )
    up_n = move(send_n, (1, 2), (2, 3))
    last = pack(
        place_ref,
        prompt_size,
        {
            0: whole(down_l, prompt_size),
            1: whole(down_i, prompt_size),
            2: whole(up_e, prompt_size),
            3: whole(up_h, prompt_size),
        },
        name="last_shard",
        after=(stages[6], send_n,),
    )
    stages += spread(last)
    send_o = choose(
        [
            lambda t, f, s, j, i: unused(part_rows, t),
            lambda t, f, s, j, i: unused(part_rows, t),
            lambda t, f, s, j, i: join(Block(i, frame, frame), j, f, s, 1, part_rows),
            lambda t, f, s, j, i: unused(part_rows, t),
        ],
        last,
        frame_kv,
        sink,
        up_j,
        down_i,
    )
    up_o = move(send_o, (2, 3))
    down_r = move(down_m, (1, 0))
    cross_out = cross(cross_queries, stages, pick, prompt_rows, send_o)
    send_q = choose(
        [
            lambda t, f, s, n, d: unused(part_rows, t),
            lambda t, f, s, n, d: unused(part_rows, t),
            lambda t, f, s, n, d: join(Block(d, 0, frame), n, f, s, 2, part_rows),
            lambda t, f, s, n, d: unused(part_rows, t),
        ],
        send_o,
        frame_kv,
        sink,
        up_n,
        down_f,
    )
    up_q = move(send_q, (2, 3))


    def finish0(q, h, f, s, x, u, d):
        return finish(q, h, [d["d"], d["o"], d["r"]], [], [], sink_rows, (f, s))

    def finish1(q, h, f, s, x, u, d):
        return finish(q, h, [d["l"], d["m"]], [u["e"], u["g"], u["h"], u["c"]], [], sink_rows)

    def finish2(q, h, f, s, x, u, d):
        return finish(q, h, [d["k"]], [u["h"], u["j"], u["n"]], [u["c"], u["g"]], sink_rows)

    def finish3(q, h, f, s, x, u, d):
        return finish(q, h, [], [u["n"], u["o"], u["q"], u["j"]], [], sink_rows)

    ups = {"c": up_c, "e": up_e, "g": up_g, "h": up_h, "j": up_j, "n": up_n, "o": up_o, "q": up_q}
    downs = {"d": down_d, "k": down_k, "l": down_l, "m": down_m, "o": down_o, "r": down_r}
    self_out = choose(
        [finish0, finish1, finish2, finish3], queries, at_home, frame_kv, sink, cross_out, ups, downs
    )
    return (self_out, cross_out)


def solution(mesh):
    in_specs = (
        P(("groups", "span"), None),
        P(("groups", "span"), None),
        P(("groups", "span"), None),
        P(("groups", "span"), None, None),
        P("groups", "span", None),
        P("groups"),
    )
    out_specs = (P(("groups", "span"), None), P(("groups", "span"), None))
    return jax.shard_map(shards, mesh=mesh, in_specs=in_specs, out_specs=out_specs, check_vma=False)
```
